32 devices in a mesh: section: 2 (over core), tensor: 4 (over y, x), dp: 4 (over z).
Axes of the slice: x: 2, y: 2, z: 4, core: 2. Of those that a mesh axis runs over, the one named last changes fastest.
Arguments:
- latents: bfloat16 [2, 4, 256, 768], P(None, 'dp', 'tensor'), may hold values from -6 to 6
- cotangent: bfloat16 [2, 4, 256, 768], P(None, 'dp', 'tensor'), may hold values from -6 to 6
- labels: int32 [2, 4], P(None, 'dp'), may hold values from 0 to 1000
- timesteps: int32 [2, 4], P(None, 'dp'), may hold values from 0 to 999
- occupied: int32 [2, 4], P(None, 'dp'), may hold values from 0 to 1, as said below
- class_table: bfloat16 [1001, 768], replicated, may hold values from -6 to 6
- time_weight: bfloat16 [256, 768], replicated, may hold values from -0.5 to 0.5
- project_in: bfloat16 [2, 768, 3, 768], P('section', 'dp', None, 'tensor'), may hold values from -0.21875 to 0.21875
- project_in_bias: bfloat16 [2, 2, 768], P('section', None, ('tensor', 'dp')), may hold values from -3 to 3
- project_out: bfloat16 [2, 768, 768], P('section', 'tensor', 'dp'), may hold values from -0.625 to 0.625
- project_out_bias: bfloat16 [2, 768], P('section', 'dp'), may hold values from -2 to 2
- up_weight: bfloat16 [2, 768, 3072], P('section', 'dp', 'tensor'), may hold values from -0.21875 to 0.21875
- up_bias: bfloat16 [2, 3072], P('section', ('tensor', 'dp')), may hold values from -3 to 3
- down_weight: bfloat16 [2, 3072, 768], P('section', 'tensor', 'dp'), may hold values from -0.109375 to 0.109375
- down_bias: bfloat16 [2, 768], P('section', 'dp'), may hold values from -2 to 2
- modulate_weight: bfloat16 [2, 768, 6, 768], P('section', 'dp', None, 'tensor'), may hold values from -0.21875 to 0.21875
- modulate_bias: bfloat16 [2, 6, 768], P('section', None, ('tensor', 'dp')), may hold values from -3 to 3
Outputs:
- activations: bfloat16 [2, 2, 4, 256, 768], P('section', None, 'dp', 'tensor')
- input_grads: float32 [2, 2, 4, 256, 768], P('section', None, 'dp', 'tensor')
- class_table_grad: float32 [1001, 768], replicated
- time_weight_grad: float32 [256, 768], replicated
- project_in_grad: float32 [2, 768, 3, 768], P('section', 'dp', None, 'tensor')
- project_in_bias_grad: float32 [2, 2, 768], P('section', None, ('tensor', 'dp'))
- project_out_grad: float32 [2, 768, 768], P('section', 'tensor', 'dp')
- project_out_bias_grad: float32 [2, 768], P('section', 'dp')
- up_weight_grad: float32 [2, 768, 3072], P('section', 'dp', 'tensor')
- up_bias_grad: float32 [2, 3072], P('section', ('tensor', 'dp'))
- down_weight_grad: float32 [2, 3072, 768], P('section', 'tensor', 'dp')
- down_bias_grad: float32 [2, 768], P('section', 'dp')
- modulate_weight_grad: float32 [2, 768, 6, 768], P('section', 'dp', None, 'tensor')
- modulate_bias_grad: float32 [2, 6, 768], P('section', None, ('tensor', 'dp'))
The draws below stay inside these ranges and needn't reach their ends.
Inputs may be any that keep to these rules, and one draw needn't show every extreme that they name: 1 where the slot holds a latent of the micro-batch, 0 where it is empty; every micro-batch has an empty slot and an occupied one.
All inputs are finite; a program needn't handle non-finite values.
Results may differ from the reference program's by a relative error of at most 0.028.
Values may be sent and summed in bfloat16 or wider, within the bound.
No kernel may reach another device: no remote copies, remote signals or barrier semaphores. Data moves between devices by JAX's collectives and lax.ppermute only.
A program may use at most 128 MiB of HBM per device.

```python
import math
import jax
import jax.numpy as jnp
from jax import lax

D = 768
HEADS = 12
HD = 64
FF = 3072
CLASSES = 1001
FREQ = 256
TIMESTEPS = 1000
TOK = 256
MICRO = 2
LATENTS = 4
SECTIONS = 2


def draw_occupied(key, part):
    key = jax.random.fold_in(key, 7)
    first_key, second_key, third_key = jax.random.split(key, 3)
    filled = (jax.random.randint(first_key, (MICRO, LATENTS), 0, 4) > 0).astype(jnp.int32)
    empty_slot = jax.random.randint(second_key, (MICRO, 1), 0, LATENTS)
    full_slot = (empty_slot + 1 + jax.random.randint(third_key, (MICRO, 1), 0, LATENTS - 1)) % LATENTS
    positions = jnp.arange(LATENTS, dtype=jnp.int32)[None, :]
    filled = jnp.where(positions == empty_slot, 0, filled)
    filled = jnp.where(positions == full_slot, 1, filled)
    return filled.astype(jnp.int32)


def plant(values, rng, least, high):
    place = [jax.random.randint(jax.random.fold_in(rng, axis), (), 0, length) for axis, length in enumerate(values.shape)]
    longest = values.shape.index(max(values.shape))
    beside = place[:longest] + [(place[longest] + 1) % values.shape[longest]] + place[longest + 1:]
    return values.at[tuple(place)].set(least).at[tuple(beside)].set(high)


def shard_levels(stream_key, dims, cuts, low, largest):
    loudness = 1.0
    for axis_at, shards_of in cuts:
        steps = jax.random.uniform(jax.random.fold_in(jax.random.fold_in(stream_key, 6), axis_at), (shards_of,), jnp.float32, low / len(cuts), largest / len(cuts))
        loudness = loudness * jnp.repeat(jnp.exp(steps), dims[axis_at] // shards_of).reshape((-1,) + (1,) * (len(dims) - 1 - axis_at))
    return loudness


def noise(rng, shape, deviation, most, cuts=(), held_as=jnp.bfloat16):
    result = deviation * jax.random.normal(rng, shape, jnp.float32)
    if cuts:
        result = result * shard_levels(rng, shape, cuts, -0.22, 0.18)
    return jnp.clip(result, -most, most).astype(held_as)


def setup_inputs(seed: int = 0) -> dict:
    keys = jax.random.split(jax.random.key(seed), 18)
    latents = noise(keys[0], (MICRO, LATENTS, TOK, D), 1.0, 6.0, ((1, 4), (2, 4)))
    cotangent = noise(keys[1], (MICRO, LATENTS, TOK, D), 1.0, 6.0, ((1, 4), (2, 4)))
    labels = plant(jax.random.randint(keys[2], (MICRO, LATENTS), 0, CLASSES), jax.random.fold_in(keys[2], 1), 0, CLASSES - 1).astype(jnp.int32)
    timesteps = plant(jax.random.randint(keys[3], (MICRO, LATENTS), 0, TIMESTEPS), jax.random.fold_in(keys[3], 1), 0, TIMESTEPS - 1).astype(jnp.int32)
    occupied = draw_occupied(jax.random.fold_in(keys[17], 71), 0)
    class_table = noise(keys[5], (CLASSES, D), 1.0, 6.0)
    time_weight = noise(keys[6], (FREQ, D), (FREQ // 2) ** -0.5, 0.5)
    project_in = noise(keys[7], (SECTIONS, D, 3, HEADS * HD), D ** -0.5, 0.21875, ((0, 2), (1, 4), (3, 4)))
    project_in_bias = noise(keys[8], (SECTIONS, 2, HEADS * HD), 0.5, 3.0, ((0, 2), (2, 16)))
    project_out = noise(keys[9], (SECTIONS, HEADS * HD, D), (HEADS * HD // 8) ** -0.5, 0.625, ((0, 2), (1, 4), (2, 4)))
    project_out_bias = noise(keys[10], (SECTIONS, D), 0.3, 2.0, ((0, 2), (1, 4)))
    up_weight = noise(keys[11], (SECTIONS, D, FF), D ** -0.5, 0.21875, ((0, 2), (1, 4), (2, 4)))
    up_bias = noise(keys[12], (SECTIONS, FF), 0.5, 3.0, ((0, 2), (1, 16)))
    down_weight = noise(keys[13], (SECTIONS, FF, D), FF ** -0.5, 0.109375, ((0, 2), (1, 4), (2, 4)))
    down_bias = noise(keys[14], (SECTIONS, D), 0.3, 2.0, ((0, 2), (1, 4)))
    modulate_weight = noise(keys[15], (SECTIONS, D, 6, D), D ** -0.5, 0.21875, ((0, 2), (1, 4), (3, 4)))
    modulate_bias = noise(keys[16], (SECTIONS, 6, D), 0.5, 3.0, ((0, 2), (2, 16)))
    return {"latents": latents, "cotangent": cotangent, "labels": labels, "timesteps": timesteps, "occupied": occupied, "class_table": class_table, "time_weight": time_weight, "project_in": project_in, "project_in_bias": project_in_bias, "project_out": project_out, "project_out_bias": project_out_bias, "up_weight": up_weight, "up_bias": up_bias, "down_weight": down_weight, "down_bias": down_bias, "modulate_weight": modulate_weight, "modulate_bias": modulate_bias}


@jax.custom_vjp
def low(v):
    return lax.optimization_barrier(v.astype(jnp.bfloat16)).astype(jnp.float32)

@jax.custom_vjp
def low_back(v):
    return v

def low_keep(v):
    return (low(v), None)

def low_pass(kept, grad):
    return (grad,)

def back_keep(v):
    return (v, None)

def back_low(kept, grad):
    return (low(grad),)
low.defvjp(low_keep, low_pass)
low_back.defvjp(back_keep, back_low)
epsilon = 1e-06
highest = lax.Precision.HIGHEST

def norm_rows(values):
    average = lax.optimization_barrier(jnp.mean(values, axis=-1, keepdims=True))
    centred = values - average
    spread = lax.optimization_barrier(jnp.mean(centred * centred, axis=-1, keepdims=True))
    return centred * lax.rsqrt(spread + epsilon)

def gelu_tanh(values):
    return jax.nn.gelu(values, approximate=True)

def sinus_features(stamps, columns):
    halfway = columns // 2
    frequency = jnp.exp(-math.log(10000.0) * jnp.arange(halfway, dtype=jnp.float32) / halfway)
    angles = stamps.astype(jnp.float32)[:, None] * frequency[None, :]
    return jnp.concatenate([jnp.cos(angles), jnp.sin(angles)], axis=-1)

def split_heads(matrix):
    return matrix.reshape(matrix.shape[0], matrix.shape[1], matrix.shape[2] // HD, HD)

def attention_core(queries, key_rows, value_rows):
    scale_factor = HD ** (-0.5)
    scores = low_back(jnp.einsum('lqhe,lkhe->lhqk', queries, key_rows, precision=highest) * scale_factor)
    attention = low(jax.nn.softmax(scores, axis=-1))
    return jnp.einsum('lhqk,lkhe->lqhe', attention, value_rows, precision=highest)

def block(inputs, modulation, inner_weight, inner_bias, outer_weight, outer_bias, upper_weight, upper_bias, lower_weight, lower_bias):
    shift_one = modulation[:, 0][:, None, :]
    scale_one = modulation[:, 1][:, None, :]
    gate_one = modulation[:, 2][:, None, :]
    shift_two = modulation[:, 3][:, None, :]
    scale_two = modulation[:, 4][:, None, :]
    gate_two = modulation[:, 5][:, None, :]
    normed_in = low(norm_rows(inputs) * (1.0 + scale_one) + shift_one)
    projected = jnp.einsum('ltd,dch->clth', normed_in, inner_weight, precision=highest)
    queries = low(low_back(projected[0] + inner_bias[0]))
    key_rows = low(low_back(projected[1]))
    value_rows = low(low_back(projected[2] + inner_bias[1]))
    mixed_heads = jax.checkpoint(attention_core)(split_heads(queries), split_heads(key_rows), split_heads(value_rows))
    mixed_heads = low(low_back(mixed_heads.reshape(queries.shape)))
    attn_out = low_back(jnp.einsum('lth,hd->ltd', mixed_heads, outer_weight, precision=highest) + outer_bias)
    middle = inputs + gate_one * attn_out
    normed_mid = low(norm_rows(middle) * (1.0 + scale_two) + shift_two)
    hidden_pre = low_back(jnp.einsum('ltd,df->ltf', normed_mid, upper_weight, precision=highest) + upper_bias)
    hidden = low(gelu_tanh(hidden_pre))
    mlp_out = low_back(jnp.einsum('ltf,fd->ltd', hidden, lower_weight, precision=highest) + lower_bias)
    return middle + gate_two * mlp_out

def reference(latents, cotangent, labels, timesteps, occupied, class_table, time_weight, project_in, project_in_bias, project_out, project_out_bias, up_weight, up_bias, down_weight, down_bias, modulate_weight, modulate_bias):
    params = tuple((member.astype(jnp.float32) for member in (class_table, time_weight, project_in, project_in_bias, project_out, project_out_bias, up_weight, up_bias, down_weight, down_bias, modulate_weight, modulate_bias)))
    inputs = latents.astype(jnp.float32).reshape(MICRO * LATENTS, TOK, D)
    probe_zero = jnp.zeros_like(inputs)
    flat_labels = labels.reshape(-1).astype(jnp.int32)
    time_feats = sinus_features(timesteps.reshape(-1), FREQ)

    def forward(inputs, probe_zero, params):
        table_float, time_float, inner_weight, inner_bias, outer_weight, outer_bias, upper_weight, upper_bias, lower_weight, lower_bias, mod_weight, mod_bias = params
        condition = table_float[flat_labels] + jnp.dot(low(time_feats), time_float, precision=highest)
        cond_act = low(jax.nn.silu(condition))

        def section_block(section_index, values):
            modulation = jnp.einsum('lc,ckd->lkd', cond_act, mod_weight[section_index], precision=highest) + mod_bias[section_index]
            return block(values, modulation, inner_weight[section_index], inner_bias[section_index], outer_weight[section_index], outer_bias[section_index], upper_weight[section_index], upper_bias[section_index], lower_weight[section_index], lower_bias[section_index])
        first_out = section_block(0, inputs)
        second_in = low_back(low(first_out)) + probe_zero
        second_out = section_block(1, second_in)
        return (first_out, second_out)
    (first_out, second_out), pullback = jax.vjp(forward, inputs, probe_zero, params)
    live_rows = occupied.reshape(-1).astype(jnp.float32)[:, None, None]
    seed_grad = cotangent.astype(jnp.float32).reshape(inputs.shape) * live_rows
    input_grad, second_grad, param_grads = pullback((jnp.zeros_like(first_out), seed_grad))
    shape_all = (MICRO, LATENTS, TOK, D)
    activations = jnp.stack([first_out.astype(jnp.bfloat16).reshape(shape_all), second_out.astype(jnp.bfloat16).reshape(shape_all)])
    input_grads = jnp.stack([input_grad.reshape(shape_all), second_grad.reshape(shape_all)])
    return (activations, input_grads, param_grads[0], param_grads[1], param_grads[2], param_grads[3], param_grads[4], param_grads[5], param_grads[6], param_grads[7], param_grads[8], param_grads[9], param_grads[10], param_grads[11])
```

```python
import math

import jax
import jax.numpy as jnp
from jax import lax
from jax.sharding import PartitionSpec as P

HD = 64
EPS = 1e-06
HIGH = lax.Precision.HIGHEST
F32 = jnp.float32
BF16 = jnp.bfloat16


def partner(axis, k):
    size = lax.axis_size(axis)
    here = lax.axis_index(axis)
    if size & (size - 1) == 0:
        return here ^ k
    return (here - k) % size


def exchange(value, axis, k):
    size = lax.axis_size(axis)
    if size & (size - 1) == 0:
        return lax.ppermute(value, axis, [(i, i ^ k) for i in range(size)])
    return lax.ppermute(value, axis, [(i, (i - k) % size) for i in range(size)])


def fetch(value, axis, k):
    size = lax.axis_size(axis)
    if size & (size - 1) == 0:
        return lax.ppermute(value, axis, [(i, i ^ k) for i in range(size)])
    return lax.ppermute(value, axis, [(i, (i + k) % size) for i in range(size)])


def swap(value):
    return lax.ppermute(value, "section", [(0, 1), (1, 0)])


def gather_list(value, axis):
    return [value] + [fetch(value, axis, k) for k in range(1, lax.axis_size(axis))]


def place(pieces, axis):
    out = jnp.zeros((len(pieces),) + pieces[0].shape, pieces[0].dtype)
    for k, piece in enumerate(pieces):
        out = lax.dynamic_update_index_in_dim(out, piece, partner(axis, k), 0)
    return out


def gather_tokens(rows):
    return jnp.concatenate(gather_list(rows, "tensor"), axis=0)


def scatter_tokens(terms):
    count = lax.axis_size("tensor")
    blocks = terms.reshape(count, terms.shape[0] // count, terms.shape[1])
    total = blocks[0]
    for k in range(1, count):
        total = total + exchange(blocks[k].astype(BF16), "tensor", k).astype(F32)
    return total


def after(value, other):
    zero = jnp.minimum(jnp.abs(other.reshape(-1)[0].astype(F32)), 0.0)
    return value + zero.astype(value.dtype)


def gather_weights(stack, layer):
    count = lax.axis_size("dp")
    if count <= 8:
        pieces = [stack]
        for k in range(1, count):
            pieces.append(
                lax.ppermute(
                    stack,
                    ("section", "dp"),
                    [(layer * count + i, layer * count + (i ^ k if count & (count - 1) == 0 else (i + k) % count)) for i in range(count)],
                )
            )
        whole = place(pieces, "dp")
    else:
        whole = lax.all_gather(stack, "dp", axis=0)
    other = lax.ppermute(whole, "section", [(layer, 1 - layer)])
    whole = jnp.where(lax.axis_index("section") == layer, whole, other)
    whole = jnp.moveaxis(whole, 0, 1)
    return whole.reshape(whole.shape[0], -1, whole.shape[3])


def scatter_grads(parts):
    core = lax.axis_index("section")
    count = lax.axis_size("dp")
    n = parts.shape[0]
    halves = parts.reshape(n, count, 2, -1, parts.shape[2])
    kept = jnp.where(core == 0, halves[:, :, 0], halves[:, :, 1])
    given = jnp.where(core == 0, halves[:, :, 1], halves[:, :, 0]).astype(BF16)
    kept = kept + swap(given).astype(F32)
    if count <= 8:
        sent = kept.astype(BF16)
        total = lax.dynamic_index_in_dim(kept, partner("dp", 0), 1, False)
        for k in range(1, count):
            block = lax.dynamic_index_in_dim(sent, partner("dp", k), 1, False)
            total = total + exchange(block, "dp", k).astype(F32)
        return total
    return lax.psum_scatter(kept.astype(BF16), "dp", scatter_dimension=1, tiled=False).astype(F32)


def norm_parts(values):
    average = jnp.mean(values, axis=-1, keepdims=True)
    centred = values - average
    spread = jnp.mean(centred * centred, axis=-1, keepdims=True)
    scale = lax.rsqrt(spread + EPS)
    return centred * scale, scale


def norm_pull(grad, normed, scale):
    first = jnp.mean(grad, axis=-1, keepdims=True)
    second = jnp.mean(grad * normed, axis=-1, keepdims=True)
    return scale * (grad - first - normed * second)


def gelu_parts(values):
    root = math.sqrt(2.0 / math.pi)
    square = values * values
    bent = jnp.tanh(root * (values + 0.044715 * values * square))
    result = 0.5 * values * (1.0 + bent)
    slope = 0.5 * (1.0 + bent) + 0.5 * values * (1.0 - bent * bent) * root * (1.0 + 0.134145 * square)
    return result.astype(BF16), slope


def sinus_features(stamps, columns):
    halfway = columns // 2
    frequency = jnp.exp(-math.log(10000.0) * jnp.arange(halfway, dtype=F32) / halfway)
    angles = stamps.astype(F32)[:, None] * frequency[None, :]
    return jnp.concatenate([jnp.cos(angles), jnp.sin(angles)], axis=-1)


def dot(left, right, left_dim, right_dim):
    return lax.dot_general(
        left, right, (((left_dim,), (right_dim,)), ((), ())), preferred_element_type=F32
    )


def split_heads(matrix):
    return matrix.reshape(matrix.shape[0], matrix.shape[1] // HD, HD)


def attention_forward(queries, key_rows, value_rows):
    scores = jnp.einsum("qhe,khe->hqk", queries, key_rows, preferred_element_type=F32) * HD**-0.5
    largest = jnp.max(scores, axis=-1, keepdims=True)
    raised = jnp.exp(scores - largest)
    attention = raised / jnp.sum(raised, axis=-1, keepdims=True)
    rounded = attention.astype(BF16)
    mixed = jnp.einsum("hqk,khe->qhe", rounded, value_rows, preferred_element_type=F32)
    return mixed.astype(BF16), attention


def attention_backward(queries, key_rows, value_rows, attention, mixed_grad):
    weight_grad = jnp.einsum("qhe,khe->hqk", mixed_grad, value_rows, preferred_element_type=F32)
    value_grad = jnp.einsum(
        "hqk,qhe->khe", attention.astype(BF16), mixed_grad, preferred_element_type=F32
    )
    row_dot = jnp.sum(attention * weight_grad, axis=-1, keepdims=True)
    score_grad = (attention * (weight_grad - row_dot)).astype(BF16)
    query_grad = (
        jnp.einsum("hqk,khe->qhe", score_grad, key_rows, preferred_element_type=F32) * HD**-0.5
    )
    key_grad = (
        jnp.einsum("hqk,qhe->khe", score_grad, queries, preferred_element_type=F32) * HD**-0.5
    )
    return query_grad.astype(BF16), key_grad.astype(BF16), value_grad.astype(BF16)


def attend(attn_in, packed, in_bias):
    width = packed.shape[1] // 4
    projected = dot(attn_in, packed[:, : 3 * width], 1, 0)
    queries = (projected[:, :width] + in_bias[0]).astype(BF16)
    key_rows = projected[:, width : 2 * width].astype(BF16)
    value_rows = (projected[:, 2 * width :] + in_bias[1]).astype(BF16)
    heads = (split_heads(queries), split_heads(key_rows), split_heads(value_rows))
    mixed, attention = attention_forward(*heads)
    mixed = mixed.reshape(queries.shape)
    return dot(mixed, packed[:, 3 * width :], 1, 1), (heads, attention, mixed)


def attend_back(outer_grad, packed, kept):
    heads, attention, mixed = kept
    width = packed.shape[1] // 4
    mixed_grad = dot(outer_grad, packed[:, 3 * width :], 1, 0).astype(BF16)
    grads = attention_backward(*heads, attention, split_heads(mixed_grad))
    stacked = jnp.concatenate([member.reshape(mixed.shape) for member in grads], axis=1)
    return dot(stacked, packed[:, : 3 * width], 1, 1), stacked


def body(
    latents,
    cotangent,
    labels,
    timesteps,
    occupied,
    class_table,
    time_weight,
    project_in,
    project_in_bias,
    project_out,
    project_out_bias,
    up_weight,
    up_bias,
    down_weight,
    down_bias,
    modulate_weight,
    modulate_bias,
):
    core = lax.axis_index("section")
    shards = lax.axis_size("dp")
    cuts = lax.axis_size("tensor")
    micro_count = latents.shape[0]
    width = latents.shape[3]
    part = width // cuts
    rows = width // shards

    def pick(first, second):
        return jnp.where(core == 0, first, second)

    tokens_own = pick(latents[0, 0], latents[1, 0])
    seed_own = pick(
        cotangent[0, 0] * occupied[0, 0].astype(BF16), cotangent[1, 0] * occupied[1, 0].astype(BF16)
    )
    tokens_all = gather_tokens(tokens_own).astype(F32)
    seed_all = gather_tokens(seed_own).astype(F32)

    packed_own = jnp.concatenate(
        [project_in[0, :, 0], project_in[0, :, 1], project_in[0, :, 2], project_out[0].T], axis=1
    )
    first_a = gather_weights(packed_own[None], 0)[0]
    mlp_own = jnp.stack([up_weight[0], down_weight[0].T])
    first_u, first_d = gather_weights(after(mlp_own, first_a), 0)
    second_a = gather_weights(after(packed_own, first_u)[None], 1)[0]
    second_u, second_d = gather_weights(after(mlp_own, second_a), 1)
    weights = ((first_a, first_u, first_d), (second_a, second_u, second_d))

    stamps = jnp.concatenate([labels.reshape(-1), timesteps.reshape(-1)])
    if shards <= 8:
        stamps = place(gather_list(stamps, "dp"), "dp")
    else:
        stamps = lax.all_gather(stamps, "dp", axis=0)
    flat_labels = stamps[:, :micro_count].reshape(-1)
    flat_times = stamps[:, micro_count:].reshape(-1)
    class_count = class_table.shape[0]
    class_hot = flat_labels[:, None] == jnp.arange(class_count, dtype=jnp.int32)[None, :]
    time_feats = sinus_features(flat_times, time_weight.shape[0]).astype(BF16)
    condition = dot(class_hot.astype(BF16), class_table, 1, 0) + dot(time_feats, time_weight, 1, 0)
    cond_act = jax.nn.silu(condition).astype(BF16)
    act_rows = lax.dynamic_slice_in_dim(cond_act, lax.axis_index("dp") * rows, rows, 1)

    mod_weight = modulate_weight[0].reshape(rows, -1)
    mod_terms = dot(act_rows, mod_weight, 1, 0).reshape(shards, micro_count, 6, part)
    bias_cols = modulate_bias.shape[2]
    bias_full = lax.dynamic_update_slice_in_dim(
        jnp.zeros((6, part), F32), modulate_bias[0].astype(F32), lax.axis_index("dp") * bias_cols, 1
    )
    mod_terms = (mod_terms + bias_full).reshape(shards, -1)
    bias_own = jnp.concatenate(
        [
            member.astype(F32).reshape(-1)
            for member in (project_in_bias, up_bias, project_out_bias, down_bias)
        ]
    )
    mod_size = mod_terms.shape[1]
    if shards <= 8:
        mod_sum = lax.dynamic_index_in_dim(mod_terms, partner("dp", 0), 0, False)
        bias_list = [bias_own]
        for k in range(1, shards):
            block = lax.dynamic_index_in_dim(mod_terms, partner("dp", k), 0, False)
            if shards & (shards - 1) == 0:
                both = exchange(jnp.concatenate([block, bias_own]), "dp", k)
                mod_sum = mod_sum + both[:mod_size]
                bias_list.append(both[mod_size:])
            else:
                mod_sum = mod_sum + exchange(block, "dp", k)
                bias_list.append(fetch(bias_own, "dp", k))
        bias_all = place(bias_list, "dp")
    else:
        mod_sum = lax.psum_scatter(mod_terms, "dp", scatter_dimension=0, tiled=False)
        bias_all = lax.all_gather(bias_own, "dp", axis=0)
    mod_sum = mod_sum.reshape(micro_count, -1)
    half_size = mod_size // micro_count
    received = swap(jnp.concatenate([pick(mod_sum[1], mod_sum[0]), bias_all.reshape(-1)]))
    mod_kept = pick(mod_sum[0], mod_sum[1])
    mod_got = received[:half_size]
    bias_got = received[half_size:].reshape(bias_all.shape)
    mod_both = jnp.stack([pick(mod_kept, mod_got), pick(mod_got, mod_kept)]).reshape(-1, part)
    mod_all = place(gather_list(mod_both, "tensor"), "tensor")
    modulation = jnp.moveaxis(mod_all, 0, 1).reshape(2, 6, width)
    biases = []
    for member in (pick(bias_all, bias_got), pick(bias_got, bias_all)):
        cols = project_in_bias.shape[2]
        in_bias = jnp.moveaxis(member[:, : 2 * cols].reshape(shards, 2, cols), 0, 1).reshape(2, part)
        rest = member[:, 2 * cols :]
        up_len, out_len = up_bias.shape[1], project_out_bias.shape[1]
        biases.append(
            (
                in_bias,
                rest[:, :up_len].reshape(-1),
                rest[:, up_len : up_len + out_len].reshape(-1),
                rest[:, up_len + out_len :].reshape(-1),
            )
        )

    kept_layers = []
    outputs = []
    inputs = tokens_own.astype(F32)
    for layer in range(2):
        shift_one, scale_one, gate_one, shift_two, scale_two, gate_two = [
            modulation[layer, k][None] for k in range(6)
        ]
        packed, upper, lower = weights[layer]
        in_bias, upper_bias, outer_bias, lower_bias = biases[layer]
        normed_one, scale_in = norm_parts(inputs)
        if layer == 0:
            normed_all = norm_parts(tokens_all)[0]
            attn_in = (normed_all * (1.0 + scale_one) + shift_one).astype(BF16)
        else:
            normed_all = None
            attn_in = gather_tokens((normed_one * (1.0 + scale_one) + shift_one).astype(BF16))
        branch, attn_kept = attend(attn_in, packed, in_bias)
        attn_out = scatter_tokens(branch) + outer_bias
        middle = inputs + gate_one * attn_out
        normed_two, scale_mid = norm_parts(middle)
        mlp_in = gather_tokens((normed_two * (1.0 + scale_two) + shift_two).astype(BF16))
        hidden, slope = gelu_parts(dot(mlp_in, upper, 1, 0) + upper_bias)
        mlp_out = scatter_tokens(dot(hidden, lower, 1, 1)) + lower_bias
        output = middle + gate_two * mlp_out
        outputs.append(output.astype(BF16))
        kept_layers.append(
            (normed_one, scale_in, normed_all, attn_in, attn_kept, attn_out, normed_two, scale_mid, mlp_in, hidden, slope, mlp_out)
        )
        inputs = outputs[-1].astype(F32)

    grad_own = seed_own.astype(F32)
    mod_grads = [None, None]
    bias_grads = [None, None]
    shard_grads = [None, None]
    input_grads = [None, None]
    for layer in (1, 0):
        shift_one, scale_one, gate_one, shift_two, scale_two, gate_two = [
            modulation[layer, k][None] for k in range(6)
        ]
        packed, upper, lower = weights[layer]
        (normed_one, scale_in, normed_all, attn_in, attn_kept, attn_out, normed_two, scale_mid, mlp_in, hidden, slope, mlp_out) = kept_layers[layer]
        if layer == 1:
            lower_grad = (seed_all * gate_two).astype(BF16)
        else:
            lower_grad = gather_tokens((grad_own * gate_two).astype(BF16))
        pre_grad = (dot(lower_grad, lower, 1, 0) * slope).astype(BF16)
        mid_grad = scatter_tokens(dot(pre_grad, upper, 1, 1))
        d_gate_two = jnp.sum(grad_own * mlp_out, axis=0)
        d_shift_two = jnp.sum(mid_grad, axis=0)
        d_scale_two = jnp.sum(mid_grad * normed_two, axis=0)
        middle_grad = grad_own + norm_pull(mid_grad * (1.0 + scale_two), normed_two, scale_mid)
        d_gate_one = jnp.sum(middle_grad * attn_out, axis=0)
        outer_grad = gather_tokens((middle_grad * gate_one).astype(BF16))
        in_terms, stacked = attend_back(outer_grad, packed, attn_kept)
        in_grad = scatter_tokens(in_terms)
        if layer == 0:
            d_shift_one = jnp.sum(in_terms, axis=0)
            d_scale_one = jnp.sum(in_terms * normed_all, axis=0)
        else:
            d_shift_one = jnp.sum(in_grad, axis=0)
            d_scale_one = jnp.sum(in_grad * normed_one, axis=0)
        input_grad = middle_grad + norm_pull(in_grad * (1.0 + scale_one), normed_one, scale_in)
        input_grads[layer] = input_grad
        grad_own = input_grad.astype(BF16).astype(F32)
        mod_grads[layer] = jnp.stack(
            [d_shift_one, d_scale_one, d_gate_one, d_shift_two, d_scale_two, d_gate_two]
        )
        mlp_grads = jnp.stack([dot(mlp_in, pre_grad, 0, 0), dot(lower_grad, hidden, 0, 0)])
        attn_grads = jnp.concatenate(
            [dot(attn_in, stacked, 0, 0), dot(outer_grad, attn_kept[2], 0, 0)], axis=1
        )
        shard_grads[layer] = jnp.concatenate(
            [scatter_grads(mlp_grads), scatter_grads(attn_grads[None])]
        )
        d_stacked = jnp.sum(stacked.astype(F32), axis=0)
        in_bias_grad = jnp.stack([d_stacked[:part], d_stacked[2 * part :]])
        in_bias_grad = jnp.moveaxis(in_bias_grad.reshape(2, shards, -1), 1, 0).reshape(shards, -1)
        bias_grads[layer] = jnp.concatenate(
            [in_bias_grad]
            + [
                jnp.sum(member.astype(F32), axis=0).reshape(shards, -1)
                for member in (pre_grad, outer_grad, lower_grad)
            ],
            axis=1,
        )

    given = swap(pick(shard_grads[1], shard_grads[0]))
    own = pick(shard_grads[0], shard_grads[1])
    grads = jnp.concatenate([pick(own, given), pick(given, own)], axis=1)
    grad_upper, grad_lower = grads[0], grads[1].T
    grad_inner = grads[2, :, : 3 * part].reshape(rows, 3, part)
    grad_outer = grads[2, :, 3 * part :].T

    mod_part = jnp.stack(mod_grads).reshape(2 * 6, cuts, part)
    mod_part = jnp.moveaxis(mod_part, 1, 0)
    mod_shard = lax.dynamic_index_in_dim(mod_part, partner("tensor", 0), 0, False)
    for k in range(1, cuts):
        block = lax.dynamic_index_in_dim(mod_part, partner("tensor", k), 0, False)
        mod_shard = mod_shard + exchange(block, "tensor", k)
    mod_shard = mod_shard.reshape(2, 6 * part)
    bias_len = bias_grads[0].shape[1]
    received = swap(
        jnp.concatenate(
            [pick(mod_shard[1], mod_shard[0]), pick(bias_grads[1], bias_grads[0]).reshape(-1)]
        )
    )
    mod_kept = pick(mod_shard[0], mod_shard[1])
    mod_got = received[: 6 * part]
    mod_micro = jnp.concatenate([pick(mod_kept, mod_got), pick(mod_got, mod_kept)])
    bias_sum = pick(bias_grads[0], bias_grads[1]) + received[6 * part :].reshape(shards, bias_len)
    if shards <= 8 and shards & (shards - 1) == 0:
        mod_list = [mod_micro]
        bias_total = lax.dynamic_index_in_dim(bias_sum, partner("dp", 0), 0, False)
        for k in range(1, shards):
            block = lax.dynamic_index_in_dim(bias_sum, partner("dp", k), 0, False)
            both = exchange(jnp.concatenate([mod_micro, block]), "dp", k)
            mod_list.append(both[: mod_micro.shape[0]])
            bias_total = bias_total + both[mod_micro.shape[0] :]
        mod_slots = place(mod_list, "dp")
    else:
        mod_slots = lax.all_gather(mod_micro, "dp", axis=0)
        bias_total = lax.psum_scatter(bias_sum, "dp", scatter_dimension=0, tiled=False)
    mod_slots = mod_slots.reshape(shards * micro_count, 6 * part)
    grad_mod_weight = lax.dot_general(
        act_rows.astype(F32), mod_slots, (((0,), (0,)), ((), ())), precision=HIGH
    ).reshape(rows, 6, part)
    mod_bias_sum = jnp.sum(mod_slots, axis=0).reshape(6, part)
    grad_mod_bias = lax.dynamic_slice_in_dim(
        mod_bias_sum, lax.axis_index("dp") * bias_cols, bias_cols, 1
    )
    act_grad = lax.dot_general(
        mod_slots, mod_weight.astype(F32), (((1,), (1,)), ((), ())), precision=HIGH
    )
    act_grad = act_grad + swap(act_grad)
    act_grad = sum(gather_list(act_grad, "tensor"))
    if shards <= 8:
        act_all = place(gather_list(act_grad, "dp"), "dp")
    else:
        act_all = lax.all_gather(act_grad, "dp", axis=0)
    act_all = jnp.moveaxis(act_all, 0, 1).reshape(-1, width)
    cond_grad = jax.vjp(jax.nn.silu, condition)[1](act_all)[0]
    table_grad = lax.dot_general(
        class_hot.astype(F32), cond_grad, (((0,), (0,)), ((), ())), precision=HIGH
    )
    time_grad = lax.dot_general(
        time_feats.astype(F32), cond_grad, (((0,), (0,)), ((), ())), precision=HIGH
    )
    cols = project_in_bias.shape[2]
    up_len, out_len = up_bias.shape[1], project_out_bias.shape[1]
    grad_in_bias = bias_total[: 2 * cols].reshape(2, cols)
    rest = bias_total[2 * cols :]

    def by_micro(first, second):
        got = swap(pick(second, first))
        held = pick(first, second)
        return jnp.stack([pick(held, got), pick(got, held)])[None, :, None]

    return (
        by_micro(outputs[0], outputs[1]),
        by_micro(input_grads[0], input_grads[1]),
        table_grad,
        time_grad,
        grad_inner[None],
        grad_in_bias[None],
        grad_outer[None],
        rest[up_len : up_len + out_len][None],
        grad_upper[None],
        rest[:up_len][None],
        grad_lower[None],
        rest[up_len + out_len :][None],
        grad_mod_weight[None],
        grad_mod_bias[None],
    )


def solution(mesh):
    in_specs = (
        P(None, "dp", "tensor", None),
        P(None, "dp", "tensor", None),
        P(None, "dp"),
        P(None, "dp"),
        P(None, "dp"),
        P(),
        P(),
        P("section", "dp", None, "tensor"),
        P("section", None, ("tensor", "dp")),
        P("section", "tensor", "dp"),
        P("section", "dp"),
        P("section", "dp", "tensor"),
        P("section", ("tensor", "dp")),
        P("section", "tensor", "dp"),
        P("section", "dp"),
        P("section", "dp", None, "tensor"),
        P("section", None, ("tensor", "dp")),
    )
    out_specs = (
        P("section", None, "dp", "tensor", None),
        P("section", None, "dp", "tensor", None),
        P(),
        P(),
        P("section", "dp", None, "tensor"),
        P("section", None, ("tensor", "dp")),
        P("section", "tensor", "dp"),
        P("section", "dp"),
        P("section", "dp", "tensor"),
        P("section", ("tensor", "dp")),
        P("section", "tensor", "dp"),
        P("section", "dp"),
        P("section", "dp", None, "tensor"),
        P("section", None, ("tensor", "dp")),
    )
    return jax.shard_map(body, mesh=mesh, in_specs=in_specs, out_specs=out_specs, check_vma=False)
```

```python
import math
from types import SimpleNamespace as Named

import jax
import jax.numpy as jnp
from jax import lax
from jax.experimental import pallas as pl
from jax.experimental.pallas import tpu as pltpu
from jax.sharding import PartitionSpec as P

HD = 64
EPS = 1e-06
HIGH = lax.Precision.HIGHEST
F32 = jnp.float32
BF16 = jnp.bfloat16
SECTION, TENSOR, SLOTS = "section", "tensor", "dp"
ROWS = (SLOTS, SECTION)
SPACE = 40 * 1024 * 1024


def cyclic(axis):
    size = lax.axis_size(axis)
    return size & (size - 1) != 0


def exchange(value, axis, k):
    size = lax.axis_size(axis)
    if cyclic(axis):
        return lax.ppermute(value, axis, [(i, (i - k) % size) for i in range(size)])
    return lax.ppermute(value, axis, [(i, i ^ k) for i in range(size)])


def fetch(value, axis, k):
    size = lax.axis_size(axis)
    if cyclic(axis):
        return lax.ppermute(value, axis, [(i, (i + k) % size) for i in range(size)])
    return lax.ppermute(value, axis, [(i, i ^ k) for i in range(size)])


def partner(axis, k):
    here = lax.axis_index(axis)
    if cyclic(axis):
        return (here - k) % lax.axis_size(axis)
    return here ^ k


def swap(value):
    return lax.ppermute(value, SECTION, [(0, 1), (1, 0)])


def gather_list(value, axis):
    return [value] + [fetch(value, axis, k) for k in range(1, lax.axis_size(axis))]


def exchange_list(values, axis):
    return [values[0]] + [exchange(values[k], axis, k) for k in range(1, lax.axis_size(axis))]


def place(pieces, axis):
    out = jnp.zeros((len(pieces),) + pieces[0].shape, pieces[0].dtype)
    for k, piece in enumerate(pieces):
        out = lax.dynamic_update_index_in_dim(out, piece, partner(axis, k), 0)
    return out


def shaped(shape, dtype):
    return jax.ShapeDtypeStruct(shape, dtype)


class Part:
    def __init__(self, value, at=None):
        self.value, self.at = value, at
        self.shape, self.dtype = value.shape, value.dtype


def run(kernel, outs, *args, flops=0, wait=()):
    def leafy(value):
        return isinstance(value, Part)

    names = list(vars(outs))
    out_flat, out_tree = jax.tree.flatten([vars(outs)[name] for name in names])
    flat, tree = jax.tree.flatten(args, is_leaf=leafy)
    moved = sum(math.prod(leaf.shape) * leaf.dtype.itemsize for leaf in flat + out_flat)

    def inner(*refs):
        ins = list(refs[: len(flat)])
        for k, leaf in enumerate(flat):
            if leafy(leaf) and leaf.at is not None:
                ins[k] = Named(ref=ins[k], at=leaf.at)
        results = jax.tree.unflatten(out_tree, refs[len(flat) + len(wait) :])
        kernel(*jax.tree.unflatten(tree, ins), Named(**dict(zip(names, results))))

    result = pl.pallas_call(
        inner,
        out_shape=out_flat,
        in_specs=[
            pl.BlockSpec(memory_space=pltpu.SMEM if leaf.dtype == jnp.int32 else pltpu.VMEM)
            for leaf in flat
        ]
        + [pl.BlockSpec(memory_space=pl.ANY)] * len(wait),
        out_specs=[pl.BlockSpec(memory_space=pltpu.VMEM)] * len(out_flat),
        compiler_params=pltpu.CompilerParams(vmem_limit_bytes=SPACE),
        cost_estimate=pl.CostEstimate(flops=flops, bytes_accessed=moved, transcendentals=0),
    )(*[leaf.value if leafy(leaf) else leaf for leaf in flat], *wait)
    return Named(**dict(zip(names, jax.tree.unflatten(out_tree, result))))


def matrix(ref):
    if isinstance(ref, Named):
        value = ref.ref[:, ref.at]
        return value.reshape(-1, value.shape[-1])
    return ref[...]


def norm_parts(values):
    average = jnp.mean(values, axis=-1, keepdims=True)
    centred = values - average
    spread = jnp.mean(centred * centred, axis=-1, keepdims=True)
    scale = lax.rsqrt(spread + EPS)
    return centred * scale, scale


def norm_pull(grad, normed, scale):
    first = jnp.mean(grad, axis=-1, keepdims=True)
    second = jnp.mean(grad * normed, axis=-1, keepdims=True)
    return scale * (grad - first - normed * second)


def dot(left, right, left_dim, right_dim):
    return lax.dot_general(
        left, right, (((left_dim,), (right_dim,)), ((), ())), preferred_element_type=F32
    )


def joined(refs):
    return jnp.concatenate([ref[...] for ref in refs], axis=0)


def summed(refs):
    total = refs[0][...].astype(F32)
    for ref in refs[1:]:
        total = total + ref[...].astype(F32)
    return total


def spread_out(terms, refs):
    rows = refs[0].shape[0]
    for k, ref in enumerate(refs):
        ref[...] = terms[k * rows : (k + 1) * rows].astype(ref.dtype)


def column_sum(values):
    return jnp.sum(values.astype(F32), axis=0, keepdims=True)


def softmax_parts(query, key):
    scores = dot(query, key, 1, 1) * HD**-0.5
    raised = jnp.exp(scores - jnp.max(scores, axis=-1, keepdims=True))
    return raised / jnp.sum(raised, axis=-1, keepdims=True)


def assemble(spot, pieces, ref):
    own, other = pieces
    rows = own[0].shape[0]
    for k, piece in enumerate(own):
        for half, block in ((spot[0], piece[...]), (1 - spot[0], other[k])):
            at = pl.multiple_of((2 * spot[3 + k] + half) * rows, rows)
            ref[pl.ds(at, rows), :] = block


def attend(first, mods, packed, in_bias, refs, layer):
    width = packed.shape[1] // 4
    attn_in = joined(first)
    if layer == 0:
        refs.kept[:, 2 * packed.shape[1] :] = attn_in
        normed = norm_parts(attn_in.astype(F32))[0]
        attn_in = (normed * (1.0 + mods[1:2]) + mods[0:1]).astype(BF16)
    refs.kept[:, : packed.shape[1]] = attn_in
    projected = dot(attn_in, packed[:, : 3 * width], 1, 0)
    queries = (projected[:, :width] + in_bias[0:1]).astype(BF16)
    keys = projected[:, width : 2 * width].astype(BF16)
    values = (projected[:, 2 * width :] + in_bias[1:2]).astype(BF16)
    mixed = []
    for at in range(0, width, HD):
        attention = softmax_parts(queries[:, at : at + HD], keys[:, at : at + HD])
        mixed.append(dot(attention.astype(BF16), values[:, at : at + HD], 1, 0))
    mixed = jnp.concatenate(mixed, axis=1).astype(BF16)
    refs.kept[:, packed.shape[1] : 2 * packed.shape[1]] = jnp.concatenate(
        [queries, keys, values, mixed], axis=1
    )
    spread_out(dot(mixed, packed[:, 3 * width :], 1, 1), refs.terms)


def attend_kernel(layer):
    def kernel(spot, first, mods_ref, packed_ref, bias_ref, refs):
        if isinstance(packed_ref, tuple):
            assemble(spot, packed_ref, refs.packed)
            packed_ref = refs.packed
        attend(first, mods_ref[6 * layer : 6 * layer + 6], matrix(packed_ref), bias_ref[...], refs, layer)

    return kernel


def middle_kernel(layer):
    def kernel(terms, inputs, mods_ref, bias_ref, refs):
        mods = mods_ref[6 * layer : 6 * layer + 6]
        attn_out = summed(terms) + bias_ref[2:3]
        rows = attn_out.shape[0]
        refs.kept[:rows] = attn_out
        middle = inputs[...].astype(F32) + mods[2:3] * attn_out
        refs.kept[rows:] = middle
        normed = norm_parts(middle)[0]
        refs.mlp_in[...] = (normed * (1.0 + mods[4:5]) + mods[3:4]).astype(BF16)

    return kernel


def mlp_kernel(pieces, upper, lower, bias_ref, refs):
    mlp_in = joined(pieces)
    size = upper.ref.shape[-1] if isinstance(upper, Named) else upper.shape[-1]
    wide = mlp_in.shape[1]
    refs.kept[:, :wide] = mlp_in
    values = dot(mlp_in, matrix(upper), 1, 0) + bias_ref[1:2]
    root = math.sqrt(2.0 / math.pi)
    square = values * values
    bent = jnp.tanh(root * (values + 0.044715 * values * square))
    hidden = (0.5 * values * (1.0 + bent)).astype(BF16)
    refs.kept[:, wide : wide + size] = hidden
    slope = 0.5 * (1.0 + bent) + 0.5 * values * (1.0 - bent * bent) * root * (
        1.0 + 0.134145 * square
    )
    refs.kept[:, wide + size :] = slope.astype(BF16)
    spread_out(dot(hidden, matrix(lower), 1, 1), refs.terms)


def last_kernel(layer):
    def kernel(terms, kept, mods_ref, bias_ref, refs):
        mlp_out = summed(terms) + bias_ref[3:4]
        refs.mlp_out[...] = mlp_out
        output = (kept[kept.shape[0] // 2 :] + mods_ref[6 * layer + 5 : 6 * layer + 6] * mlp_out).astype(BF16)
        refs.output[...] = output
        if layer == 0:
            normed = norm_parts(output.astype(F32))[0]
            refs.attn_in[...] = (normed * (1.0 + mods_ref[7:8]) + mods_ref[6:7]).astype(BF16)

    return kernel


def mlp_back_kernel(layer):
    def kernel(pieces, mods_ref, upper, lower, kept, refs):
        lower_grad = joined(pieces)
        if layer == 1:
            lower_grad = (lower_grad.astype(F32) * mods_ref[11:12]).astype(BF16)
        wide = lower_grad.shape[1]
        refs.grads[:, :wide] = lower_grad
        pre_grad = dot(lower_grad, matrix(lower), 1, 0)
        slope = kept[:, wide + pre_grad.shape[1] :].astype(F32)
        pre_grad = (pre_grad * slope).astype(BF16)
        refs.grads[:, wide:] = pre_grad
        spread_out(dot(pre_grad, matrix(upper), 1, 1), refs.terms)
        refs.bias[0:1] = column_sum(pre_grad)
        refs.bias[1:2] = column_sum(lower_grad)

    return kernel


def middle_back_kernel(layer):
    def kernel(terms, grad_ref, kept, mlp_out, mods_ref, refs):
        mods = mods_ref[6 * layer : 6 * layer + 6]
        grad = grad_ref[...].astype(F32)
        mid_grad = summed(terms)
        normed, scale = norm_parts(kept[kept.shape[0] // 2 :])
        middle_grad = grad + norm_pull(mid_grad * (1.0 + mods[4:5]), normed, scale)
        refs.middle_grad[...] = middle_grad
        refs.outer[...] = (middle_grad * mods[2:3]).astype(BF16)
        refs.rows[0:1] = column_sum(middle_grad * kept[: kept.shape[0] // 2])
        refs.rows[1:2] = column_sum(mid_grad)
        refs.rows[2:3] = column_sum(mid_grad * normed)
        refs.rows[3:4] = column_sum(grad * mlp_out[...])

    return kernel


def attend_back_kernel(layer):
    def kernel(pieces, packed, kept, refs):
        outer_grad = joined(pieces)
        wide = outer_grad.shape[1]
        refs.grads[:, :wide] = outer_grad
        packed = matrix(packed)
        width = packed.shape[1] // 4
        mixed_grad = dot(outer_grad, packed[:, 3 * width :], 1, 0).astype(BF16)
        queries, keys, values = [
            kept[:, wide + k * width : wide + (k + 1) * width] for k in range(3)
        ]
        d_queries, d_keys, d_values = [], [], []
        for at in range(0, width, HD):
            query, key = queries[:, at : at + HD], keys[:, at : at + HD]
            grad = mixed_grad[:, at : at + HD]
            attention = softmax_parts(query, key)
            weight_grad = dot(grad, values[:, at : at + HD], 1, 1)
            d_values.append(dot(attention.astype(BF16), grad, 0, 0))
            row_dot = jnp.sum(attention * weight_grad, axis=-1, keepdims=True)
            score_grad = (attention * (weight_grad - row_dot)).astype(BF16)
            d_queries.append(dot(score_grad, key, 1, 0) * HD**-0.5)
            d_keys.append(dot(score_grad, query, 0, 0) * HD**-0.5)
        stacked = jnp.concatenate(d_queries + d_keys + d_values, axis=1).astype(BF16)
        refs.grads[:, wide:] = stacked
        terms = dot(stacked, packed[:, : 3 * width], 1, 1)
        spread_out(terms, refs.terms)
        refs.out_bias[...] = column_sum(outer_grad)
        refs.in_bias[...] = column_sum(stacked)
        if layer == 0:
            normed = norm_parts(kept[:, 2 * wide :].astype(F32))[0]
            refs.rows[0:1] = column_sum(terms)
            refs.rows[1:2] = column_sum(terms * normed)

    return kernel


def first_back_kernel(layer):
    def kernel(terms, middle_grad, inputs, mods_ref, refs):
        in_grad = summed(terms)
        normed, scale = norm_parts(inputs[...].astype(F32))
        scale_one = mods_ref[6 * layer + 1 : 6 * layer + 2]
        input_grad = middle_grad[...] + norm_pull(in_grad * (1.0 + scale_one), normed, scale)
        refs.input_grad[...] = input_grad
        if layer == 1:
            refs.rows[0:1] = column_sum(in_grad)
            refs.rows[1:2] = column_sum(in_grad * normed)
            rounded = input_grad.astype(BF16)
            refs.grad[...] = rounded
            refs.lower[...] = (rounded.astype(F32) * mods_ref[5:6]).astype(BF16)

    return kernel


def cut(grad, ref, at):
    count, rows, half = ref.shape[0], ref.shape[2], ref.shape[3]
    for block in range(count):
        place_at = block // 2 * rows
        ref[block, at] = grad[
            place_at : place_at + rows, block % 2 * half : block % 2 * half + half
        ].astype(BF16)


def mlp_grads_kernel(kept, grads, refs):
    wide = 2 * refs.grads.shape[3]
    size = grads.shape[1] - wide
    cut(dot(kept[:, :wide], grads[:, wide:], 0, 0), refs.grads, 0)
    cut(dot(grads[:, :wide], kept[:, wide : wide + size], 0, 0), refs.grads, 1)


def packed_grads(kept, grads, wide):
    width = wide // 4
    inner = dot(kept[:, :wide], grads[:, wide:], 0, 0)
    outer = dot(grads[:, :wide], kept[:, wide + 3 * width : 2 * wide], 0, 0)
    return jnp.concatenate([inner, outer], axis=1)


def attend_grads_kernel(kept, grads, refs):
    cut(packed_grads(kept, grads, 2 * refs.grads.shape[3]), refs.grads, 0)


def attend_halves_kernel(spot, kept, grads, refs):
    half = refs.kept.shape[1]
    grad = packed_grads(kept, grads, 2 * half)
    left, right = grad[:, :half], grad[:, half:]
    refs.kept[...] = jnp.where(spot[0] == 0, left, right)
    refs.given[...] = jnp.where(spot[0] == 0, right, left).astype(BF16)


def share_kernel(spot, kept, received, refs):
    rows = refs.own.shape[0]
    for k, ref in enumerate([refs.own] + refs.sent):
        at = pl.ds(pl.multiple_of(spot[3 + k] * rows, rows), rows)
        ref[...] = (kept[at, :] + received[at, :].astype(F32)).astype(ref.dtype)


def ordered(spot, at, pieces):
    result = []
    for j in range(len(pieces)):
        chosen = pieces[0]
        for k in range(1, len(pieces)):
            chosen = jnp.where(spot[at + k] == j, pieces[k], chosen)
        result.append(chosen)
    return result


def mods_kernel(spot, mod_pieces, kept, got, refs):
    count = len(kept)
    refs.mods[...] = jnp.concatenate(
        ordered(spot, 3 + count, [ref[...] for ref in mod_pieces]), axis=1
    )
    mine = ordered(spot, 3, [ref[...] for ref in kept])
    theirs = ordered(spot, 3, [got[4 * k : 4 * k + 4] for k in range(count)])
    cols = refs.inner[0].shape[1] // count
    for layer in range(2):
        pieces = [
            jnp.where(spot[0] == layer, first, second) for first, second in zip(mine, theirs)
        ]
        refs.biases[layer][...] = jnp.concatenate(pieces, axis=1)
        for k in range(2):
            refs.inner[layer][k : k + 1] = jnp.concatenate(
                [piece[0:1, k * cols : (k + 1) * cols] for piece in pieces], axis=1
            )


def pack_kernel(spot, mod_one, mod_two, bias_one, bias_two, refs):
    core, here, cycle = spot[0], spot[1], spot[2]
    mods = jnp.concatenate([ref[...] for ref in mod_one + mod_two], axis=0)
    cuts = len(refs.mods)
    part = mods.shape[1] // cuts
    blocks = [mods[:, j * part : (j + 1) * part] for j in range(cuts)]
    for k, ref in enumerate(refs.mods):
        index = jnp.where(cycle == 1, (here - k + cuts) % cuts, here ^ k)
        chosen = blocks[0]
        for j in range(1, cuts):
            chosen = jnp.where(index == j, blocks[j], chosen)
        ref[...] = chosen
    packs = []
    for in_bias, out_bias, mlp_bias in (bias_one, bias_two):
        shards = refs.kept.shape[0]
        rows = refs.kept.shape[2]
        cols = part // shards
        pieces = []
        for z in range(shards):
            start = jnp.concatenate(
                [
                    in_bias[:, z * cols : (z + 1) * cols],
                    in_bias[:, 2 * part + z * cols : 2 * part + (z + 1) * cols],
                    jnp.zeros((1, rows - 2 * cols), F32),
                ],
                axis=1,
            )
            here_rows = slice(z * rows, (z + 1) * rows)
            pieces.append(
                jnp.concatenate(
                    [start, mlp_bias[0:1, here_rows], out_bias[:, here_rows], mlp_bias[1:2, here_rows]],
                    axis=0,
                )
            )
        packs.append(pieces)
    for z in range(refs.kept.shape[0]):
        refs.kept[z] = jnp.where(core == 0, packs[0][z], packs[1][z])
        refs.given[z] = jnp.where(core == 0, packs[1][z], packs[0][z])


def bundle_kernel(layers):
    def kernel(spot, kept, got, refs):
        for k, layer in enumerate(layers):
            refs.rows[k] = jnp.where(spot[0] == layer, kept[k][...], got[k][...])

    return kernel


def stack_kernel(pieces, refs):
    for k, piece in enumerate(pieces):
        refs.stack[k] = piece[...]


def turn_kernel(spot, mod_pieces, given, refs):
    total = summed(mod_pieces)
    first, second = total[:6], total[6:]
    refs.kept[...] = jnp.where(spot[0] == 0, first, second)
    refs.given[:6] = jnp.where(spot[0] == 0, second, first)
    for z in range(given.shape[0]):
        refs.given[6 + 4 * z : 10 + 4 * z] = given[z]


def slots_kernel(spot, mod_kept, kept, received, refs):
    mine, theirs = mod_kept[...], received[:6]
    for k, ref in enumerate(refs.sent):
        ref[:6] = jnp.where(spot[0] == 0, mine, theirs)
        ref[6:12] = jnp.where(spot[0] == 0, theirs, mine)
        total = kept[0] + received[6:10]
        for z in range(1, kept.shape[0]):
            total = jnp.where(spot[3 + k] == z, kept[z] + received[6 + 4 * z : 10 + 4 * z], total)
        ref[12:16] = total


def sinus_features(stamps, columns):
    halfway = columns // 2
    frequency = jnp.exp(-math.log(10000.0) * jnp.arange(halfway, dtype=F32) / halfway)
    angles = stamps.astype(F32)[:, None] * frequency[None, :]
    return jnp.concatenate([jnp.cos(angles), jnp.sin(angles)], axis=-1)


def body(
    latents,
    cotangent,
    labels,
    timesteps,
    occupied,
    class_table,
    time_weight,
    project_in,
    project_in_bias,
    project_out,
    project_out_bias,
    up_weight,
    up_bias,
    down_weight,
    down_bias,
    modulate_weight,
    modulate_bias,
):
    core = lax.axis_index(SECTION)
    shard = lax.axis_index(SLOTS)
    shards = lax.axis_size(SLOTS)
    cuts = lax.axis_size(TENSOR)
    micro_count = latents.shape[0]
    width = latents.shape[3]
    own_tokens = latents.shape[2]
    tokens = own_tokens * cuts
    part = width // cuts
    rows = width // shards
    hidden_part = up_weight.shape[2]
    near = shards <= 8 and not cyclic(SLOTS) and rows == part

    def pick(first, second):
        return jnp.where(core == 0, first, second)

    spot = jnp.stack(
        [core, lax.axis_index(TENSOR), jnp.int32(1 if cyclic(TENSOR) else 0)]
        + [partner(SLOTS, k) for k in range(shards if near else 0)]
        + [partner(TENSOR, k) for k in range(cuts)]
    ).astype(jnp.int32)

    packed_own = jnp.concatenate(
        [project_in[0, :, 0], project_in[0, :, 1], project_in[0, :, 2], project_out[0].T], axis=1
    )
    stack = [packed_own, up_weight[0], down_weight[0].T]
    half = rows // 2
    given = swap(jnp.concatenate([pick(member[half:], member[:half]) for member in stack]))
    kept_halves = [pick(member[:half], member[half:]) for member in stack]
    got_halves = [given[k * half : (k + 1) * half] for k in range(3)]

    def bundle(members, wait):
        return run(
            bundle_kernel([layer for _, layer in members]),
            Named(rows=shaped((len(members), half, width), BF16)),
            spot,
            [kept_halves[k] for k, _ in members],
            [got_halves[k] for k, _ in members],
            wait=wait,
        ).rows

    def gather_blocks(members, wait=()):
        if near:
            whole = lax.all_gather(bundle(members, wait), ROWS, axis=0)
            return [Part(whole, k) for k in range(len(members))]
        return [
            gather_rows(
                pick(kept_halves[k], got_halves[k])
                if layer == 0
                else pick(got_halves[k], kept_halves[k])
            )
            for k, layer in members
        ]

    def gather_rows(value):
        return lax.all_gather(value, ROWS, axis=0, tiled=True)

    stamps = jnp.concatenate([labels.reshape(1, -1), timesteps.reshape(1, -1)], axis=1)
    if near:
        stamps = jnp.concatenate(gather_list(stamps, SLOTS), axis=0)
    else:
        stamps = lax.all_gather(stamps, SLOTS, axis=0, tiled=True)
    flat_labels = stamps[:, :micro_count].reshape(-1)
    flat_times = stamps[:, micro_count:].reshape(-1)
    class_count = class_table.shape[0]
    class_hot = flat_labels[:, None] == jnp.arange(class_count, dtype=jnp.int32)[None, :]
    time_feats = sinus_features(flat_times, time_weight.shape[0]).astype(BF16)
    condition = dot(class_hot.astype(BF16), class_table, 1, 0) + dot(time_feats, time_weight, 1, 0)
    cond_act = jax.nn.silu(condition).astype(BF16)
    act_rows = lax.dynamic_slice_in_dim(cond_act, shard * rows, rows, 1)

    if near:
        first_pieces = gather_list(pick(kept_halves[0], got_halves[0]), SLOTS)
    else:
        (first_a,) = gather_blocks([(0, 0)])

    tokens_own = pick(latents[0, 0], latents[1, 0])
    seed_own = pick(
        cotangent[0, 0] * occupied[0, 0].astype(BF16), cotangent[1, 0] * occupied[1, 0].astype(BF16)
    )
    token_list = gather_list(tokens_own, TENSOR)

    mod_weight = modulate_weight[0].reshape(rows, -1)
    bias_cols = modulate_bias.shape[2]
    bias_full = lax.dynamic_update_slice_in_dim(
        jnp.zeros((6, part), F32), modulate_bias[0].astype(F32), shard * bias_cols, 1
    )
    mod_terms = dot(act_rows, mod_weight, 1, 0) + bias_full.reshape(1, -1)
    mod_terms = mod_terms.reshape(shards, micro_count * 6, part)
    in_bias_own = project_in_bias.astype(F32).reshape(1, -1)
    bias_own = jnp.concatenate(
        [
            jnp.pad(in_bias_own, ((0, 0), (0, rows - in_bias_own.shape[1]))),
            up_bias.astype(F32),
            project_out_bias.astype(F32),
            down_bias.astype(F32),
        ],
        axis=0,
    )
    if near:
        got = exchange_list(
            [jnp.concatenate([mod_terms[k], bias_own], axis=0) for k in range(shards)], SLOTS
        )
        mod_sum = sum(member[: micro_count * 6] for member in got)
        bias_list = [member[micro_count * 6 :] for member in got]
    else:
        mod_sum = lax.psum_scatter(mod_terms, SLOTS, scatter_dimension=0, tiled=False)
        bias_all = lax.all_gather(bias_own, SLOTS, axis=0)
    if near:
        received = swap(jnp.concatenate([pick(mod_sum[6:], mod_sum[:6])] + bias_list, axis=0))
        mod_got, bias_got = received[:6], received[6:]
    else:
        mod_got, bias_got = swap(pick(mod_sum[6:], mod_sum[:6])), swap(bias_all)
    mod_kept = pick(mod_sum[:6], mod_sum[6:])
    mod_both = jnp.concatenate([pick(mod_kept, mod_got), pick(mod_got, mod_kept)], axis=0)
    mod_list = gather_list(mod_both, TENSOR)
    if near:
        ready = run(
            mods_kernel,
            Named(
                mods=shaped((12, width), F32),
                biases=[shaped((4, width), F32)] * 2,
                inner=[shaped((2, part), F32)] * 2,
            ),
            spot,
            mod_list,
            bias_list,
            bias_got,
        )
        mods, biases, in_biases = ready.mods, ready.biases, ready.inner
    else:
        mods = jnp.moveaxis(place(mod_list, TENSOR), 0, 1).reshape(12, width)
        in_biases, biases = [], []
        for member in (pick(bias_all, bias_got), pick(bias_got, bias_all)):
            cols = project_in_bias.shape[2]
            columns = member[:, 0, : 2 * cols].reshape(shards, 2, cols)
            in_biases.append(jnp.moveaxis(columns, 0, 1).reshape(2, part))
            biases.append(jnp.moveaxis(member, 0, 1).reshape(4, width))
    if near:
        stacked_pieces = run(
            stack_kernel,
            Named(stack=shaped((shards, half, width), BF16)),
            first_pieces,
            wait=tuple(mod_list[1:]),
        ).stack
        first_a = (first_pieces, swap(stacked_pieces))
    first_u, first_d, second_a = gather_blocks(
        [(1, 0), (2, 0), (0, 1)], tuple(bias_list[1:]) if near else ()
    )
    weights = [(first_a, first_u, first_d), None]

    def terms_out(count=1):
        return [shaped((own_tokens, width), F32)] + [
            shaped((own_tokens, width), BF16) for k in range(1, cuts)
        ]

    own_f32 = shaped((own_tokens, width), F32)
    both_f32 = shaped((2 * own_tokens, width), F32)
    own_b16 = shaped((own_tokens, width), BF16)
    attend_flops = 2 * tokens * width * width + 4 * tokens * tokens * part
    mlp_flops = 4 * tokens * width * hidden_part

    kept, packs = [], []
    inputs = tokens_own
    first = token_list
    for layer in range(2):
        packed, upper, lower = weights[layer]
        outs = Named(kept=shaped((tokens, (3 - layer) * width), BF16), terms=terms_out())
        if isinstance(packed, tuple):
            outs.packed = shaped((width, width), BF16)
        attn = run(
            attend_kernel(layer),
            outs,
            spot,
            first,
            mods,
            packed,
            in_biases[layer],
            flops=attend_flops,
        )
        packs.append(attn.packed if isinstance(packed, tuple) else packed)
        if layer == 0:
            second_u, second_d = gather_blocks([(1, 1), (2, 1)], (attn.kept,))
            weights[1] = (second_a, second_u, second_d)
        middle = run(
            middle_kernel(layer),
            Named(kept=both_f32, mlp_in=own_b16),
            exchange_list(attn.terms, TENSOR),
            inputs,
            mods,
            biases[layer],
        )
        mlp = run(
            mlp_kernel,
            Named(kept=shaped((tokens, width + 2 * hidden_part), BF16), terms=terms_out()),
            gather_list(middle.mlp_in, TENSOR),
            upper,
            lower,
            biases[layer],
            flops=mlp_flops,
        )
        outs = Named(mlp_out=own_f32, output=own_b16)
        if layer == 0:
            outs.attn_in = own_b16
        last = run(
            last_kernel(layer),
            outs,
            exchange_list(mlp.terms, TENSOR),
            middle.kept,
            mods,
            biases[layer],
        )
        kept.append((inputs, attn, middle, mlp, last))
        inputs = last.output
        if layer == 0:
            first = gather_list(last.attn_in, TENSOR)
            seed_list = gather_list(seed_own, TENSOR)

    row = shaped((1, width), F32)
    grad_own, pieces = seed_own, seed_list
    mod_rows, bias_rows, blocks, input_grads = [None] * 2, [None] * 2, [None] * 2, [None] * 2
    wait = ()
    for layer in (1, 0):
        packed, upper, lower = packs[layer], weights[layer][1], weights[layer][2]
        inputs, attn, middle, mlp, last = kept[layer]
        mlp_back = run(
            mlp_back_kernel(layer),
            Named(
                grads=shaped((tokens, width + hidden_part), BF16),
                terms=terms_out(),
                bias=shaped((2, hidden_part), F32),
            ),
            pieces,
            mods,
            upper,
            lower,
            mlp.kept,
            flops=mlp_flops,
        )
        mlp_grads = run(
            mlp_grads_kernel,
            Named(grads=shaped((2 * shards, 2, rows, width // 2), BF16)),
            mlp.kept,
            mlp_back.grads,
            flops=mlp_flops,
        ).grads
        middle_back = run(
            middle_back_kernel(layer),
            Named(
                middle_grad=own_f32,
                outer=own_b16,
                rows=shaped((4, width), F32),
            ),
            exchange_list(mlp_back.terms, TENSOR),
            grad_own,
            middle.kept,
            last.mlp_out,
            mods,
        )
        outs = Named(
            grads=shaped((tokens, width + 3 * part), BF16),
            terms=terms_out(),
            out_bias=row,
            in_bias=shaped((1, 3 * part), F32),
        )
        if layer == 0:
            outs.rows = shaped((2, width), F32)
        attn_back = run(
            attend_back_kernel(layer),
            outs,
            gather_list(middle_back.outer, TENSOR),
            packed,
            attn.kept,
            flops=2 * attend_flops,
            wait=wait,
        )
        operands = (attn.kept, attn_back.grads)
        if layer == 1 or not near:
            attn_grads = run(
                attend_grads_kernel,
                Named(grads=shaped((2 * shards, 1, rows, width // 2), BF16)),
                *operands,
                flops=2 * tokens * width * width,
            ).grads
        else:
            attn_grads = run(
                attend_halves_kernel,
                Named(kept=shaped((width, width // 2), F32), given=shaped((width, width // 2), BF16)),
                spot,
                *operands,
                flops=2 * tokens * width * width,
            )
        outs = Named(input_grad=own_f32)
        if layer == 1:
            outs.rows, outs.grad, outs.lower = shaped((2, width), F32), own_b16, own_b16
        first_back = run(
            first_back_kernel(layer),
            outs,
            exchange_list(attn_back.terms, TENSOR),
            middle_back.middle_grad,
            inputs,
            mods,
        )
        input_grads[layer] = first_back.input_grad
        mod_rows[layer] = [
            attn_back.rows if layer == 0 else first_back.rows,
            middle_back.rows,
        ]
        bias_rows[layer] = (attn_back.in_bias, attn_back.out_bias, mlp_back.bias)

        def scatter(grads):
            return lax.psum_scatter(grads, ROWS, scatter_dimension=0, tiled=False)

        if layer == 1:
            blocks[1] = scatter(jnp.concatenate([mlp_grads, attn_grads], axis=1))
            grad_own = first_back.grad
            pieces = gather_list(first_back.lower, TENSOR)
            wait = (blocks[1],)
        else:
            mlp_block = scatter(mlp_grads)
            if near:
                shares = run(
                    share_kernel,
                    Named(
                        own=shaped((rows, width // 2), F32),
                        sent=[shaped((rows, width // 2), BF16)] * (shards - 1),
                    ),
                    spot,
                    attn_grads.kept,
                    swap(attn_grads.given),
                )
                got = exchange_list([shares.own] + shares.sent, SLOTS)
                attn_block = sum(member.astype(F32) for member in got)[None].astype(BF16)
            else:
                attn_block = scatter(attn_grads)
            blocks[0] = jnp.concatenate([mlp_block, attn_block], axis=0)

    given = swap(pick(blocks[1], blocks[0]))
    own = pick(blocks[0], blocks[1])
    grads = jnp.concatenate([pick(own, given), pick(given, own)], axis=2).astype(F32)
    grad_upper, grad_lower = grads[0], grads[1].T
    grad_inner = grads[2, :, : 3 * part].reshape(rows, 3, part)
    grad_outer = grads[2, :, 3 * part :].T

    tail = run(
        pack_kernel,
        Named(mods=[shaped((12, part), F32) for k in range(cuts)],
            kept=shaped((shards, 4, rows), F32),
            given=shaped((shards, 4, rows), F32),
        ),
        spot,
        mod_rows[0],
        mod_rows[1],
        bias_rows[0],
        bias_rows[1],
    )
    mod_list = exchange_list(tail.mods, TENSOR)
    if near:
        turned = run(
            turn_kernel,
            Named(kept=shaped((6, part), F32), given=shaped((6 + 4 * shards, part), F32)),
            spot,
            mod_list,
            tail.given,
        )
        sent = run(
            slots_kernel,
            Named(sent=[shaped((16, part), F32)] * shards),
            spot,
            turned.kept,
            tail.kept,
            swap(turned.given),
            wait=(shares.own,),
        ).sent
        got = exchange_list(sent, SLOTS)
        mod_slots = jnp.concatenate([member[:12] for member in got], axis=0)
        bias_total = sum(member[12:] for member in got)
    else:
        mod_shard = sum(mod_list)
        mod_given, mod_kept = pick(mod_shard[6:], mod_shard[:6]), pick(mod_shard[:6], mod_shard[6:])
        mod_got, bias_got = swap(mod_given), swap(tail.given)
        mod_micro = jnp.concatenate([pick(mod_kept, mod_got), pick(mod_got, mod_kept)], axis=0)
        bias_sum = tail.kept + bias_got
        mod_slots = lax.all_gather(mod_micro, SLOTS, axis=0, tiled=True)
        bias_total = lax.psum_scatter(bias_sum, SLOTS, scatter_dimension=0, tiled=False)
    mod_slots = mod_slots.reshape(shards * micro_count, 6 * part)
    act_grad = lax.dot_general(
        mod_slots, mod_weight.astype(F32), (((1,), (1,)), ((), ())), precision=HIGH
    )
    act_grad = act_grad + swap(act_grad)
    act_grad = sum(gather_list(act_grad, TENSOR))
    if near:
        act_list = []
        for k, member in enumerate(gather_list(act_grad, SLOTS)):
            member = member.reshape(shards, micro_count, rows)
            act_list.append(jnp.concatenate([member[j ^ k] for j in range(shards)], axis=0))
        act_all = place(act_list, SLOTS)
    else:
        act_all = lax.all_gather(act_grad, SLOTS, axis=0)
    act_all = jnp.moveaxis(act_all, 0, 1).reshape(-1, width)
    cond_grad = jax.vjp(jax.nn.silu, condition)[1](act_all)[0]
    table_grad = lax.dot_general(
        class_hot.astype(F32), cond_grad, (((0,), (0,)), ((), ())), precision=HIGH
    )
    time_grad = lax.dot_general(
        time_feats.astype(F32), cond_grad, (((0,), (0,)), ((), ())), precision=HIGH
    )
    grad_mod_weight = lax.dot_general(
        act_rows.astype(F32), mod_slots, (((0,), (0,)), ((), ())), precision=HIGH
    ).reshape(rows, 6, part)
    mod_bias_sum = jnp.sum(mod_slots, axis=0).reshape(6, part)
    grad_mod_bias = lax.dynamic_slice_in_dim(mod_bias_sum, shard * bias_cols, bias_cols, 1)
    grad_in_bias = bias_total[0, : in_bias_own.shape[1]].reshape(2, -1)

    def by_micro(first, second):
        got = swap(pick(second, first))
        held = pick(first, second)
        return jnp.stack([pick(held, got), pick(got, held)])[None, :, None]

    return (
        by_micro(kept[0][4].output, kept[1][4].output),
        by_micro(input_grads[0], input_grads[1]),
        table_grad,
        time_grad,
        grad_inner[None],
        grad_in_bias[None],
        grad_outer[None],
        bias_total[2][None],
        grad_upper[None],
        bias_total[1][None],
        grad_lower[None],
        bias_total[3][None],
        grad_mod_weight[None],
        grad_mod_bias[None],
    )


def solution(mesh):
    in_specs = (
        P(None, SLOTS, TENSOR, None),
        P(None, SLOTS, TENSOR, None),
        P(None, SLOTS),
        P(None, SLOTS),
        P(None, SLOTS),
        P(),
        P(),
        P(SECTION, SLOTS, None, TENSOR),
        P(SECTION, None, (TENSOR, SLOTS)),
        P(SECTION, TENSOR, SLOTS),
        P(SECTION, SLOTS),
        P(SECTION, SLOTS, TENSOR),
        P(SECTION, (TENSOR, SLOTS)),
        P(SECTION, TENSOR, SLOTS),
        P(SECTION, SLOTS),
        P(SECTION, SLOTS, None, TENSOR),
        P(SECTION, None, (TENSOR, SLOTS)),
    )
    out_specs = (
        P(SECTION, None, SLOTS, TENSOR, None),
        P(SECTION, None, SLOTS, TENSOR, None),
        P(),
        P(),
        P(SECTION, SLOTS, None, TENSOR),
        P(SECTION, None, (TENSOR, SLOTS)),
        P(SECTION, TENSOR, SLOTS),
        P(SECTION, SLOTS),
        P(SECTION, SLOTS, TENSOR),
        P(SECTION, (TENSOR, SLOTS)),
        P(SECTION, TENSOR, SLOTS),
        P(SECTION, SLOTS),
        P(SECTION, SLOTS, None, TENSOR),
        P(SECTION, None, (TENSOR, SLOTS)),
    )
    return jax.shard_map(body, mesh=mesh, in_specs=in_specs, out_specs=out_specs, check_vma=False)
```

```python
import math
from types import SimpleNamespace as Named

import jax
import jax.numpy as jnp
from jax import lax
from jax.experimental import pallas as pl
from jax.experimental.pallas import tpu as pltpu
from jax.sharding import PartitionSpec as P

HD = 64
EPS = 1e-06
HIGH = lax.Precision.HIGHEST
F32 = jnp.float32
BF16 = jnp.bfloat16
SECTION, TENSOR, SLOTS = "section", "tensor", "dp"
LAYER = (SECTION, TENSOR)
ROWS = (SLOTS, SECTION)
SPACE = 40 * 1024 * 1024


def cyclic(axis):
    size = lax.axis_size(axis)
    return size & (size - 1) != 0


def exchange(value, axis, k):
    size = lax.axis_size(axis)
    if cyclic(axis):
        return lax.ppermute(value, axis, [(i, (i - k) % size) for i in range(size)])
    return lax.ppermute(value, axis, [(i, i ^ k) for i in range(size)])


def fetch(value, axis, k):
    size = lax.axis_size(axis)
    if cyclic(axis):
        return lax.ppermute(value, axis, [(i, (i + k) % size) for i in range(size)])
    return lax.ppermute(value, axis, [(i, i ^ k) for i in range(size)])


def partner(axis, k):
    here = lax.axis_index(axis)
    if cyclic(axis):
        return (here - k) % lax.axis_size(axis)
    return here ^ k


def swap(value):
    return lax.ppermute(value, SECTION, [(0, 1), (1, 0)])


def across(value, axis):
    return lax.all_to_all(value, axis, 0, 0)


def gather_list(value, axis):
    return [value] + [fetch(value, axis, k) for k in range(1, lax.axis_size(axis))]


def exchange_list(values, axis):
    return [values[0]] + [exchange(values[k], axis, k) for k in range(1, lax.axis_size(axis))]


def place(pieces, axis):
    out = jnp.zeros((len(pieces),) + pieces[0].shape, pieces[0].dtype)
    for k, piece in enumerate(pieces):
        out = lax.dynamic_update_index_in_dim(out, piece, partner(axis, k), 0)
    return out


def shaped(shape, dtype):
    return jax.ShapeDtypeStruct(shape, dtype)


class Part:
    def __init__(self, value, at=None):
        self.value, self.at = value, at
        self.shape, self.dtype = value.shape, value.dtype


def run(kernel, outs, *args, flops=0, wait=()):
    def leafy(value):
        return isinstance(value, Part)

    names = list(vars(outs))
    out_flat, out_tree = jax.tree.flatten([vars(outs)[name] for name in names])
    flat, tree = jax.tree.flatten(args, is_leaf=leafy)
    moved = sum(math.prod(leaf.shape) * leaf.dtype.itemsize for leaf in flat + out_flat)

    def inner(*refs):
        ins = list(refs[: len(flat)])
        for k, leaf in enumerate(flat):
            if leafy(leaf) and leaf.at is not None:
                ins[k] = Named(ref=ins[k], at=leaf.at)
        results = jax.tree.unflatten(out_tree, refs[len(flat) + len(wait) :])
        kernel(*jax.tree.unflatten(tree, ins), Named(**dict(zip(names, results))))

    result = pl.pallas_call(
        inner,
        out_shape=out_flat,
        in_specs=[
            pl.BlockSpec(memory_space=pltpu.SMEM if leaf.dtype == jnp.int32 else pltpu.VMEM)
            for leaf in flat
        ]
        + [pl.BlockSpec(memory_space=pl.ANY)] * len(wait),
        out_specs=[pl.BlockSpec(memory_space=pltpu.VMEM)] * len(out_flat),
        compiler_params=pltpu.CompilerParams(vmem_limit_bytes=SPACE),
        cost_estimate=pl.CostEstimate(flops=flops, bytes_accessed=moved, transcendentals=0),
    )(*[leaf.value if leafy(leaf) else leaf for leaf in flat], *wait)
    return Named(**dict(zip(names, jax.tree.unflatten(out_tree, result))))


def matrix(ref):
    if isinstance(ref, Named):
        value = ref.ref[:, ref.at]
        return value.reshape(-1, value.shape[-1])
    return ref[...]


def norm_parts(values):
    average = jnp.mean(values, axis=-1, keepdims=True)
    centred = values - average
    spread = jnp.mean(centred * centred, axis=-1, keepdims=True)
    scale = lax.rsqrt(spread + EPS)
    return centred * scale, scale


def norm_pull(grad, normed, scale):
    first = jnp.mean(grad, axis=-1, keepdims=True)
    second = jnp.mean(grad * normed, axis=-1, keepdims=True)
    return scale * (grad - first - normed * second)


def dot(left, right, left_dim, right_dim):
    return lax.dot_general(
        left, right, (((left_dim,), (right_dim,)), ((), ())), preferred_element_type=F32
    )


def joined(refs):
    return jnp.concatenate([ref[...] for ref in refs], axis=0)


def summed(refs):
    total = refs[0][...].astype(F32)
    for ref in refs[1:]:
        total = total + ref[...].astype(F32)
    return total


def spread_out(terms, refs):
    rows = refs[0].shape[0]
    for k, ref in enumerate(refs):
        ref[...] = terms[k * rows : (k + 1) * rows].astype(ref.dtype)


def column_sum(values):
    return jnp.sum(values.astype(F32), axis=0, keepdims=True)


def softmax_parts(query, key):
    scores = dot(query, key, 1, 1) * HD**-0.5
    raised = jnp.exp(scores - jnp.max(scores, axis=-1, keepdims=True))
    return raised / jnp.sum(raised, axis=-1, keepdims=True)


def assemble(spot, pieces, ref):
    own, other = pieces
    rows = own.shape[1]
    for k in range(own.shape[0]):
        for half, block in ((spot[0], own[k]), (1 - spot[0], other[k])):
            at = pl.multiple_of((2 * spot[3 + k] + half) * rows, rows)
            ref[pl.ds(at, rows), :] = block


def attend(first, mods, packed, in_bias, refs, layer):
    width = packed.shape[1] // 4
    attn_in = joined(first)
    if layer == 0:
        refs.kept[:, 2 * packed.shape[1] :] = attn_in
        normed = norm_parts(attn_in.astype(F32))[0]
        attn_in = (normed * (1.0 + mods[1:2]) + mods[0:1]).astype(BF16)
    refs.kept[:, : packed.shape[1]] = attn_in
    projected = dot(attn_in, packed[:, : 3 * width], 1, 0)
    queries = (projected[:, :width] + in_bias[0:1]).astype(BF16)
    keys = projected[:, width : 2 * width].astype(BF16)
    values = (projected[:, 2 * width :] + in_bias[1:2]).astype(BF16)
    mixed = []
    for at in range(0, width, HD):
        attention = softmax_parts(queries[:, at : at + HD], keys[:, at : at + HD])
        mixed.append(dot(attention.astype(BF16), values[:, at : at + HD], 1, 0))
    mixed = jnp.concatenate(mixed, axis=1).astype(BF16)
    refs.kept[:, packed.shape[1] : 2 * packed.shape[1]] = jnp.concatenate(
        [queries, keys, values, mixed], axis=1
    )
    spread_out(dot(mixed, packed[:, 3 * width :], 1, 1), refs.terms)


def attend_kernel(layer):
    def kernel(spot, first, mods_ref, packed_ref, bias_ref, refs):
        if isinstance(packed_ref, tuple):
            assemble(spot, packed_ref, refs.packed)
            packed_ref = refs.packed
        attend(first, mods_ref[6 * layer : 6 * layer + 6], matrix(packed_ref), bias_ref[...], refs, layer)

    return kernel


def middle_kernel(layer):
    def kernel(terms, inputs, mods_ref, bias_ref, refs):
        mods = mods_ref[6 * layer : 6 * layer + 6]
        attn_out = summed(terms) + bias_ref[2:3]
        rows = attn_out.shape[0]
        refs.kept[:rows] = attn_out
        middle = inputs[...].astype(F32) + mods[2:3] * attn_out
        refs.kept[rows:] = middle
        normed = norm_parts(middle)[0]
        refs.mlp_in[...] = (normed * (1.0 + mods[4:5]) + mods[3:4]).astype(BF16)

    return kernel


def mlp_kernel(pieces, upper, lower, bias_ref, refs):
    mlp_in = joined(pieces)
    size = upper.ref.shape[-1] if isinstance(upper, Named) else upper.shape[-1]
    wide = mlp_in.shape[1]
    refs.kept[:, :wide] = mlp_in
    values = dot(mlp_in, matrix(upper), 1, 0) + bias_ref[1:2]
    root = math.sqrt(2.0 / math.pi)
    square = values * values
    bent = jnp.tanh(root * (values + 0.044715 * values * square))
    hidden = (0.5 * values * (1.0 + bent)).astype(BF16)
    refs.kept[:, wide : wide + size] = hidden
    slope = 0.5 * (1.0 + bent) + 0.5 * values * (1.0 - bent * bent) * root * (
        1.0 + 0.134145 * square
    )
    refs.kept[:, wide + size :] = slope.astype(BF16)
    spread_out(dot(hidden, matrix(lower), 1, 1), refs.terms)


def last_kernel(layer):
    def kernel(terms, kept, mods_ref, bias_ref, refs):
        mlp_out = summed(terms) + bias_ref[3:4]
        refs.mlp_out[...] = mlp_out
        output = (kept[kept.shape[0] // 2 :] + mods_ref[6 * layer + 5 : 6 * layer + 6] * mlp_out).astype(BF16)
        refs.output[...] = output
        if layer == 0:
            normed = norm_parts(output.astype(F32))[0]
            refs.attn_in[...] = (normed * (1.0 + mods_ref[7:8]) + mods_ref[6:7]).astype(BF16)

    return kernel


def mlp_back_kernel(layer):
    def kernel(pieces, mods_ref, upper, lower, kept, refs):
        lower_grad = joined(pieces)
        if layer == 1:
            lower_grad = (lower_grad.astype(F32) * mods_ref[11:12]).astype(BF16)
        wide = lower_grad.shape[1]
        refs.grads[:, :wide] = lower_grad
        pre_grad = dot(lower_grad, matrix(lower), 1, 0)
        slope = kept[:, wide + pre_grad.shape[1] :].astype(F32)
        pre_grad = (pre_grad * slope).astype(BF16)
        refs.grads[:, wide:] = pre_grad
        spread_out(dot(pre_grad, matrix(upper), 1, 1), refs.terms)
        refs.bias[0:1] = column_sum(pre_grad)
        refs.bias[1:2] = column_sum(lower_grad)

    return kernel


def middle_back_kernel(layer):
    def kernel(terms, grad_ref, kept, mlp_out, mods_ref, refs):
        mods = mods_ref[6 * layer : 6 * layer + 6]
        grad = grad_ref[...].astype(F32)
        mid_grad = summed(terms)
        normed, scale = norm_parts(kept[kept.shape[0] // 2 :])
        middle_grad = grad + norm_pull(mid_grad * (1.0 + mods[4:5]), normed, scale)
        refs.middle_grad[...] = middle_grad
        refs.outer[...] = (middle_grad * mods[2:3]).astype(BF16)
        refs.rows[0:1] = column_sum(middle_grad * kept[: kept.shape[0] // 2])
        refs.rows[1:2] = column_sum(mid_grad)
        refs.rows[2:3] = column_sum(mid_grad * normed)
        refs.rows[3:4] = column_sum(grad * mlp_out[...])

    return kernel


def attend_back_kernel(layer):
    def kernel(pieces, packed, kept, others, refs):
        outer_grad = joined(pieces)
        wide = outer_grad.shape[1]
        refs.grads[:, :wide] = outer_grad
        packed = matrix(packed)
        width = packed.shape[1] // 4
        mixed_grad = dot(outer_grad, packed[:, 3 * width :], 1, 0).astype(BF16)
        queries, keys, values = [
            kept[:, wide + k * width : wide + (k + 1) * width] for k in range(3)
        ]
        d_queries, d_keys, d_values = [], [], []
        for at in range(0, width, HD):
            query, key = queries[:, at : at + HD], keys[:, at : at + HD]
            grad = mixed_grad[:, at : at + HD]
            attention = softmax_parts(query, key)
            weight_grad = dot(grad, values[:, at : at + HD], 1, 1)
            d_values.append(dot(attention.astype(BF16), grad, 0, 0))
            row_dot = jnp.sum(attention * weight_grad, axis=-1, keepdims=True)
            score_grad = (attention * (weight_grad - row_dot)).astype(BF16)
            d_queries.append(dot(score_grad, key, 1, 0) * HD**-0.5)
            d_keys.append(dot(score_grad, query, 0, 0) * HD**-0.5)
        stacked = jnp.concatenate(d_queries + d_keys + d_values, axis=1).astype(BF16)
        refs.grads[:, wide:] = stacked
        terms = dot(stacked, packed[:, : 3 * width], 1, 1)
        if others is None:
            spread_out(terms, refs.terms)
        else:
            refs.terms[...] = terms
        in_bias, out_bias = column_sum(stacked), column_sum(outer_grad)
        refs.out_bias[...] = out_bias
        refs.in_bias[...] = in_bias
        if layer == 0:
            normed = norm_parts(kept[:, 2 * wide :].astype(F32))[0]
            rows = jnp.concatenate([column_sum(terms), column_sum(terms * normed)], axis=0)
            if others is None:
                refs.rows[...] = rows
            else:
                middle_rows, mlp_bias, other_rows, other_bias = others
                mods = [
                    jnp.concatenate([rows, middle_rows[...]], axis=0),
                    jnp.concatenate([ref[...] for ref in other_rows], axis=0),
                ]
                send_rows(mods, [(in_bias, out_bias, mlp_bias), other_bias], refs.sent)

    return kernel


def first_back_kernel(layer):
    def kernel(terms, middle_grad, inputs, mods_ref, refs):
        in_grad = summed(terms)
        normed, scale = norm_parts(inputs[...].astype(F32))
        scale_one = mods_ref[6 * layer + 1 : 6 * layer + 2]
        input_grad = middle_grad[...] + norm_pull(in_grad * (1.0 + scale_one), normed, scale)
        refs.input_grad[...] = input_grad
        if layer == 1:
            refs.rows[0:1] = column_sum(in_grad)
            refs.rows[1:2] = column_sum(in_grad * normed)
            rounded = input_grad.astype(BF16)
            refs.grad[...] = rounded
            refs.lower[...] = (rounded.astype(F32) * mods_ref[5:6]).astype(BF16)

    return kernel


def cut(grad, ref, at):
    count, rows, half = ref.shape[0], ref.shape[2], ref.shape[3]
    for block in range(count):
        place_at = block // 2 * rows
        ref[block, at] = grad[
            place_at : place_at + rows, block % 2 * half : block % 2 * half + half
        ].astype(BF16)


def grads_kernel(mlp_kept, mlp_grads, attn_kept, attn_grads, refs):
    wide = 2 * refs.grads.shape[3]
    size, width = mlp_grads.shape[1] - wide, wide // 4
    cut(dot(mlp_kept[:, :wide], mlp_grads[:, wide:], 0, 0), refs.grads, 0)
    cut(dot(mlp_grads[:, :wide], mlp_kept[:, wide : wide + size], 0, 0), refs.grads, 1)
    inner = dot(attn_kept[:, :wide], attn_grads[:, wide:], 0, 0)
    outer = dot(attn_grads[:, :wide], attn_kept[:, wide + 3 * width : 2 * wide], 0, 0)
    cut(jnp.concatenate([inner, outer], axis=1), refs.grads, 2)


def mods_kernel(spot, got, refs):
    cuts = got.shape[0] // 2
    count = (got.shape[1] - 6) // 4
    cols = refs.inner[0].shape[1] // count
    for layer in range(2):
        refs.mods[6 * layer : 6 * layer + 6] = jnp.concatenate(
            [got[cuts * layer + t, :6] for t in range(cuts)], axis=1
        )
        rows = got[cuts * layer + spot[1], 6:]
        pieces = [rows[4 * k : 4 * k + 4] for k in range(count)]
        refs.biases[layer][...] = jnp.concatenate(pieces, axis=1)
        for k in range(2):
            refs.inner[layer][k : k + 1] = jnp.concatenate(
                [piece[0:1, k * cols : (k + 1) * cols] for piece in pieces], axis=1
            )


def bias_rows_of(part, rows, shards, in_bias, out_bias, mlp_bias):
    cols = part // shards
    pieces = []
    for z in range(shards):
        start = jnp.concatenate(
            [
                in_bias[:, z * cols : (z + 1) * cols],
                in_bias[:, 2 * part + z * cols : 2 * part + (z + 1) * cols],
                jnp.zeros((1, rows - 2 * cols), F32),
            ],
            axis=1,
        )
        at = slice(z * rows, (z + 1) * rows)
        pieces += [start, mlp_bias[0:1, at], out_bias[:, at], mlp_bias[1:2, at]]
    return jnp.concatenate(pieces, axis=0)


def send_rows(mods, biases, sent):
    cuts, part = sent.shape[0] // 2, sent.shape[2]
    shards = (sent.shape[1] - 6) // 4
    for layer in range(2):
        rows = bias_rows_of(part, part, shards, *biases[layer])
        for t in range(cuts):
            sent[cuts * layer + t, :6] = mods[layer][:, t * part : (t + 1) * part]
            sent[cuts * layer + t, 6:] = rows


def pack_kernel(spot, mod_one, mod_two, bias_one, bias_two, refs):
    core, here, cycle = spot[0], spot[1], spot[2]
    mods = jnp.concatenate([ref[...] for ref in mod_one + mod_two], axis=0)
    cuts = len(refs.mods)
    part = mods.shape[1] // cuts
    blocks = [mods[:, j * part : (j + 1) * part] for j in range(cuts)]
    for k, ref in enumerate(refs.mods):
        index = jnp.where(cycle == 1, (here - k + cuts) % cuts, here ^ k)
        chosen = blocks[0]
        for j in range(1, cuts):
            chosen = jnp.where(index == j, blocks[j], chosen)
        ref[...] = chosen
    shards, _, rows = refs.kept.shape
    first = bias_rows_of(part, rows, shards, *bias_one)
    second = bias_rows_of(part, rows, shards, *bias_two)
    for z in range(shards):
        at = slice(4 * z, 4 * z + 4)
        refs.kept[z] = jnp.where(core == 0, first[at], second[at])
        refs.given[z] = jnp.where(core == 0, second[at], first[at])


def bundle_kernel(members):
    def kernel(spot, kept, got, refs):
        for k, (weight, layer) in enumerate(members):
            refs.rows[k] = jnp.where(spot[0] == layer, kept[weight], got[weight])

    return kernel


def slots_kernel(spot, received, refs):
    cuts = received.shape[0] // 2
    shards = (received.shape[1] - 6) // 4
    mods = []
    for micro in range(2):
        total = received[cuts * micro, :6]
        for t in range(1, cuts):
            total = total + received[cuts * micro + t, :6]
        mods.append(total)
    here = spot[1]
    biases = received[here, 6:] + received[cuts + here, 6:]
    for k, ref in enumerate(refs.sent):
        ref[:6], ref[6:12] = mods
        total = biases[:4]
        for z in range(1, shards):
            total = jnp.where(spot[3 + k] == z, biases[4 * z : 4 * z + 4], total)
        ref[12:16] = total


def modulate_kernel(act, weights, mod_bias, own, refs):
    shards, _, part = refs.sent.shape
    micro = act.shape[0] // shards
    for k in range(6):
        terms = dot(act[...], weights[k], 1, 0) + mod_bias[k : k + 1]
        for z in range(shards):
            for m in range(micro):
                at = z * micro + m
                refs.sent[z, 6 * m + k : 6 * m + k + 1] = terms[at : at + 1]
    for z in range(shards):
        refs.sent[z, 6 * micro :] = own[...]


def assemble_kernel(spot, first, second, given, refs):
    wide = []
    for k in range(3):
        own = jnp.where(spot[0] == 0, first[k], second[k]).astype(F32)
        other = given[k].astype(F32)
        left, right = jnp.where(spot[0] == 0, own, other), jnp.where(spot[0] == 0, other, own)
        wide.append(jnp.concatenate([left, right], axis=1))
    refs.upper[...], refs.lower[...] = wide[0], wide[1]
    width = wide[2].shape[1] // 4
    for k in range(3):
        refs.inner[k] = wide[2][:, k * width : (k + 1) * width]
    refs.outer[...] = wide[2][:, 3 * width :].T


def split_kernel(terms, refs):
    spread_out(terms[...], refs.terms)


def prepare_kernel(spot, inner, outer, upper, lower, refs):
    half = upper.shape[0] // 2
    packed = jnp.concatenate([inner[0], inner[1], inner[2], outer[...].T], axis=1)
    for k, member in enumerate((packed, upper[...], lower[...])):
        first, second = member[:half], member[half:]
        refs.kept[k] = jnp.where(spot[0] == 0, first, second)
        refs.given[k] = jnp.where(spot[0] == 0, second, first)


def sinus_features(stamps, columns):
    halfway = columns // 2
    frequency = jnp.exp(-math.log(10000.0) * jnp.arange(halfway, dtype=F32) / halfway)
    angles = stamps.astype(F32)[:, None] * frequency[None, :]
    return jnp.concatenate([jnp.cos(angles), jnp.sin(angles)], axis=-1)


def body(
    latents,
    cotangent,
    labels,
    timesteps,
    occupied,
    class_table,
    time_weight,
    project_in,
    project_in_bias,
    project_out,
    project_out_bias,
    up_weight,
    up_bias,
    down_weight,
    down_bias,
    modulate_weight,
    modulate_bias,
):
    core = lax.axis_index(SECTION)
    shard = lax.axis_index(SLOTS)
    shards = lax.axis_size(SLOTS)
    cuts = lax.axis_size(TENSOR)
    micro_count = latents.shape[0]
    width = latents.shape[3]
    own_tokens = latents.shape[2]
    tokens = own_tokens * cuts
    part = width // cuts
    rows = width // shards
    hidden_part = up_weight.shape[2]
    near = shards <= 8 and not cyclic(SLOTS) and rows == part

    def pick(first, second):
        return jnp.where(core == 0, first, second)

    spot = jnp.stack(
        [core, lax.axis_index(TENSOR), jnp.int32(1 if cyclic(TENSOR) else 0)]
        + [partner(SLOTS, k) for k in range(shards if near else 0)]
        + [partner(TENSOR, k) for k in range(cuts)]
    ).astype(jnp.int32)

    half = rows // 2
    if near:
        inner = jnp.moveaxis(project_in[0], 1, 0)
        ready = run(
            prepare_kernel,
            Named(kept=shaped((3, half, width), BF16), given=shaped((3, half, width), BF16)),
            spot,
            inner,
            project_out[0],
            up_weight[0],
            down_weight[0].T,
        )
        given = swap(ready.given)
        kept_halves, got_halves = ready.kept, given
    else:
        packed_own = jnp.concatenate(
            [project_in[0, :, 0], project_in[0, :, 1], project_in[0, :, 2], project_out[0].T], axis=1
        )
        stack = [packed_own, up_weight[0], down_weight[0].T]
        given = swap(jnp.concatenate([pick(member[half:], member[:half]) for member in stack]))
        kept_halves = [pick(member[:half], member[half:]) for member in stack]
        got_halves = [given[k * half : (k + 1) * half] for k in range(3)]

    def bundle(members, wait):
        return run(
            bundle_kernel(members),
            Named(rows=shaped((len(members), half, width), BF16)),
            spot,
            kept_halves,
            got_halves,
            wait=wait,
        ).rows

    def gather_blocks(members, wait=()):
        if near:
            whole = lax.all_gather(bundle(members, wait), ROWS, axis=0)
            return [Part(whole, k) for k in range(len(members))]
        return [
            gather_rows(
                pick(kept_halves[k], got_halves[k])
                if layer == 0
                else pick(got_halves[k], kept_halves[k])
            )
            for k, layer in members
        ]

    def gather_rows(value):
        return lax.all_gather(value, ROWS, axis=0, tiled=True)

    stamps = jnp.concatenate([labels.reshape(1, -1), timesteps.reshape(1, -1)], axis=1)
    if near:
        stamps = place(gather_list(stamps, SLOTS), SLOTS).reshape(shards, -1)
    else:
        stamps = lax.all_gather(stamps, SLOTS, axis=0, tiled=True)
    flat_labels = stamps[:, :micro_count].reshape(-1)
    flat_times = stamps[:, micro_count:].reshape(-1)
    class_count = class_table.shape[0]
    class_hot = flat_labels[:, None] == jnp.arange(class_count, dtype=jnp.int32)[None, :]
    time_feats = sinus_features(flat_times, time_weight.shape[0]).astype(BF16)
    condition = dot(class_hot.astype(BF16), class_table, 1, 0) + dot(time_feats, time_weight, 1, 0)
    cond_act = jax.nn.silu(condition).astype(BF16)
    act_rows = lax.dynamic_slice_in_dim(cond_act, shard * rows, rows, 1)

    if near:
        first_pieces = gather_list(pick(kept_halves[0], got_halves[0]), SLOTS)
    else:
        (first_a,) = gather_blocks([(0, 0)])

    tokens_own = pick(latents[0, 0], latents[1, 0])
    seed_own = pick(
        cotangent[0, 0] * occupied[0, 0].astype(BF16), cotangent[1, 0] * occupied[1, 0].astype(BF16)
    )
    token_list = gather_list(tokens_own, TENSOR)

    mod_weight = modulate_weight[0].reshape(rows, -1)
    bias_cols = modulate_bias.shape[2]
    bias_full = lax.dynamic_update_slice_in_dim(
        jnp.zeros((6, part), F32), modulate_bias[0].astype(F32), shard * bias_cols, 1
    )
    mod_terms = dot(act_rows, mod_weight, 1, 0) + bias_full.reshape(1, -1)
    mod_terms = mod_terms.reshape(shards, micro_count * 6, part)
    in_bias_own = project_in_bias.astype(F32).reshape(1, -1)
    bias_own = jnp.concatenate(
        [
            jnp.pad(in_bias_own, ((0, 0), (0, rows - in_bias_own.shape[1]))),
            up_bias.astype(F32),
            project_out_bias.astype(F32),
            down_bias.astype(F32),
        ],
        axis=0,
    )
    if near:
        sent = run(
            modulate_kernel,
            Named(sent=shaped((shards, 6 * micro_count + 4, part), F32)),
            act_rows,
            jnp.moveaxis(modulate_weight[0], 1, 0),
            bias_full,
            bias_own,
        ).sent
        got = across(sent, SLOTS)
        mod_sum = jnp.sum(got[:, : micro_count * 6], axis=0).reshape(micro_count, 6, part)
        bias_all = jnp.broadcast_to(
            got[:, micro_count * 6 :].reshape(1, 4 * shards, part), (micro_count, 4 * shards, part)
        )
        sent = jnp.concatenate([mod_sum, bias_all], axis=1)
        got_all = across(jnp.repeat(sent, cuts, axis=0), LAYER)
        ready = run(
            mods_kernel,
            Named(
                mods=shaped((12, width), F32),
                biases=[shaped((4, width), F32)] * 2,
                inner=[shaped((2, part), F32)] * 2,
            ),
            spot,
            got_all,
        )
        mods, biases, in_biases = ready.mods, ready.biases, ready.inner
    else:
        mod_sum = lax.psum_scatter(mod_terms, SLOTS, scatter_dimension=0, tiled=False)
        bias_all = lax.all_gather(bias_own, SLOTS, axis=0)
        mod_got, bias_got = swap(pick(mod_sum[6:], mod_sum[:6])), swap(bias_all)
        mod_kept = pick(mod_sum[:6], mod_sum[6:])
        mod_both = jnp.concatenate([pick(mod_kept, mod_got), pick(mod_got, mod_kept)], axis=0)
        mod_list = gather_list(mod_both, TENSOR)
        mods = jnp.moveaxis(place(mod_list, TENSOR), 0, 1).reshape(12, width)
        in_biases, biases = [], []
        for member in (pick(bias_all, bias_got), pick(bias_got, bias_all)):
            cols = project_in_bias.shape[2]
            columns = member[:, 0, : 2 * cols].reshape(shards, 2, cols)
            in_biases.append(jnp.moveaxis(columns, 0, 1).reshape(2, part))
            biases.append(jnp.moveaxis(member, 0, 1).reshape(4, width))
    if near:
        first_stack = jnp.stack(first_pieces)
        first_a = (first_stack, swap(first_stack))
    first_u, first_d, second_a = gather_blocks([(1, 0), (2, 0), (0, 1)], (got, *first_pieces[1:]) if near else ())
    weights = [(first_a, first_u, first_d), None]

    def terms_out(count=1):
        return [shaped((own_tokens, width), F32)] + [
            shaped((own_tokens, width), BF16) for k in range(1, cuts)
        ]

    own_f32 = shaped((own_tokens, width), F32)
    both_f32 = shaped((2 * own_tokens, width), F32)
    own_b16 = shaped((own_tokens, width), BF16)
    attend_flops = 2 * tokens * width * width + 4 * tokens * tokens * part
    mlp_flops = 4 * tokens * width * hidden_part

    kept, packs = [], []
    inputs = tokens_own
    first = token_list
    for layer in range(2):
        packed, upper, lower = weights[layer]
        outs = Named(kept=shaped((tokens, (3 - layer) * width), BF16), terms=terms_out())
        if isinstance(packed, tuple):
            outs.packed = shaped((width, width), BF16)
        attn = run(
            attend_kernel(layer),
            outs,
            spot,
            first,
            mods,
            packed,
            in_biases[layer],
            flops=attend_flops,
        )
        packs.append(attn.packed if isinstance(packed, tuple) else packed)
        terms = exchange_list(attn.terms, TENSOR)
        if layer == 0:
            second_u, second_d = gather_blocks([(1, 1), (2, 1)], tuple(terms[1:]))
            weights[1] = (second_a, second_u, second_d)
        middle = run(
            middle_kernel(layer),
            Named(kept=both_f32, mlp_in=own_b16),
            terms,
            inputs,
            mods,
            biases[layer],
        )
        mlp = run(
            mlp_kernel,
            Named(kept=shaped((tokens, width + 2 * hidden_part), BF16), terms=terms_out()),
            gather_list(middle.mlp_in, TENSOR),
            upper,
            lower,
            biases[layer],
            flops=mlp_flops,
        )
        outs = Named(mlp_out=own_f32, output=own_b16)
        if layer == 0:
            outs.attn_in = own_b16
        last = run(
            last_kernel(layer),
            outs,
            exchange_list(mlp.terms, TENSOR),
            middle.kept,
            mods,
            biases[layer],
        )
        kept.append((inputs, attn, middle, mlp, last))
        inputs = last.output
        if layer == 0:
            first = gather_list(last.attn_in, TENSOR)
            seed_list = gather_list(seed_own, TENSOR)

    row = shaped((1, width), F32)
    grad_own, pieces = seed_own, seed_list
    mod_rows, bias_rows, blocks, input_grads = [None] * 2, [None] * 2, [None] * 2, [None] * 2
    for layer in (1, 0):
        packed, upper, lower = packs[layer], weights[layer][1], weights[layer][2]
        inputs, attn, middle, mlp, last = kept[layer]
        mlp_back = run(
            mlp_back_kernel(layer),
            Named(
                grads=shaped((tokens, width + hidden_part), BF16),
                terms=terms_out(),
                bias=shaped((2, hidden_part), F32),
            ),
            pieces,
            mods,
            upper,
            lower,
            mlp.kept,
            flops=mlp_flops,
        )
        middle_back = run(
            middle_back_kernel(layer),
            Named(
                middle_grad=own_f32,
                outer=own_b16,
                rows=shaped((4, width), F32),
            ),
            exchange_list(mlp_back.terms, TENSOR),
            grad_own,
            middle.kept,
            last.mlp_out,
            mods,
        )
        outs = Named(
            grads=shaped((tokens, width + 3 * part), BF16),
            terms=terms_out(),
            out_bias=row,
            in_bias=shaped((1, 3 * part), F32),
        )
        others = None
        if layer == 0 and near:
            outs.sent = shaped((2 * cuts, 6 + 4 * shards, part), F32)
            outs.terms = shaped((tokens, width), F32)
            others = (middle_back.rows, mlp_back.bias, mod_rows[1], bias_rows[1])
        elif layer == 0:
            outs.rows = shaped((2, width), F32)
        attn_back = run(
            attend_back_kernel(layer),
            outs,
            gather_list(middle_back.outer, TENSOR),
            packed,
            attn.kept,
            others,
            flops=2 * attend_flops,
        )
        grads = run(
            grads_kernel,
            Named(grads=shaped((2 * shards, 3, rows, width // 2), BF16)),
            mlp.kept,
            mlp_back.grads,
            attn.kept,
            attn_back.grads,
            flops=mlp_flops + 2 * tokens * width * width,
        ).grads
        blocks[layer] = lax.psum_scatter(grads, ROWS, scatter_dimension=0, tiled=False)
        terms = attn_back.terms
        if layer == 0 and near:
            sent = run(
                slots_kernel,
                Named(sent=[shaped((16, part), F32)] * shards),
                spot,
                across(attn_back.sent, LAYER),
            ).sent
            got = exchange_list(sent, SLOTS)
            terms = run(
                split_kernel, Named(terms=terms_out()), terms, wait=(*got[1:], blocks[1])
            ).terms
        outs = Named(input_grad=own_f32)
        if layer == 1:
            outs.rows, outs.grad, outs.lower = shaped((2, width), F32), own_b16, own_b16
        first_back = run(
            first_back_kernel(layer),
            outs,
            exchange_list(terms, TENSOR),
            middle_back.middle_grad,
            inputs,
            mods,
        )
        input_grads[layer] = first_back.input_grad
        if layer == 1 or not near:
            mod_rows[layer] = [
                attn_back.rows if layer == 0 else first_back.rows,
                middle_back.rows,
            ]
        bias_rows[layer] = (attn_back.in_bias, attn_back.out_bias, mlp_back.bias)

        if layer == 1:
            grad_own = first_back.grad
            pieces = gather_list(first_back.lower, TENSOR)

    given = swap(pick(blocks[1], blocks[0]))
    if near:
        ready = run(
            assemble_kernel,
            Named(
                upper=shaped((rows, hidden_part), F32),
                lower=shaped((rows, hidden_part), F32),
                inner=shaped((3, rows, part), F32),
                outer=shaped((part, rows), F32),
            ),
            spot,
            blocks[0],
            blocks[1],
            given,
        )
        grad_upper, grad_lower, grad_outer = ready.upper, ready.lower.T, ready.outer
        grad_inner = jnp.moveaxis(ready.inner, 0, 1)
    else:
        own = pick(blocks[0], blocks[1])
        grads = jnp.concatenate([pick(own, given), pick(given, own)], axis=2).astype(F32)
        grad_upper, grad_lower = grads[0], grads[1].T
        grad_inner = grads[2, :, : 3 * part].reshape(rows, 3, part)
        grad_outer = grads[2, :, 3 * part :].T

    if near:
        mod_slots = place([member[:12] for member in got], SLOTS)
        bias_total = sum(member[12:] for member in got)
    else:
        tail = run(
            pack_kernel,
            Named(
                mods=[shaped((12, part), F32) for k in range(cuts)],
                kept=shaped((shards, 4, rows), F32),
                given=shaped((shards, 4, rows), F32),
            ),
            spot,
            mod_rows[0],
            mod_rows[1],
            bias_rows[0],
            bias_rows[1],
        )
        mod_shard = sum(exchange_list(tail.mods, TENSOR))
        mod_given, mod_kept = pick(mod_shard[6:], mod_shard[:6]), pick(mod_shard[:6], mod_shard[6:])
        mod_got, bias_got = swap(mod_given), swap(tail.given)
        mod_micro = jnp.concatenate([pick(mod_kept, mod_got), pick(mod_got, mod_kept)], axis=0)
        bias_sum = tail.kept + bias_got
        mod_slots = lax.all_gather(mod_micro, SLOTS, axis=0, tiled=True)
        bias_total = lax.psum_scatter(bias_sum, SLOTS, scatter_dimension=0, tiled=False)
    mod_slots = mod_slots.reshape(shards * micro_count, 6 * part)
    act_grad = lax.dot_general(
        mod_slots, mod_weight.astype(F32), (((1,), (1,)), ((), ())), precision=HIGH
    )
    mod_slots = mod_slots + jnp.minimum(jnp.abs(act_grad[:1, :1]), 0.0)
    if near:
        spread = jnp.broadcast_to(act_grad, (2 * cuts, *act_grad.shape))
        act_grad = jnp.sum(across(spread, LAYER), axis=0)
        act_all = place(gather_list(act_grad, SLOTS), SLOTS)
    else:
        act_grad = act_grad + swap(act_grad)
        act_grad = sum(gather_list(act_grad, TENSOR))
        act_all = lax.all_gather(act_grad, SLOTS, axis=0)
    act_all = jnp.moveaxis(act_all, 0, 1).reshape(-1, width)
    cond_grad = jax.vjp(jax.nn.silu, condition)[1](act_all)[0]
    pieces = []
    rest = cond_grad
    for _ in range(3):
        pieces.append(rest.astype(BF16))
        rest = rest - pieces[-1].astype(F32)
    pieces = jnp.concatenate(pieces, axis=0)
    table_grad = dot(jnp.concatenate([class_hot.astype(BF16)] * 3, axis=0), pieces, 0, 0)
    time_grad = dot(jnp.concatenate([time_feats] * 3, axis=0), pieces, 0, 0)
    grad_mod_weight = lax.dot_general(
        act_rows.astype(F32), mod_slots, (((0,), (0,)), ((), ())), precision=HIGH
    ).reshape(rows, 6, part)
    mod_bias_sum = jnp.sum(mod_slots, axis=0).reshape(6, part)
    grad_mod_bias = lax.dynamic_slice_in_dim(mod_bias_sum, shard * bias_cols, bias_cols, 1)
    grad_in_bias = bias_total[0, : in_bias_own.shape[1]].reshape(2, -1)

    def by_micro(first, second):
        got = swap(pick(second, first))
        held = pick(first, second)
        return jnp.stack([pick(held, got), pick(got, held)])[None, :, None]

    return (
        by_micro(kept[0][4].output, kept[1][4].output),
        by_micro(input_grads[0], input_grads[1]),
        table_grad,
        time_grad,
        grad_inner[None],
        grad_in_bias[None],
        grad_outer[None],
        bias_total[2][None],
        grad_upper[None],
        bias_total[1][None],
        grad_lower[None],
        bias_total[3][None],
        grad_mod_weight[None],
        grad_mod_bias[None],
    )


def solution(mesh):
    in_specs = (
        P(None, SLOTS, TENSOR, None),
        P(None, SLOTS, TENSOR, None),
        P(None, SLOTS),
        P(None, SLOTS),
        P(None, SLOTS),
        P(),
        P(),
        P(SECTION, SLOTS, None, TENSOR),
        P(SECTION, None, (TENSOR, SLOTS)),
        P(SECTION, TENSOR, SLOTS),
        P(SECTION, SLOTS),
        P(SECTION, SLOTS, TENSOR),
        P(SECTION, (TENSOR, SLOTS)),
        P(SECTION, TENSOR, SLOTS),
        P(SECTION, SLOTS),
        P(SECTION, SLOTS, None, TENSOR),
        P(SECTION, None, (TENSOR, SLOTS)),
    )
    out_specs = (
        P(SECTION, None, SLOTS, TENSOR, None),
        P(SECTION, None, SLOTS, TENSOR, None),
        P(),
        P(),
        P(SECTION, SLOTS, None, TENSOR),
        P(SECTION, None, (TENSOR, SLOTS)),
        P(SECTION, TENSOR, SLOTS),
        P(SECTION, SLOTS),
        P(SECTION, SLOTS, TENSOR),
        P(SECTION, (TENSOR, SLOTS)),
        P(SECTION, TENSOR, SLOTS),
        P(SECTION, SLOTS),
        P(SECTION, SLOTS, None, TENSOR),
        P(SECTION, None, (TENSOR, SLOTS)),
    )
    return jax.shard_map(body, mesh=mesh, in_specs=in_specs, out_specs=out_specs, check_vma=False)
```

```python
import math
from types import SimpleNamespace as Named

import jax
import jax.numpy as jnp
from jax import lax
from jax.experimental import pallas as pl
from jax.experimental.pallas import tpu as pltpu
from jax.sharding import PartitionSpec as P

HD = 64
EPS = 1e-06
HIGH = lax.Precision.HIGHEST
F32 = jnp.float32
BF16 = jnp.bfloat16
SECTION, TENSOR, SLOTS = "section", "tensor", "dp"
LAYER = (SECTION, TENSOR)
ROWS = (SLOTS, SECTION)
SPACE = 40 * 1024 * 1024


def cyclic(axis):
    size = lax.axis_size(axis)
    return size & (size - 1) != 0


def exchange(value, axis, k):
    size = lax.axis_size(axis)
    if cyclic(axis):
        return lax.ppermute(value, axis, [(i, (i - k) % size) for i in range(size)])
    return lax.ppermute(value, axis, [(i, i ^ k) for i in range(size)])


def fetch(value, axis, k):
    size = lax.axis_size(axis)
    if cyclic(axis):
        return lax.ppermute(value, axis, [(i, (i + k) % size) for i in range(size)])
    return lax.ppermute(value, axis, [(i, i ^ k) for i in range(size)])


def partner(axis, k):
    here = lax.axis_index(axis)
    if cyclic(axis):
        return (here - k) % lax.axis_size(axis)
    return here ^ k


def swap(value):
    return lax.ppermute(value, SECTION, [(0, 1), (1, 0)])


def across(value, axis):
    return lax.all_to_all(value, axis, 0, 0)


def gather_list(value, axis):
    got = {k: fetch(value, axis, k) for k in reversed(range(1, lax.axis_size(axis)))}
    return [value] + [got[k] for k in range(1, lax.axis_size(axis))]


def exchange_list(values, axis):
    got = {k: exchange(values[k], axis, k) for k in reversed(range(1, lax.axis_size(axis)))}
    return [values[0]] + [got[k] for k in range(1, lax.axis_size(axis))]


def place(pieces, axis):
    out = jnp.zeros((len(pieces),) + pieces[0].shape, pieces[0].dtype)
    for k, piece in enumerate(pieces):
        out = lax.dynamic_update_index_in_dim(out, piece, partner(axis, k), 0)
    return out


def shaped(shape, dtype):
    return jax.ShapeDtypeStruct(shape, dtype)


class Part:
    def __init__(self, value, at=None):
        self.value, self.at = value, at
        self.shape, self.dtype = value.shape, value.dtype


def run(kernel, outs, *args, flops=0, wait=()):
    def leafy(value):
        return isinstance(value, Part)

    names = list(vars(outs))
    out_flat, out_tree = jax.tree.flatten([vars(outs)[name] for name in names])
    flat, tree = jax.tree.flatten(args, is_leaf=leafy)
    moved = sum(math.prod(leaf.shape) * leaf.dtype.itemsize for leaf in flat + out_flat)

    def inner(*refs):
        ins = list(refs[: len(flat)])
        for k, leaf in enumerate(flat):
            if leafy(leaf) and leaf.at is not None:
                ins[k] = Named(ref=ins[k], at=leaf.at)
        results = jax.tree.unflatten(out_tree, refs[len(flat) + len(wait) :])
        kernel(*jax.tree.unflatten(tree, ins), Named(**dict(zip(names, results))))

    result = pl.pallas_call(
        inner,
        out_shape=out_flat,
        in_specs=[
            pl.BlockSpec(memory_space=pltpu.SMEM if leaf.dtype == jnp.int32 else pltpu.VMEM)
            for leaf in flat
        ]
        + [pl.BlockSpec(memory_space=pl.ANY)] * len(wait),
        out_specs=[pl.BlockSpec(memory_space=pltpu.VMEM)] * len(out_flat),
        compiler_params=pltpu.CompilerParams(vmem_limit_bytes=SPACE),
        cost_estimate=pl.CostEstimate(flops=flops, bytes_accessed=moved, transcendentals=0),
    )(*[leaf.value if leafy(leaf) else leaf for leaf in flat], *wait)
    return Named(**dict(zip(names, jax.tree.unflatten(out_tree, result))))


def matrix(ref):
    if isinstance(ref, Named):
        value = ref.ref[:, ref.at]
        return value.reshape(-1, value.shape[-1])
    return ref[...]


def norm_parts(values):
    average = jnp.mean(values, axis=-1, keepdims=True)
    centred = values - average
    spread = jnp.mean(centred * centred, axis=-1, keepdims=True)
    scale = lax.rsqrt(spread + EPS)
    return centred * scale, scale


def norm_pull(grad, normed, scale):
    first = jnp.mean(grad, axis=-1, keepdims=True)
    second = jnp.mean(grad * normed, axis=-1, keepdims=True)
    return scale * (grad - first - normed * second)


def dot(left, right, left_dim, right_dim):
    return lax.dot_general(
        left, right, (((left_dim,), (right_dim,)), ((), ())), preferred_element_type=F32
    )


def joined(refs):
    return jnp.concatenate([ref[...] for ref in refs], axis=0)


def summed(refs):
    total = refs[0][...].astype(F32)
    for ref in refs[1:]:
        total = total + ref[...].astype(F32)
    return total


def spread_out(terms, refs):
    rows = refs[0].shape[0]
    for k, ref in enumerate(refs):
        ref[...] = terms[k * rows : (k + 1) * rows].astype(ref.dtype)


def column_sum(values):
    return jnp.sum(values.astype(F32), axis=0, keepdims=True)


def softmax_parts(query, key):
    scores = dot(query, key, 1, 1) * HD**-0.5
    raised = jnp.exp(scores - jnp.max(scores, axis=-1, keepdims=True))
    return raised / jnp.sum(raised, axis=-1, keepdims=True)


def assemble(spot, pieces, ref):
    own, other = pieces
    rows = own.shape[1]
    for k in range(own.shape[0]):
        for half, block in ((spot[0], own[k]), (1 - spot[0], other[k])):
            at = pl.multiple_of((2 * spot[3 + k] + half) * rows, rows)
            ref[pl.ds(at, rows), :] = block


def attend(first, mods, packed, in_bias, refs, layer):
    width = packed.shape[1] // 4
    attn_in = joined(first)
    if layer == 0:
        refs.kept[:, 2 * packed.shape[1] :] = attn_in
        normed = norm_parts(attn_in.astype(F32))[0]
        attn_in = (normed * (1.0 + mods[1:2]) + mods[0:1]).astype(BF16)
    refs.kept[:, : packed.shape[1]] = attn_in
    projected = dot(attn_in, packed[:, : 3 * width], 1, 0)
    queries = (projected[:, :width] + in_bias[0:1]).astype(BF16)
    keys = projected[:, width : 2 * width].astype(BF16)
    values = (projected[:, 2 * width :] + in_bias[1:2]).astype(BF16)
    mixed = []
    for at in range(0, width, HD):
        attention = softmax_parts(queries[:, at : at + HD], keys[:, at : at + HD])
        mixed.append(dot(attention.astype(BF16), values[:, at : at + HD], 1, 0))
    mixed = jnp.concatenate(mixed, axis=1).astype(BF16)
    refs.kept[:, packed.shape[1] : 2 * packed.shape[1]] = jnp.concatenate(
        [queries, keys, values, mixed], axis=1
    )
    spread_out(dot(mixed, packed[:, 3 * width :], 1, 1), refs.terms)


def attend_kernel(layer):
    def kernel(spot, first, mods_ref, packed_ref, bias_ref, refs):
        if isinstance(packed_ref, tuple):
            assemble(spot, packed_ref, refs.packed)
            packed_ref = refs.packed
        attend(first, mods_ref[6 * layer : 6 * layer + 6], matrix(packed_ref), bias_ref[...], refs, layer)

    return kernel


def middle_kernel(layer):
    def kernel(terms, inputs, mods_ref, bias_ref, refs):
        mods = mods_ref[6 * layer : 6 * layer + 6]
        attn_out = summed(terms) + bias_ref[2:3]
        rows = attn_out.shape[0]
        refs.kept[:rows] = attn_out
        middle = inputs[...].astype(F32) + mods[2:3] * attn_out
        refs.kept[rows:] = middle
        normed = norm_parts(middle)[0]
        refs.mlp_in[...] = (normed * (1.0 + mods[4:5]) + mods[3:4]).astype(BF16)

    return kernel


def mlp_kernel(pieces, upper, lower, bias_ref, refs):
    mlp_in = joined(pieces)
    size = upper.ref.shape[-1] if isinstance(upper, Named) else upper.shape[-1]
    wide = mlp_in.shape[1]
    refs.kept[:, :wide] = mlp_in
    values = dot(mlp_in, matrix(upper), 1, 0) + bias_ref[1:2]
    root = math.sqrt(2.0 / math.pi)
    square = values * values
    bent = jnp.tanh(root * (values + 0.044715 * values * square))
    hidden = (0.5 * values * (1.0 + bent)).astype(BF16)
    refs.kept[:, wide : wide + size] = hidden
    slope = 0.5 * (1.0 + bent) + 0.5 * values * (1.0 - bent * bent) * root * (
        1.0 + 0.134145 * square
    )
    refs.kept[:, wide + size :] = slope.astype(BF16)
    spread_out(dot(hidden, matrix(lower), 1, 1), refs.terms)


def last_kernel(layer):
    def kernel(terms, kept, mods_ref, bias_ref, refs):
        mlp_out = summed(terms) + bias_ref[3:4]
        refs.mlp_out[...] = mlp_out
        output = (kept[kept.shape[0] // 2 :] + mods_ref[6 * layer + 5 : 6 * layer + 6] * mlp_out).astype(BF16)
        refs.output[...] = output
        if layer == 0:
            normed = norm_parts(output.astype(F32))[0]
            refs.attn_in[...] = (normed * (1.0 + mods_ref[7:8]) + mods_ref[6:7]).astype(BF16)

    return kernel


def mlp_back_kernel(layer):
    def kernel(pieces, mods_ref, upper, lower, kept, refs):
        lower_grad = joined(pieces)
        if layer == 1:
            lower_grad = (lower_grad.astype(F32) * mods_ref[11:12]).astype(BF16)
        wide = lower_grad.shape[1]
        refs.grads[:, :wide] = lower_grad
        pre_grad = dot(lower_grad, matrix(lower), 1, 0)
        slope = kept[:, wide + pre_grad.shape[1] :].astype(F32)
        pre_grad = (pre_grad * slope).astype(BF16)
        refs.grads[:, wide:] = pre_grad
        spread_out(dot(pre_grad, matrix(upper), 1, 1), refs.terms)
        refs.bias[0:1] = column_sum(pre_grad)
        refs.bias[1:2] = column_sum(lower_grad)

    return kernel


def middle_back_kernel(layer):
    def kernel(terms, grad_ref, kept, mlp_out, mods_ref, refs):
        mods = mods_ref[6 * layer : 6 * layer + 6]
        grad = grad_ref[...].astype(F32)
        mid_grad = summed(terms)
        normed, scale = norm_parts(kept[kept.shape[0] // 2 :])
        middle_grad = grad + norm_pull(mid_grad * (1.0 + mods[4:5]), normed, scale)
        refs.middle_grad[...] = middle_grad
        refs.outer[...] = (middle_grad * mods[2:3]).astype(BF16)
        refs.rows[0:1] = column_sum(middle_grad * kept[: kept.shape[0] // 2])
        refs.rows[1:2] = column_sum(mid_grad)
        refs.rows[2:3] = column_sum(mid_grad * normed)
        refs.rows[3:4] = column_sum(grad * mlp_out[...])

    return kernel


def attend_back_kernel(layer):
    def kernel(pieces, packed, kept, others, refs):
        outer_grad = joined(pieces)
        wide = outer_grad.shape[1]
        refs.grads[:, :wide] = outer_grad
        packed = matrix(packed)
        width = packed.shape[1] // 4
        mixed_grad = dot(outer_grad, packed[:, 3 * width :], 1, 0).astype(BF16)
        queries, keys, values = [
            kept[:, wide + k * width : wide + (k + 1) * width] for k in range(3)
        ]
        d_queries, d_keys, d_values = [], [], []
        for at in range(0, width, HD):
            query, key = queries[:, at : at + HD], keys[:, at : at + HD]
            grad = mixed_grad[:, at : at + HD]
            attention = softmax_parts(query, key)
            weight_grad = dot(grad, values[:, at : at + HD], 1, 1)
            d_values.append(dot(attention.astype(BF16), grad, 0, 0))
            row_dot = jnp.sum(attention * weight_grad, axis=-1, keepdims=True)
            score_grad = (attention * (weight_grad - row_dot)).astype(BF16)
            d_queries.append(dot(score_grad, key, 1, 0) * HD**-0.5)
            d_keys.append(dot(score_grad, query, 0, 0) * HD**-0.5)
        stacked = jnp.concatenate(d_queries + d_keys + d_values, axis=1).astype(BF16)
        refs.grads[:, wide:] = stacked
        terms = dot(stacked, packed[:, : 3 * width], 1, 1)
        if others is None:
            spread_out(terms, refs.terms)
        else:
            refs.terms[...] = terms
        in_bias, out_bias = column_sum(stacked), column_sum(outer_grad)
        refs.out_bias[...] = out_bias
        refs.in_bias[...] = in_bias
        if layer == 0:
            normed = norm_parts(kept[:, 2 * wide :].astype(F32))[0]
            rows = jnp.concatenate([column_sum(terms), column_sum(terms * normed)], axis=0)
            if others is None:
                refs.rows[...] = rows
            else:
                middle_rows, mlp_bias, other_rows, other_bias = others
                mods = [
                    jnp.concatenate([rows, middle_rows[...]], axis=0),
                    jnp.concatenate([ref[...] for ref in other_rows], axis=0),
                ]
                send_rows(mods, [(in_bias, out_bias, mlp_bias), other_bias], refs.sent)

    return kernel


def first_back_kernel(layer):
    def kernel(terms, middle_grad, inputs, mods_ref, refs):
        in_grad = summed(terms)
        normed, scale = norm_parts(inputs[...].astype(F32))
        scale_one = mods_ref[6 * layer + 1 : 6 * layer + 2]
        input_grad = middle_grad[...] + norm_pull(in_grad * (1.0 + scale_one), normed, scale)
        refs.input_grad[...] = input_grad
        if layer == 1:
            refs.rows[0:1] = column_sum(in_grad)
            refs.rows[1:2] = column_sum(in_grad * normed)
            rounded = input_grad.astype(BF16)
            refs.grad[...] = rounded
            refs.lower[...] = (rounded.astype(F32) * mods_ref[5:6]).astype(BF16)

    return kernel


def cut(grad, ref, at):
    count, rows, half = ref.shape[0], ref.shape[2], ref.shape[3]
    for block in range(count):
        place_at = block // 2 * rows
        ref[block, at] = grad[
            place_at : place_at + rows, block % 2 * half : block % 2 * half + half
        ].astype(BF16)


def grads_kernel(mlp_kept, mlp_grads, attn_kept, attn_grads, refs):
    wide = 2 * refs.grads.shape[3]
    size, width = mlp_grads.shape[1] - wide, wide // 4
    cut(dot(mlp_kept[:, :wide], mlp_grads[:, wide:], 0, 0), refs.grads, 0)
    cut(dot(mlp_grads[:, :wide], mlp_kept[:, wide : wide + size], 0, 0), refs.grads, 1)
    inner = dot(attn_kept[:, :wide], attn_grads[:, wide:], 0, 0)
    outer = dot(attn_grads[:, :wide], attn_kept[:, wide + 3 * width : 2 * wide], 0, 0)
    cut(jnp.concatenate([inner, outer], axis=1), refs.grads, 2)


def mods_kernel(spot, got, refs):
    cuts = got.shape[0] // 2
    count = (got.shape[1] - 6) // 4
    cols = refs.inner[0].shape[1] // count
    for layer in range(2):
        refs.mods[6 * layer : 6 * layer + 6] = jnp.concatenate(
            [got[cuts * layer + t, :6] for t in range(cuts)], axis=1
        )
        rows = got[cuts * layer + spot[1], 6:]
        pieces = [rows[4 * k : 4 * k + 4] for k in range(count)]
        refs.biases[layer][...] = jnp.concatenate(pieces, axis=1)
        for k in range(2):
            refs.inner[layer][k : k + 1] = jnp.concatenate(
                [piece[0:1, k * cols : (k + 1) * cols] for piece in pieces], axis=1
            )


def bias_rows_of(part, rows, shards, in_bias, out_bias, mlp_bias):
    cols = part // shards
    pieces = []
    for z in range(shards):
        start = jnp.concatenate(
            [
                in_bias[:, z * cols : (z + 1) * cols],
                in_bias[:, 2 * part + z * cols : 2 * part + (z + 1) * cols],
                jnp.zeros((1, rows - 2 * cols), F32),
            ],
            axis=1,
        )
        at = slice(z * rows, (z + 1) * rows)
        pieces += [start, mlp_bias[0:1, at], out_bias[:, at], mlp_bias[1:2, at]]
    return jnp.concatenate(pieces, axis=0)


def send_rows(mods, biases, sent):
    cuts, part = sent.shape[0] // 2, sent.shape[2]
    shards = (sent.shape[1] - 6) // 4
    for layer in range(2):
        rows = bias_rows_of(part, part, shards, *biases[layer])
        for t in range(cuts):
            sent[cuts * layer + t, :6] = mods[layer][:, t * part : (t + 1) * part]
            sent[cuts * layer + t, 6:] = rows


def pack_kernel(spot, mod_one, mod_two, bias_one, bias_two, refs):
    core, here, cycle = spot[0], spot[1], spot[2]
    mods = jnp.concatenate([ref[...] for ref in mod_one + mod_two], axis=0)
    cuts = len(refs.mods)
    part = mods.shape[1] // cuts
    blocks = [mods[:, j * part : (j + 1) * part] for j in range(cuts)]
    for k, ref in enumerate(refs.mods):
        index = jnp.where(cycle == 1, (here - k + cuts) % cuts, here ^ k)
        chosen = blocks[0]
        for j in range(1, cuts):
            chosen = jnp.where(index == j, blocks[j], chosen)
        ref[...] = chosen
    shards, _, rows = refs.kept.shape
    first = bias_rows_of(part, rows, shards, *bias_one)
    second = bias_rows_of(part, rows, shards, *bias_two)
    for z in range(shards):
        at = slice(4 * z, 4 * z + 4)
        refs.kept[z] = jnp.where(core == 0, first[at], second[at])
        refs.given[z] = jnp.where(core == 0, second[at], first[at])


def bundle_kernel(members):
    def kernel(spot, kept, got, refs):
        for k, (weight, layer) in enumerate(members):
            refs.rows[k] = jnp.where(spot[0] == layer, kept[weight], got[weight])

    return kernel


def slots_kernel(spot, received, refs):
    cuts = received.shape[0] // 2
    shards = (received.shape[1] - 6) // 4
    mods = []
    for micro in range(2):
        total = received[cuts * micro, :6]
        for t in range(1, cuts):
            total = total + received[cuts * micro + t, :6]
        mods.append(total)
    here = spot[1]
    biases = received[here, 6:] + received[cuts + here, 6:]
    for k, ref in enumerate(refs.sent):
        ref[:6], ref[6:12] = mods
        total = biases[:4]
        for z in range(1, shards):
            total = jnp.where(spot[3 + k] == z, biases[4 * z : 4 * z + 4], total)
        ref[12:16] = total


def modulate_kernel(act, weights, mod_bias, own, refs):
    shards, _, part = refs.sent.shape
    micro = act.shape[0] // shards
    for k in range(6):
        terms = dot(act[...], weights[k], 1, 0) + mod_bias[k : k + 1]
        for z in range(shards):
            for m in range(micro):
                at = z * micro + m
                refs.sent[z, 6 * m + k : 6 * m + k + 1] = terms[at : at + 1]
    for z in range(shards):
        refs.sent[z, 6 * micro :] = own[...]


def act_kernel(spot, pieces, weights, refs):
    shards = len(pieces)
    blocks = []
    for z in range(shards):
        chosen = pieces[0][...]
        for k in range(1, shards):
            chosen = jnp.where(spot[3 + k] == z, pieces[k][...], chosen)
        blocks.append(chosen)
    total = jnp.zeros(refs.sent.shape[1:], F32)
    for k in range(6):
        rest = jnp.concatenate([b[at : at + 1] for b in blocks for at in (k, 6 + k)], axis=0)
        for _ in range(3):
            rounded = rest.astype(BF16)
            total = total + dot(rounded, weights[k], 1, 1)
            rest = rest - rounded.astype(F32)
    repeat_rows(total, refs.sent)


def repeat_rows(values, ref):
    for k in range(ref.shape[0]):
        ref[k] = values


def assemble_kernel(spot, first, second, given, refs):
    wide = []
    for k in range(3):
        own = jnp.where(spot[0] == 0, first[k], second[k]).astype(F32)
        other = given[k].astype(F32)
        left, right = jnp.where(spot[0] == 0, own, other), jnp.where(spot[0] == 0, other, own)
        wide.append(jnp.concatenate([left, right], axis=1))
    refs.upper[...], refs.lower[...] = wide[0], wide[1]
    width = wide[2].shape[1] // 4
    for k in range(3):
        refs.inner[k] = wide[2][:, k * width : (k + 1) * width]
    refs.outer[...] = wide[2][:, 3 * width :].T


def split_kernel(terms, refs):
    spread_out(terms[...], refs.terms)


def prepare_kernel(spot, inner, outer, upper, lower, refs):
    half = upper.shape[0] // 2
    packed = jnp.concatenate([inner[0], inner[1], inner[2], outer[...].T], axis=1)
    for k, member in enumerate((packed, upper[...], lower[...])):
        first, second = member[:half], member[half:]
        refs.kept[k] = jnp.where(spot[0] == 0, first, second)
        refs.given[k] = jnp.where(spot[0] == 0, second, first)


def sinus_features(stamps, columns):
    halfway = columns // 2
    frequency = jnp.exp(-math.log(10000.0) * jnp.arange(halfway, dtype=F32) / halfway)
    angles = stamps.astype(F32)[:, None] * frequency[None, :]
    return jnp.concatenate([jnp.cos(angles), jnp.sin(angles)], axis=-1)


def body(
    latents,
    cotangent,
    labels,
    timesteps,
    occupied,
    class_table,
    time_weight,
    project_in,
    project_in_bias,
    project_out,
    project_out_bias,
    up_weight,
    up_bias,
    down_weight,
    down_bias,
    modulate_weight,
    modulate_bias,
):
    core = lax.axis_index(SECTION)
    shard = lax.axis_index(SLOTS)
    shards = lax.axis_size(SLOTS)
    cuts = lax.axis_size(TENSOR)
    micro_count = latents.shape[0]
    width = latents.shape[3]
    own_tokens = latents.shape[2]
    tokens = own_tokens * cuts
    part = width // cuts
    rows = width // shards
    hidden_part = up_weight.shape[2]
    near = shards <= 8 and not cyclic(SLOTS) and rows == part

    def pick(first, second):
        return jnp.where(core == 0, first, second)

    spot = jnp.stack(
        [core, lax.axis_index(TENSOR), jnp.int32(1 if cyclic(TENSOR) else 0)]
        + [partner(SLOTS, k) for k in range(shards if near else 0)]
        + [partner(TENSOR, k) for k in range(cuts)]
    ).astype(jnp.int32)

    half = rows // 2
    if near:
        inner = jnp.moveaxis(project_in[0], 1, 0)
        ready = run(
            prepare_kernel,
            Named(kept=shaped((3, half, width), BF16), given=shaped((3, half, width), BF16)),
            spot,
            inner,
            project_out[0],
            up_weight[0],
            down_weight[0].T,
        )
        given = swap(ready.given)
        kept_halves, got_halves = ready.kept, given
    else:
        packed_own = jnp.concatenate(
            [project_in[0, :, 0], project_in[0, :, 1], project_in[0, :, 2], project_out[0].T], axis=1
        )
        stack = [packed_own, up_weight[0], down_weight[0].T]
        given = swap(jnp.concatenate([pick(member[half:], member[:half]) for member in stack]))
        kept_halves = [pick(member[:half], member[half:]) for member in stack]
        got_halves = [given[k * half : (k + 1) * half] for k in range(3)]

    def bundle(members, wait):
        return run(
            bundle_kernel(members),
            Named(rows=shaped((len(members), half, width), BF16)),
            spot,
            kept_halves,
            got_halves,
            wait=wait,
        ).rows

    bundles = []

    def gather_blocks(members, wait=()):
        if near:
            own = bundle(members, wait)
            bundles.append(own)
            whole = lax.all_gather(own, ROWS, axis=0)
            return [Part(whole, k) for k in range(len(members))]
        return [
            gather_rows(
                pick(kept_halves[k], got_halves[k])
                if layer == 0
                else pick(got_halves[k], kept_halves[k])
            )
            for k, layer in members
        ]

    def gather_rows(value):
        return lax.all_gather(value, ROWS, axis=0, tiled=True)

    stamps = jnp.concatenate([labels.reshape(1, -1), timesteps.reshape(1, -1)], axis=1)
    if near:
        stamps = place(gather_list(stamps, SLOTS), SLOTS).reshape(shards, -1)
    else:
        stamps = lax.all_gather(stamps, SLOTS, axis=0, tiled=True)
    flat_labels = stamps[:, :micro_count].reshape(-1)
    flat_times = stamps[:, micro_count:].reshape(-1)
    class_count = class_table.shape[0]
    class_hot = flat_labels[:, None] == jnp.arange(class_count, dtype=jnp.int32)[None, :]
    time_feats = sinus_features(flat_times, time_weight.shape[0]).astype(BF16)
    condition = dot(class_hot.astype(BF16), class_table, 1, 0) + dot(time_feats, time_weight, 1, 0)
    cond_act = jax.nn.silu(condition).astype(BF16)
    act_rows = lax.dynamic_slice_in_dim(cond_act, shard * rows, rows, 1)

    if near:
        first_pieces = gather_list(pick(kept_halves[0], got_halves[0]), SLOTS)
    else:
        (first_a,) = gather_blocks([(0, 0)])

    tokens_own = pick(latents[0, 0], latents[1, 0])
    seed_own = pick(
        cotangent[0, 0] * occupied[0, 0].astype(BF16), cotangent[1, 0] * occupied[1, 0].astype(BF16)
    )
    token_list = gather_list(tokens_own, TENSOR)

    mod_weight = modulate_weight[0].reshape(rows, -1)
    bias_cols = modulate_bias.shape[2]
    bias_full = lax.dynamic_update_slice_in_dim(
        jnp.zeros((6, part), F32), modulate_bias[0].astype(F32), shard * bias_cols, 1
    )
    mod_terms = dot(act_rows, mod_weight, 1, 0) + bias_full.reshape(1, -1)
    mod_terms = mod_terms.reshape(shards, micro_count * 6, part)
    in_bias_own = project_in_bias.astype(F32).reshape(1, -1)
    bias_own = jnp.concatenate(
        [
            jnp.pad(in_bias_own, ((0, 0), (0, rows - in_bias_own.shape[1]))),
            up_bias.astype(F32),
            project_out_bias.astype(F32),
            down_bias.astype(F32),
        ],
        axis=0,
    )
    if near:
        sent = run(
            modulate_kernel,
            Named(sent=shaped((shards, 6 * micro_count + 4, part), F32)),
            act_rows,
            jnp.moveaxis(modulate_weight[0], 1, 0),
            bias_full,
            bias_own,
        ).sent
        got = across(sent, SLOTS)
        mod_sum = jnp.sum(got[:, : micro_count * 6], axis=0).reshape(micro_count, 6, part)
        bias_all = jnp.broadcast_to(
            got[:, micro_count * 6 :].reshape(1, 4 * shards, part), (micro_count, 4 * shards, part)
        )
        sent = jnp.concatenate([mod_sum, bias_all], axis=1)
        got_all = across(jnp.repeat(sent, cuts, axis=0), LAYER)
        ready = run(
            mods_kernel,
            Named(
                mods=shaped((12, width), F32),
                biases=[shaped((4, width), F32)] * 2,
                inner=[shaped((2, part), F32)] * 2,
            ),
            spot,
            got_all,
        )
        mods, biases, in_biases = ready.mods, ready.biases, ready.inner
    else:
        mod_sum = lax.psum_scatter(mod_terms, SLOTS, scatter_dimension=0, tiled=False)
        bias_all = lax.all_gather(bias_own, SLOTS, axis=0)
        mod_got, bias_got = swap(pick(mod_sum[6:], mod_sum[:6])), swap(bias_all)
        mod_kept = pick(mod_sum[:6], mod_sum[6:])
        mod_both = jnp.concatenate([pick(mod_kept, mod_got), pick(mod_got, mod_kept)], axis=0)
        mod_list = gather_list(mod_both, TENSOR)
        mods = jnp.moveaxis(place(mod_list, TENSOR), 0, 1).reshape(12, width)
        in_biases, biases = [], []
        for member in (pick(bias_all, bias_got), pick(bias_got, bias_all)):
            cols = project_in_bias.shape[2]
            columns = member[:, 0, : 2 * cols].reshape(shards, 2, cols)
            in_biases.append(jnp.moveaxis(columns, 0, 1).reshape(2, part))
            biases.append(jnp.moveaxis(member, 0, 1).reshape(4, width))
    if near:
        first_stack = jnp.stack(first_pieces)
        first_a = (first_stack, swap(first_stack))
    first_u, first_d, second_a = gather_blocks([(1, 0), (2, 0), (0, 1)], (got, *first_pieces[1:]) if near else ())
    second_u, second_d = gather_blocks([(1, 1), (2, 1)], tuple(bundles))
    weights = [(first_a, first_u, first_d), (second_a, second_u, second_d)]

    def terms_out(count=1):
        return [shaped((own_tokens, width), F32)] + [
            shaped((own_tokens, width), BF16) for k in range(1, cuts)
        ]

    own_f32 = shaped((own_tokens, width), F32)
    both_f32 = shaped((2 * own_tokens, width), F32)
    own_b16 = shaped((own_tokens, width), BF16)
    attend_flops = 2 * tokens * width * width + 4 * tokens * tokens * part
    mlp_flops = 4 * tokens * width * hidden_part

    kept, packs = [], []
    inputs = tokens_own
    first = token_list
    for layer in range(2):
        packed, upper, lower = weights[layer]
        outs = Named(kept=shaped((tokens, (3 - layer) * width), BF16), terms=terms_out())
        if isinstance(packed, tuple):
            outs.packed = shaped((width, width), BF16)
        attn = run(
            attend_kernel(layer),
            outs,
            spot,
            first,
            mods,
            packed,
            in_biases[layer],
            flops=attend_flops,
        )
        packs.append(attn.packed if isinstance(packed, tuple) else packed)
        terms = exchange_list(attn.terms, TENSOR)
        middle = run(
            middle_kernel(layer),
            Named(kept=both_f32, mlp_in=own_b16),
            terms,
            inputs,
            mods,
            biases[layer],
        )
        mlp = run(
            mlp_kernel,
            Named(kept=shaped((tokens, width + 2 * hidden_part), BF16), terms=terms_out()),
            gather_list(middle.mlp_in, TENSOR),
            upper,
            lower,
            biases[layer],
            flops=mlp_flops,
        )
        outs = Named(mlp_out=own_f32, output=own_b16)
        if layer == 0:
            outs.attn_in = own_b16
        last = run(
            last_kernel(layer),
            outs,
            exchange_list(mlp.terms, TENSOR),
            middle.kept,
            mods,
            biases[layer],
        )
        kept.append((inputs, attn, middle, mlp, last))
        inputs = last.output
        if layer == 0:
            first = gather_list(last.attn_in, TENSOR)
            seed_list = gather_list(seed_own, TENSOR)

    row = shaped((1, width), F32)
    grad_own, pieces = seed_own, seed_list
    mod_rows, bias_rows, blocks, input_grads = [None] * 2, [None] * 2, [None] * 2, [None] * 2
    for layer in (1, 0):
        packed, upper, lower = packs[layer], weights[layer][1], weights[layer][2]
        inputs, attn, middle, mlp, last = kept[layer]
        mlp_back = run(
            mlp_back_kernel(layer),
            Named(
                grads=shaped((tokens, width + hidden_part), BF16),
                terms=terms_out(),
                bias=shaped((2, hidden_part), F32),
            ),
            pieces,
            mods,
            upper,
            lower,
            mlp.kept,
            flops=mlp_flops,
        )
        middle_back = run(
            middle_back_kernel(layer),
            Named(
                middle_grad=own_f32,
                outer=own_b16,
                rows=shaped((4, width), F32),
            ),
            exchange_list(mlp_back.terms, TENSOR),
            grad_own,
            middle.kept,
            last.mlp_out,
            mods,
        )
        outs = Named(
            grads=shaped((tokens, width + 3 * part), BF16),
            terms=terms_out(),
            out_bias=row,
            in_bias=shaped((1, 3 * part), F32),
        )
        others = None
        if layer == 0 and near:
            outs.sent = shaped((2 * cuts, 6 + 4 * shards, part), F32)
            outs.terms = shaped((tokens, width), F32)
            others = (middle_back.rows, mlp_back.bias, mod_rows[1], bias_rows[1])
        elif layer == 0:
            outs.rows = shaped((2, width), F32)
        attn_back = run(
            attend_back_kernel(layer),
            outs,
            gather_list(middle_back.outer, TENSOR),
            packed,
            attn.kept,
            others,
            flops=2 * attend_flops,
        )
        grads = run(
            grads_kernel,
            Named(grads=shaped((2 * shards, 3, rows, width // 2), BF16)),
            mlp.kept,
            mlp_back.grads,
            attn.kept,
            attn_back.grads,
            flops=mlp_flops + 2 * tokens * width * width,
        ).grads
        blocks[layer] = lax.psum_scatter(grads, ROWS, scatter_dimension=0, tiled=False)
        terms = attn_back.terms
        if layer == 0 and near:
            sent = run(
                slots_kernel,
                Named(sent=[shaped((16, part), F32)] * shards),
                spot,
                across(attn_back.sent, LAYER),
            ).sent
            got = exchange_list(sent, SLOTS)
            terms = run(
                split_kernel, Named(terms=terms_out()), terms, wait=tuple(got[1:])
            ).terms
        outs = Named(input_grad=own_f32)
        if layer == 1:
            outs.rows, outs.grad, outs.lower = shaped((2, width), F32), own_b16, own_b16
        first_back = run(
            first_back_kernel(layer),
            outs,
            exchange_list(terms, TENSOR),
            middle_back.middle_grad,
            inputs,
            mods,
        )
        input_grads[layer] = first_back.input_grad
        if layer == 1 or not near:
            mod_rows[layer] = [
                attn_back.rows if layer == 0 else first_back.rows,
                middle_back.rows,
            ]
        bias_rows[layer] = (attn_back.in_bias, attn_back.out_bias, mlp_back.bias)

        if layer == 1:
            grad_own = first_back.grad
            pieces = gather_list(first_back.lower, TENSOR)

    given = swap(pick(blocks[1], blocks[0]))
    if near:
        ready = run(
            assemble_kernel,
            Named(
                upper=shaped((rows, hidden_part), F32),
                lower=shaped((rows, hidden_part), F32),
                inner=shaped((3, rows, part), F32),
                outer=shaped((part, rows), F32),
            ),
            spot,
            blocks[0],
            blocks[1],
            given,
        )
        grad_upper, grad_lower, grad_outer = ready.upper, ready.lower.T, ready.outer
        grad_inner = jnp.moveaxis(ready.inner, 0, 1)
    else:
        own = pick(blocks[0], blocks[1])
        grads = jnp.concatenate([pick(own, given), pick(given, own)], axis=2).astype(F32)
        grad_upper, grad_lower = grads[0], grads[1].T
        grad_inner = grads[2, :, : 3 * part].reshape(rows, 3, part)
        grad_outer = grads[2, :, 3 * part :].T

    if near:
        mod_slots = place([member[:12] for member in got], SLOTS)
        bias_total = sum(member[12:] for member in got)
    else:
        tail = run(
            pack_kernel,
            Named(
                mods=[shaped((12, part), F32) for k in range(cuts)],
                kept=shaped((shards, 4, rows), F32),
                given=shaped((shards, 4, rows), F32),
            ),
            spot,
            mod_rows[0],
            mod_rows[1],
            bias_rows[0],
            bias_rows[1],
        )
        mod_shard = sum(exchange_list(tail.mods, TENSOR))
        mod_given, mod_kept = pick(mod_shard[6:], mod_shard[:6]), pick(mod_shard[:6], mod_shard[6:])
        mod_got, bias_got = swap(mod_given), swap(tail.given)
        mod_micro = jnp.concatenate([pick(mod_kept, mod_got), pick(mod_got, mod_kept)], axis=0)
        bias_sum = tail.kept + bias_got
        mod_slots = lax.all_gather(mod_micro, SLOTS, axis=0, tiled=True)
        bias_total = lax.psum_scatter(bias_sum, SLOTS, scatter_dimension=0, tiled=False)
    mod_slots = mod_slots.reshape(shards * micro_count, 6 * part)
    if near:
        sent = run(
            act_kernel,
            Named(sent=shaped((2 * cuts, shards * micro_count, rows), F32)),
            spot,
            got,
            jnp.moveaxis(modulate_weight[0], 1, 0),
        ).sent
        act_grad = jnp.sum(across(sent, LAYER), axis=0)
        act_all = place(gather_list(act_grad, SLOTS), SLOTS)
    else:
        act_grad = lax.dot_general(
            mod_slots, mod_weight.astype(F32), (((1,), (1,)), ((), ())), precision=HIGH
        )
        act_grad = act_grad + swap(act_grad)
        act_grad = sum(gather_list(act_grad, TENSOR))
        act_all = lax.all_gather(act_grad, SLOTS, axis=0)
    act_all = jnp.moveaxis(act_all, 0, 1).reshape(-1, width)
    cond_grad = jax.vjp(jax.nn.silu, condition)[1](act_all)[0]
    pieces = []
    rest = cond_grad
    for _ in range(3):
        pieces.append(rest.astype(BF16))
        rest = rest - pieces[-1].astype(F32)
    pieces = jnp.concatenate(pieces, axis=0)
    table_grad = dot(jnp.concatenate([class_hot.astype(BF16)] * 3, axis=0), pieces, 0, 0)
    time_grad = dot(jnp.concatenate([time_feats] * 3, axis=0), pieces, 0, 0)
    grad_mod_weight = lax.dot_general(
        act_rows.astype(F32), mod_slots, (((0,), (0,)), ((), ())), precision=HIGH
    ).reshape(rows, 6, part)
    mod_bias_sum = jnp.sum(mod_slots, axis=0).reshape(6, part)
    grad_mod_bias = lax.dynamic_slice_in_dim(mod_bias_sum, shard * bias_cols, bias_cols, 1)
    grad_in_bias = bias_total[0, : in_bias_own.shape[1]].reshape(2, -1)

    def by_micro(first, second):
        got = swap(pick(second, first))
        held = pick(first, second)
        return jnp.stack([pick(held, got), pick(got, held)])[None, :, None]

    return (
        by_micro(kept[0][4].output, kept[1][4].output),
        by_micro(input_grads[0], input_grads[1]),
        table_grad,
        time_grad,
        grad_inner[None],
        grad_in_bias[None],
        grad_outer[None],
        bias_total[2][None],
        grad_upper[None],
        bias_total[1][None],
        grad_lower[None],
        bias_total[3][None],
        grad_mod_weight[None],
        grad_mod_bias[None],
    )


def solution(mesh):
    in_specs = (
        P(None, SLOTS, TENSOR, None),
        P(None, SLOTS, TENSOR, None),
        P(None, SLOTS),
        P(None, SLOTS),
        P(None, SLOTS),
        P(),
        P(),
        P(SECTION, SLOTS, None, TENSOR),
        P(SECTION, None, (TENSOR, SLOTS)),
        P(SECTION, TENSOR, SLOTS),
        P(SECTION, SLOTS),
        P(SECTION, SLOTS, TENSOR),
        P(SECTION, (TENSOR, SLOTS)),
        P(SECTION, TENSOR, SLOTS),
        P(SECTION, SLOTS),
        P(SECTION, SLOTS, None, TENSOR),
        P(SECTION, None, (TENSOR, SLOTS)),
    )
    out_specs = (
        P(SECTION, None, SLOTS, TENSOR, None),
        P(SECTION, None, SLOTS, TENSOR, None),
        P(),
        P(),
        P(SECTION, SLOTS, None, TENSOR),
        P(SECTION, None, (TENSOR, SLOTS)),
        P(SECTION, TENSOR, SLOTS),
        P(SECTION, SLOTS),
        P(SECTION, SLOTS, TENSOR),
        P(SECTION, (TENSOR, SLOTS)),
        P(SECTION, TENSOR, SLOTS),
        P(SECTION, SLOTS),
        P(SECTION, SLOTS, None, TENSOR),
        P(SECTION, None, (TENSOR, SLOTS)),
    )
    return jax.shard_map(body, mesh=mesh, in_specs=in_specs, out_specs=out_specs, check_vma=False)
```

```python
import math
from types import SimpleNamespace as Named

import jax
import jax.numpy as jnp
from jax import lax
from jax.experimental import pallas as pl
from jax.experimental.pallas import tpu as pltpu
from jax.sharding import PartitionSpec as P

HD = 64
EPS = 1e-06
HIGH = lax.Precision.HIGHEST
F32 = jnp.float32
BF16 = jnp.bfloat16
SECTION, TENSOR, SLOTS = "section", "tensor", "dp"
LAYER = (SECTION, TENSOR)
ROWS = (SLOTS, SECTION)
SPACE = 40 * 1024 * 1024


def cyclic(axis):
    size = lax.axis_size(axis)
    return size & (size - 1) != 0


def exchange(value, axis, k):
    size = lax.axis_size(axis)
    if cyclic(axis):
        return lax.ppermute(value, axis, [(i, (i - k) % size) for i in range(size)])
    return lax.ppermute(value, axis, [(i, i ^ k) for i in range(size)])


def fetch(value, axis, k):
    size = lax.axis_size(axis)
    if cyclic(axis):
        return lax.ppermute(value, axis, [(i, (i + k) % size) for i in range(size)])
    return lax.ppermute(value, axis, [(i, i ^ k) for i in range(size)])


def partner(axis, k):
    here = lax.axis_index(axis)
    if cyclic(axis):
        return (here - k) % lax.axis_size(axis)
    return here ^ k


def swap(value):
    return lax.ppermute(value, SECTION, [(0, 1), (1, 0)])


def across(value, axis):
    return lax.all_to_all(value, axis, 0, 0)


def gather_list(value, axis):
    got = {k: fetch(value, axis, k) for k in reversed(range(1, lax.axis_size(axis)))}
    return [value] + [got[k] for k in range(1, lax.axis_size(axis))]


def exchange_list(values, axis):
    got = {k: exchange(values[k], axis, k) for k in reversed(range(1, lax.axis_size(axis)))}
    return [values[0]] + [got[k] for k in range(1, lax.axis_size(axis))]


def place(pieces, axis):
    out = jnp.zeros((len(pieces),) + pieces[0].shape, pieces[0].dtype)
    for k, piece in enumerate(pieces):
        out = lax.dynamic_update_index_in_dim(out, piece, partner(axis, k), 0)
    return out


def shaped(shape, dtype):
    return jax.ShapeDtypeStruct(shape, dtype)


class Part:
    def __init__(self, value, at=None):
        self.value, self.at = value, at
        self.shape, self.dtype = value.shape, value.dtype


def run(kernel, outs, *args, flops=0, wait=()):
    def leafy(value):
        return isinstance(value, Part)

    names = list(vars(outs))
    out_flat, out_tree = jax.tree.flatten([vars(outs)[name] for name in names])
    flat, tree = jax.tree.flatten(args, is_leaf=leafy)
    moved = sum(math.prod(leaf.shape) * leaf.dtype.itemsize for leaf in flat + out_flat)

    def inner(*refs):
        ins = list(refs[: len(flat)])
        for k, leaf in enumerate(flat):
            if leafy(leaf) and leaf.at is not None:
                ins[k] = Named(ref=ins[k], at=leaf.at)
        results = jax.tree.unflatten(out_tree, refs[len(flat) + len(wait) :])
        kernel(*jax.tree.unflatten(tree, ins), Named(**dict(zip(names, results))))

    result = pl.pallas_call(
        inner,
        out_shape=out_flat,
        in_specs=[
            pl.BlockSpec(memory_space=pltpu.SMEM if leaf.dtype == jnp.int32 else pltpu.VMEM)
            for leaf in flat
        ]
        + [pl.BlockSpec(memory_space=pl.ANY)] * len(wait),
        out_specs=[pl.BlockSpec(memory_space=pltpu.VMEM)] * len(out_flat),
        compiler_params=pltpu.CompilerParams(vmem_limit_bytes=SPACE),
        cost_estimate=pl.CostEstimate(flops=flops, bytes_accessed=moved, transcendentals=0),
    )(*[leaf.value if leafy(leaf) else leaf for leaf in flat], *wait)
    return Named(**dict(zip(names, jax.tree.unflatten(out_tree, result))))


def matrix(ref):
    if isinstance(ref, Named):
        value = ref.ref[:, ref.at]
        return value.reshape(-1, value.shape[-1])
    return ref[...]


def norm_parts(values):
    average = jnp.mean(values, axis=-1, keepdims=True)
    centred = values - average
    spread = jnp.mean(centred * centred, axis=-1, keepdims=True)
    scale = lax.rsqrt(spread + EPS)
    return centred * scale, scale


def norm_pull(grad, normed, scale):
    first = jnp.mean(grad, axis=-1, keepdims=True)
    second = jnp.mean(grad * normed, axis=-1, keepdims=True)
    return scale * (grad - first - normed * second)


def dot(left, right, left_dim, right_dim):
    return lax.dot_general(
        left, right, (((left_dim,), (right_dim,)), ((), ())), preferred_element_type=F32
    )


def joined(refs):
    return jnp.concatenate([ref[...] for ref in refs], axis=0)


def summed(refs):
    total = refs[0][...].astype(F32)
    for ref in refs[1:]:
        total = total + ref[...].astype(F32)
    return total


def spread_out(terms, refs):
    rows = refs[0].shape[0]
    for k, ref in enumerate(refs):
        ref[...] = terms[k * rows : (k + 1) * rows].astype(ref.dtype)


def column_sum(values):
    return jnp.sum(values.astype(F32), axis=0, keepdims=True)


def softmax_parts(query, key):
    scores = dot(query, key, 1, 1) * HD**-0.5
    raised = jnp.exp(scores - jnp.max(scores, axis=-1, keepdims=True))
    return raised / jnp.sum(raised, axis=-1, keepdims=True)


def assemble(spot, pieces, ref):
    own, other = pieces
    rows = own.shape[1]
    for k in range(own.shape[0]):
        for half, block in ((spot[0], own[k]), (1 - spot[0], other[k])):
            at = pl.multiple_of((2 * spot[3 + k] + half) * rows, rows)
            ref[pl.ds(at, rows), :] = block


def attend(first, mods, packed, in_bias, refs, layer):
    width = packed.shape[1] // 4
    attn_in = joined(first)
    if layer == 0:
        refs.kept[:, 2 * packed.shape[1] :] = attn_in
        normed = norm_parts(attn_in.astype(F32))[0]
        attn_in = (normed * (1.0 + mods[1:2]) + mods[0:1]).astype(BF16)
    refs.kept[:, : packed.shape[1]] = attn_in
    projected = dot(attn_in, packed[:, : 3 * width], 1, 0)
    queries = (projected[:, :width] + in_bias[0:1]).astype(BF16)
    keys = projected[:, width : 2 * width].astype(BF16)
    values = (projected[:, 2 * width :] + in_bias[1:2]).astype(BF16)
    mixed = []
    for at in range(0, width, HD):
        attention = softmax_parts(queries[:, at : at + HD], keys[:, at : at + HD])
        mixed.append(dot(attention.astype(BF16), values[:, at : at + HD], 1, 0))
    mixed = jnp.concatenate(mixed, axis=1).astype(BF16)
    refs.kept[:, packed.shape[1] : 2 * packed.shape[1]] = jnp.concatenate(
        [queries, keys, values, mixed], axis=1
    )
    spread_out(dot(mixed, packed[:, 3 * width :], 1, 1), refs.terms)


def attend_kernel(layer):
    def kernel(spot, first, mods_ref, packed_ref, bias_ref, refs):
        if isinstance(packed_ref, tuple):
            assemble(spot, packed_ref, refs.packed)
            packed_ref = refs.packed
        attend(first, mods_ref[6 * layer : 6 * layer + 6], matrix(packed_ref), bias_ref[...], refs, layer)

    return kernel


def middle_kernel(layer):
    def kernel(terms, inputs, mods_ref, bias_ref, refs):
        mods = mods_ref[6 * layer : 6 * layer + 6]
        attn_out = summed(terms) + bias_ref[2:3]
        rows = attn_out.shape[0]
        refs.kept[:rows] = attn_out
        middle = inputs[...].astype(F32) + mods[2:3] * attn_out
        refs.kept[rows:] = middle
        normed = norm_parts(middle)[0]
        refs.mlp_in[...] = (normed * (1.0 + mods[4:5]) + mods[3:4]).astype(BF16)

    return kernel


def mlp_kernel(pieces, upper, lower, bias_ref, refs):
    mlp_in = joined(pieces)
    size = upper.ref.shape[-1] if isinstance(upper, Named) else upper.shape[-1]
    wide = mlp_in.shape[1]
    refs.kept[:, :wide] = mlp_in
    values = dot(mlp_in, matrix(upper), 1, 0) + bias_ref[1:2]
    root = math.sqrt(2.0 / math.pi)
    square = values * values
    bent = jnp.tanh(root * (values + 0.044715 * values * square))
    hidden = (0.5 * values * (1.0 + bent)).astype(BF16)
    refs.kept[:, wide : wide + size] = hidden
    slope = 0.5 * (1.0 + bent) + 0.5 * values * (1.0 - bent * bent) * root * (
        1.0 + 0.134145 * square
    )
    refs.kept[:, wide + size :] = slope.astype(BF16)
    spread_out(dot(hidden, matrix(lower), 1, 1), refs.terms)


def last_kernel(layer):
    def kernel(terms, kept, mods_ref, bias_ref, refs):
        mlp_out = summed(terms) + bias_ref[3:4]
        refs.mlp_out[...] = mlp_out
        output = (kept[kept.shape[0] // 2 :] + mods_ref[6 * layer + 5 : 6 * layer + 6] * mlp_out).astype(BF16)
        refs.output[...] = output
        if layer == 0:
            normed = norm_parts(output.astype(F32))[0]
            refs.attn_in[...] = (normed * (1.0 + mods_ref[7:8]) + mods_ref[6:7]).astype(BF16)

    return kernel


def mlp_back_kernel(layer):
    def kernel(pieces, mods_ref, upper, lower, kept, refs):
        lower_grad = joined(pieces)
        if layer == 1:
            lower_grad = (lower_grad.astype(F32) * mods_ref[11:12]).astype(BF16)
        wide = lower_grad.shape[1]
        refs.grads[:, :wide] = lower_grad
        pre_grad = dot(lower_grad, matrix(lower), 1, 0)
        slope = kept[:, wide + pre_grad.shape[1] :].astype(F32)
        pre_grad = (pre_grad * slope).astype(BF16)
        refs.grads[:, wide:] = pre_grad
        spread_out(dot(pre_grad, matrix(upper), 1, 1), refs.terms)
        refs.bias[0:1] = column_sum(pre_grad)
        refs.bias[1:2] = column_sum(lower_grad)

    return kernel


def middle_back_kernel(layer):
    def kernel(terms, grad_ref, kept, mlp_out, mods_ref, refs):
        mods = mods_ref[6 * layer : 6 * layer + 6]
        grad = grad_ref[...].astype(F32)
        mid_grad = summed(terms)
        normed, scale = norm_parts(kept[kept.shape[0] // 2 :])
        middle_grad = grad + norm_pull(mid_grad * (1.0 + mods[4:5]), normed, scale)
        refs.middle_grad[...] = middle_grad
        refs.outer[...] = (middle_grad * mods[2:3]).astype(BF16)
        refs.rows[0:1] = column_sum(middle_grad * kept[: kept.shape[0] // 2])
        refs.rows[1:2] = column_sum(mid_grad)
        refs.rows[2:3] = column_sum(mid_grad * normed)
        refs.rows[3:4] = column_sum(grad * mlp_out[...])

    return kernel


def attend_back_kernel(layer):
    def kernel(pieces, packed, kept, others, refs):
        outer_grad = joined(pieces)
        wide = outer_grad.shape[1]
        refs.grads[:, :wide] = outer_grad
        packed = matrix(packed)
        width = packed.shape[1] // 4
        mixed_grad = dot(outer_grad, packed[:, 3 * width :], 1, 0).astype(BF16)
        queries, keys, values = [
            kept[:, wide + k * width : wide + (k + 1) * width] for k in range(3)
        ]
        d_queries, d_keys, d_values = [], [], []
        for at in range(0, width, HD):
            query, key = queries[:, at : at + HD], keys[:, at : at + HD]
            grad = mixed_grad[:, at : at + HD]
            attention = softmax_parts(query, key)
            weight_grad = dot(grad, values[:, at : at + HD], 1, 1)
            d_values.append(dot(attention.astype(BF16), grad, 0, 0))
            row_dot = jnp.sum(attention * weight_grad, axis=-1, keepdims=True)
            score_grad = (attention * (weight_grad - row_dot)).astype(BF16)
            d_queries.append(dot(score_grad, key, 1, 0) * HD**-0.5)
            d_keys.append(dot(score_grad, query, 0, 0) * HD**-0.5)
        stacked = jnp.concatenate(d_queries + d_keys + d_values, axis=1).astype(BF16)
        refs.grads[:, wide:] = stacked
        terms = dot(stacked, packed[:, : 3 * width], 1, 1)
        if others is None:
            spread_out(terms, refs.terms)
        else:
            refs.terms[...] = terms
        in_bias, out_bias = column_sum(stacked), column_sum(outer_grad)
        refs.out_bias[...] = out_bias
        refs.in_bias[...] = in_bias
        if layer == 0:
            normed = norm_parts(kept[:, 2 * wide :].astype(F32))[0]
            rows = jnp.concatenate([column_sum(terms), column_sum(terms * normed)], axis=0)
            if others is None:
                refs.rows[...] = rows
            else:
                middle_rows, mlp_bias, other_rows, other_bias = others
                mods = [
                    jnp.concatenate([rows, middle_rows[...]], axis=0),
                    jnp.concatenate([ref[...] for ref in other_rows], axis=0),
                ]
                send_rows(mods, [(in_bias, out_bias, mlp_bias), other_bias], refs.sent)

    return kernel


def first_back_kernel(layer):
    def kernel(terms, middle_grad, inputs, mods_ref, refs):
        in_grad = summed(terms)
        normed, scale = norm_parts(inputs[...].astype(F32))
        scale_one = mods_ref[6 * layer + 1 : 6 * layer + 2]
        input_grad = middle_grad[...] + norm_pull(in_grad * (1.0 + scale_one), normed, scale)
        refs.input_grad[...] = input_grad
        if layer == 1:
            refs.rows[0:1] = column_sum(in_grad)
            refs.rows[1:2] = column_sum(in_grad * normed)
            rounded = input_grad.astype(BF16)
            refs.grad[...] = rounded
            refs.lower[...] = (rounded.astype(F32) * mods_ref[5:6]).astype(BF16)

    return kernel


def cut(grad, ref, at):
    count, rows, half = ref.shape[0], ref.shape[2], ref.shape[3]
    for block in range(count):
        place_at = block // 2 * rows
        ref[block, at] = grad[
            place_at : place_at + rows, block % 2 * half : block % 2 * half + half
        ].astype(BF16)


def grads_kernel(mlp_kept, mlp_grads, attn_kept, attn_grads, refs):
    wide = 2 * refs.grads.shape[3]
    size, width = mlp_grads.shape[1] - wide, wide // 4
    cut(dot(mlp_kept[:, :wide], mlp_grads[:, wide:], 0, 0), refs.grads, 0)
    cut(dot(mlp_grads[:, :wide], mlp_kept[:, wide : wide + size], 0, 0), refs.grads, 1)
    inner = dot(attn_kept[:, :wide], attn_grads[:, wide:], 0, 0)
    outer = dot(attn_grads[:, :wide], attn_kept[:, wide + 3 * width : 2 * wide], 0, 0)
    cut(jnp.concatenate([inner, outer], axis=1), refs.grads, 2)


def mods_kernel(spot, got, refs):
    cuts = got.shape[0] // 2
    count = (got.shape[1] - 6) // 4
    cols = refs.inner[0].shape[1] // count
    for layer in range(2):
        refs.mods[6 * layer : 6 * layer + 6] = jnp.concatenate(
            [got[cuts * layer + t, :6] for t in range(cuts)], axis=1
        )
        rows = got[cuts * layer + spot[1], 6:]
        pieces = [rows[4 * k : 4 * k + 4] for k in range(count)]
        refs.biases[layer][...] = jnp.concatenate(pieces, axis=1)
        for k in range(2):
            refs.inner[layer][k : k + 1] = jnp.concatenate(
                [piece[0:1, k * cols : (k + 1) * cols] for piece in pieces], axis=1
            )


def bias_rows_of(part, rows, shards, in_bias, out_bias, mlp_bias):
    cols = part // shards
    pieces = []
    for z in range(shards):
        start = jnp.concatenate(
            [
                in_bias[:, z * cols : (z + 1) * cols],
                in_bias[:, 2 * part + z * cols : 2 * part + (z + 1) * cols],
                jnp.zeros((1, rows - 2 * cols), F32),
            ],
            axis=1,
        )
        at = slice(z * rows, (z + 1) * rows)
        pieces += [start, mlp_bias[0:1, at], out_bias[:, at], mlp_bias[1:2, at]]
    return jnp.concatenate(pieces, axis=0)


def send_rows(mods, biases, sent):
    cuts, part = sent.shape[0] // 2, sent.shape[2]
    shards = (sent.shape[1] - 6) // 4
    for layer in range(2):
        rows = bias_rows_of(part, part, shards, *biases[layer])
        for t in range(cuts):
            sent[cuts * layer + t, :6] = mods[layer][:, t * part : (t + 1) * part]
            sent[cuts * layer + t, 6:] = rows


def pack_kernel(spot, mod_one, mod_two, bias_one, bias_two, refs):
    core, here, cycle = spot[0], spot[1], spot[2]
    mods = jnp.concatenate([ref[...] for ref in mod_one + mod_two], axis=0)
    cuts = len(refs.mods)
    part = mods.shape[1] // cuts
    blocks = [mods[:, j * part : (j + 1) * part] for j in range(cuts)]
    for k, ref in enumerate(refs.mods):
        index = jnp.where(cycle == 1, (here - k + cuts) % cuts, here ^ k)
        chosen = blocks[0]
        for j in range(1, cuts):
            chosen = jnp.where(index == j, blocks[j], chosen)
        ref[...] = chosen
    shards, _, rows = refs.kept.shape
    first = bias_rows_of(part, rows, shards, *bias_one)
    second = bias_rows_of(part, rows, shards, *bias_two)
    for z in range(shards):
        at = slice(4 * z, 4 * z + 4)
        refs.kept[z] = jnp.where(core == 0, first[at], second[at])
        refs.given[z] = jnp.where(core == 0, second[at], first[at])


def bundle_kernel(members):
    def kernel(spot, kept, got, refs):
        for k, (weight, layer) in enumerate(members):
            refs.rows[k] = jnp.where(spot[0] == layer, kept[weight], got[weight])

    return kernel


def slots_kernel(spot, received, refs):
    cuts = received.shape[0] // 2
    shards = (received.shape[1] - 6) // 4
    mods = []
    for micro in range(2):
        total = received[cuts * micro, :6]
        for t in range(1, cuts):
            total = total + received[cuts * micro + t, :6]
        mods.append(total)
    here = spot[1]
    biases = received[here, 6:] + received[cuts + here, 6:]
    for k, ref in enumerate(refs.sent):
        ref[:6], ref[6:12] = mods
        total = biases[:4]
        for z in range(1, shards):
            total = jnp.where(spot[3 + k] == z, biases[4 * z : 4 * z + 4], total)
        ref[12:16] = total


def modulate_kernel(act, weights, mod_bias, own, refs):
    shards, _, part = refs.sent.shape
    micro = act.shape[0] // shards
    for k in range(6):
        terms = dot(act[...], weights[k], 1, 0) + mod_bias[k : k + 1]
        for z in range(shards):
            for m in range(micro):
                at = z * micro + m
                refs.sent[z, 6 * m + k : 6 * m + k + 1] = terms[at : at + 1]
    for z in range(shards):
        refs.sent[z, 6 * micro :] = own[...]


def act_kernel(spot, pieces, weights, refs):
    shards = len(pieces)
    blocks = []
    for z in range(shards):
        chosen = pieces[0][...]
        for k in range(1, shards):
            chosen = jnp.where(spot[3 + k] == z, pieces[k][...], chosen)
        blocks.append(chosen)
    total = jnp.zeros(refs.sent.shape[1:], F32)
    for k in range(6):
        rest = jnp.concatenate([b[at : at + 1] for b in blocks for at in (k, 6 + k)], axis=0)
        for _ in range(3):
            rounded = rest.astype(BF16)
            total = total + dot(rounded, weights[k], 1, 1)
            rest = rest - rounded.astype(F32)
    repeat_rows(total, refs.sent)


def repeat_rows(values, ref):
    for k in range(ref.shape[0]):
        ref[k] = values


def assemble_kernel(spot, first, second, given, refs):
    wide = []
    for k in range(3):
        own = jnp.where(spot[0] == 0, first[k], second[k]).astype(F32)
        other = given[k].astype(F32)
        left, right = jnp.where(spot[0] == 0, own, other), jnp.where(spot[0] == 0, other, own)
        wide.append(jnp.concatenate([left, right], axis=1))
    refs.upper[...], refs.lower[...] = wide[0], wide[1]
    width = wide[2].shape[1] // 4
    for k in range(3):
        refs.inner[k] = wide[2][:, k * width : (k + 1) * width]
    refs.outer[...] = wide[2][:, 3 * width :].T


def split_kernel(terms, refs):
    spread_out(terms[...], refs.terms)


def prepare_kernel(spot, inner, outer, upper, lower, refs):
    half = upper.shape[0] // 2
    packed = jnp.concatenate([inner[0], inner[1], inner[2], outer[...].T], axis=1)
    for k, member in enumerate((packed, upper[...], lower[...])):
        first, second = member[:half], member[half:]
        refs.kept[k] = jnp.where(spot[0] == 0, first, second)
        refs.given[k] = jnp.where(spot[0] == 0, second, first)


def sinus_features(stamps, columns):
    halfway = columns // 2
    frequency = jnp.exp(-math.log(10000.0) * jnp.arange(halfway, dtype=F32) / halfway)
    angles = stamps.astype(F32)[:, None] * frequency[None, :]
    return jnp.concatenate([jnp.cos(angles), jnp.sin(angles)], axis=-1)


def body(
    latents,
    cotangent,
    labels,
    timesteps,
    occupied,
    class_table,
    time_weight,
    project_in,
    project_in_bias,
    project_out,
    project_out_bias,
    up_weight,
    up_bias,
    down_weight,
    down_bias,
    modulate_weight,
    modulate_bias,
):
    core = lax.axis_index(SECTION)
    shard = lax.axis_index(SLOTS)
    shards = lax.axis_size(SLOTS)
    cuts = lax.axis_size(TENSOR)
    micro_count = latents.shape[0]
    width = latents.shape[3]
    own_tokens = latents.shape[2]
    tokens = own_tokens * cuts
    part = width // cuts
    rows = width // shards
    hidden_part = up_weight.shape[2]
    near = shards <= 8 and not cyclic(SLOTS) and rows == part

    def pick(first, second):
        return jnp.where(core == 0, first, second)

    spot = jnp.stack(
        [core, lax.axis_index(TENSOR), jnp.int32(1 if cyclic(TENSOR) else 0)]
        + [partner(SLOTS, k) for k in range(shards if near else 0)]
        + [partner(TENSOR, k) for k in range(cuts)]
    ).astype(jnp.int32)

    half = rows // 2
    if near:
        inner = jnp.moveaxis(project_in[0], 1, 0)
        ready = run(
            prepare_kernel,
            Named(kept=shaped((3, half, width), BF16), given=shaped((3, half, width), BF16)),
            spot,
            inner,
            project_out[0],
            up_weight[0],
            down_weight[0].T,
        )
        given = swap(ready.given)
        kept_halves, got_halves = ready.kept, given
    else:
        packed_own = jnp.concatenate(
            [project_in[0, :, 0], project_in[0, :, 1], project_in[0, :, 2], project_out[0].T], axis=1
        )
        stack = [packed_own, up_weight[0], down_weight[0].T]
        given = swap(jnp.concatenate([pick(member[half:], member[:half]) for member in stack]))
        kept_halves = [pick(member[:half], member[half:]) for member in stack]
        got_halves = [given[k * half : (k + 1) * half] for k in range(3)]

    def bundle(members, wait):
        return run(
            bundle_kernel(members),
            Named(rows=shaped((len(members), half, width), BF16)),
            spot,
            kept_halves,
            got_halves,
            wait=wait,
        ).rows

    bundles = []

    def gather_blocks(members, wait=()):
        if near:
            own = bundle(members, wait)
            bundles.append(own)
            whole = lax.all_gather(own, ROWS, axis=0)
            return [Part(whole, k) for k in range(len(members))]
        return [
            gather_rows(
                pick(kept_halves[k], got_halves[k])
                if layer == 0
                else pick(got_halves[k], kept_halves[k])
            )
            for k, layer in members
        ]

    def gather_rows(value):
        return lax.all_gather(value, ROWS, axis=0, tiled=True)

    stamps = jnp.concatenate([labels.reshape(1, -1), timesteps.reshape(1, -1)], axis=1)
    if near:
        stamps = place(gather_list(stamps, SLOTS), SLOTS).reshape(shards, -1)
    else:
        stamps = lax.all_gather(stamps, SLOTS, axis=0, tiled=True)
    flat_labels = stamps[:, :micro_count].reshape(-1)
    flat_times = stamps[:, micro_count:].reshape(-1)
    class_count = class_table.shape[0]
    class_hot = flat_labels[:, None] == jnp.arange(class_count, dtype=jnp.int32)[None, :]
    time_feats = sinus_features(flat_times, time_weight.shape[0]).astype(BF16)
    condition = dot(class_hot.astype(BF16), class_table, 1, 0) + dot(time_feats, time_weight, 1, 0)
    cond_act = jax.nn.silu(condition).astype(BF16)
    act_rows = lax.dynamic_slice_in_dim(cond_act, shard * rows, rows, 1)

    if near:
        first_pieces = gather_list(pick(kept_halves[0], got_halves[0]), SLOTS)
    else:
        (first_a,) = gather_blocks([(0, 0)])

    tokens_own = pick(latents[0, 0], latents[1, 0])
    seed_own = pick(
        cotangent[0, 0] * occupied[0, 0].astype(BF16), cotangent[1, 0] * occupied[1, 0].astype(BF16)
    )
    token_list = gather_list(tokens_own, TENSOR)

    mod_weight = modulate_weight[0].reshape(rows, -1)
    bias_cols = modulate_bias.shape[2]
    bias_full = lax.dynamic_update_slice_in_dim(
        jnp.zeros((6, part), F32), modulate_bias[0].astype(F32), shard * bias_cols, 1
    )
    mod_terms = dot(act_rows, mod_weight, 1, 0) + bias_full.reshape(1, -1)
    mod_terms = mod_terms.reshape(shards, micro_count * 6, part)
    in_bias_own = project_in_bias.astype(F32).reshape(1, -1)
    bias_own = jnp.concatenate(
        [
            jnp.pad(in_bias_own, ((0, 0), (0, rows - in_bias_own.shape[1]))),
            up_bias.astype(F32),
            project_out_bias.astype(F32),
            down_bias.astype(F32),
        ],
        axis=0,
    )
    if near:
        sent = run(
            modulate_kernel,
            Named(sent=shaped((shards, 6 * micro_count + 4, part), F32)),
            act_rows,
            jnp.moveaxis(modulate_weight[0], 1, 0),
            bias_full,
            bias_own,
        ).sent
        got = across(sent, SLOTS)
        mod_sum = jnp.sum(got[:, : micro_count * 6], axis=0).reshape(micro_count, 6, part)
        bias_all = jnp.broadcast_to(
            got[:, micro_count * 6 :].reshape(1, 4 * shards, part), (micro_count, 4 * shards, part)
        )
        sent = jnp.concatenate([mod_sum, bias_all], axis=1)
        got_all = across(jnp.repeat(sent, cuts, axis=0), LAYER)
        ready = run(
            mods_kernel,
            Named(
                mods=shaped((12, width), F32),
                biases=[shaped((4, width), F32)] * 2,
                inner=[shaped((2, part), F32)] * 2,
            ),
            spot,
            got_all,
        )
        mods, biases, in_biases = ready.mods, ready.biases, ready.inner
    else:
        mod_sum = lax.psum_scatter(mod_terms, SLOTS, scatter_dimension=0, tiled=False)
        bias_all = lax.all_gather(bias_own, SLOTS, axis=0)
        mod_got, bias_got = swap(pick(mod_sum[6:], mod_sum[:6])), swap(bias_all)
        mod_kept = pick(mod_sum[:6], mod_sum[6:])
        mod_both = jnp.concatenate([pick(mod_kept, mod_got), pick(mod_got, mod_kept)], axis=0)
        mod_list = gather_list(mod_both, TENSOR)
        mods = jnp.moveaxis(place(mod_list, TENSOR), 0, 1).reshape(12, width)
        in_biases, biases = [], []
        for member in (pick(bias_all, bias_got), pick(bias_got, bias_all)):
            cols = project_in_bias.shape[2]
            columns = member[:, 0, : 2 * cols].reshape(shards, 2, cols)
            in_biases.append(jnp.moveaxis(columns, 0, 1).reshape(2, part))
            biases.append(jnp.moveaxis(member, 0, 1).reshape(4, width))
    if near:
        first_stack = jnp.stack(first_pieces)
        first_a = (first_stack, swap(first_stack))
    first_u, first_d, second_a = gather_blocks([(1, 0), (2, 0), (0, 1)], (got, first_stack) if near else ())
    second_u, second_d = gather_blocks([(1, 1), (2, 1)], tuple(bundles))
    weights = [(first_a, first_u, first_d), (second_a, second_u, second_d)]

    def terms_out(count=1):
        return [shaped((own_tokens, width), F32)] + [
            shaped((own_tokens, width), BF16) for k in range(1, cuts)
        ]

    own_f32 = shaped((own_tokens, width), F32)
    both_f32 = shaped((2 * own_tokens, width), F32)
    own_b16 = shaped((own_tokens, width), BF16)
    attend_flops = 2 * tokens * width * width + 4 * tokens * tokens * part
    mlp_flops = 4 * tokens * width * hidden_part

    kept, packs = [], []
    inputs = tokens_own
    first = [jnp.concatenate(token_list)]
    for layer in range(2):
        packed, upper, lower = weights[layer]
        outs = Named(kept=shaped((tokens, (3 - layer) * width), BF16), terms=terms_out())
        if isinstance(packed, tuple):
            outs.packed = shaped((width, width), BF16)
        attn = run(
            attend_kernel(layer),
            outs,
            spot,
            first,
            mods,
            packed,
            in_biases[layer],
            flops=attend_flops,
        )
        packs.append(attn.packed if isinstance(packed, tuple) else packed)
        terms = exchange_list(attn.terms, TENSOR)
        middle = run(
            middle_kernel(layer),
            Named(kept=both_f32, mlp_in=own_b16),
            terms,
            inputs,
            mods,
            biases[layer],
        )
        mlp = run(
            mlp_kernel,
            Named(kept=shaped((tokens, width + 2 * hidden_part), BF16), terms=terms_out()),
            [jnp.concatenate(gather_list(middle.mlp_in, TENSOR))]
            if layer == 0
            else gather_list(middle.mlp_in, TENSOR),
            upper,
            lower,
            biases[layer],
            flops=mlp_flops,
        )
        outs = Named(mlp_out=own_f32, output=own_b16)
        if layer == 0:
            outs.attn_in = own_b16
        last = run(
            last_kernel(layer),
            outs,
            exchange_list(mlp.terms, TENSOR),
            middle.kept,
            mods,
            biases[layer],
        )
        kept.append((inputs, attn, middle, mlp, last))
        inputs = last.output
        if layer == 0:
            first = gather_list(last.attn_in, TENSOR)
            seed_list = [jnp.concatenate(gather_list(seed_own, TENSOR))]

    row = shaped((1, width), F32)
    grad_own, pieces = seed_own, seed_list
    mod_rows, bias_rows, blocks, input_grads = [None] * 2, [None] * 2, [None] * 2, [None] * 2
    for layer in (1, 0):
        packed, upper, lower = packs[layer], weights[layer][1], weights[layer][2]
        inputs, attn, middle, mlp, last = kept[layer]
        mlp_back = run(
            mlp_back_kernel(layer),
            Named(
                grads=shaped((tokens, width + hidden_part), BF16),
                terms=terms_out(),
                bias=shaped((2, hidden_part), F32),
            ),
            pieces,
            mods,
            upper,
            lower,
            mlp.kept,
            flops=mlp_flops,
        )
        middle_back = run(
            middle_back_kernel(layer),
            Named(
                middle_grad=own_f32,
                outer=own_b16,
                rows=shaped((4, width), F32),
            ),
            exchange_list(mlp_back.terms, TENSOR),
            grad_own,
            middle.kept,
            last.mlp_out,
            mods,
        )
        outs = Named(
            grads=shaped((tokens, width + 3 * part), BF16),
            terms=terms_out(),
            out_bias=row,
            in_bias=shaped((1, 3 * part), F32),
        )
        others = None
        if layer == 0 and near:
            outs.sent = shaped((2 * cuts, 6 + 4 * shards, part), F32)
            outs.terms = shaped((tokens, width), F32)
            others = (middle_back.rows, mlp_back.bias, mod_rows[1], bias_rows[1])
        elif layer == 0:
            outs.rows = shaped((2, width), F32)
        attn_back = run(
            attend_back_kernel(layer),
            outs,
            gather_list(middle_back.outer, TENSOR),
            packed,
            attn.kept,
            others,
            flops=2 * attend_flops,
        )
        grads = run(
            grads_kernel,
            Named(grads=shaped((2 * shards, 3, rows, width // 2), BF16)),
            mlp.kept,
            mlp_back.grads,
            attn.kept,
            attn_back.grads,
            flops=mlp_flops + 2 * tokens * width * width,
        ).grads
        blocks[layer] = lax.psum_scatter(grads, ROWS, scatter_dimension=0, tiled=False)
        terms = attn_back.terms
        if layer == 0 and near:
            sent = run(
                slots_kernel,
                Named(sent=[shaped((16, part), F32)] * shards),
                spot,
                across(attn_back.sent, LAYER),
            ).sent
            got = exchange_list(sent, SLOTS)
            terms = run(
                split_kernel, Named(terms=terms_out()), terms, wait=tuple(got[1:])
            ).terms
        outs = Named(input_grad=own_f32)
        if layer == 1:
            outs.rows, outs.grad, outs.lower = shaped((2, width), F32), own_b16, own_b16
        first_back = run(
            first_back_kernel(layer),
            outs,
            exchange_list(terms, TENSOR),
            middle_back.middle_grad,
            inputs,
            mods,
        )
        input_grads[layer] = first_back.input_grad
        if layer == 1 or not near:
            mod_rows[layer] = [
                attn_back.rows if layer == 0 else first_back.rows,
                middle_back.rows,
            ]
        bias_rows[layer] = (attn_back.in_bias, attn_back.out_bias, mlp_back.bias)

        if layer == 1:
            grad_own = first_back.grad
            pieces = gather_list(first_back.lower, TENSOR)

    given = swap(pick(blocks[1], blocks[0]))
    if near:
        ready = run(
            assemble_kernel,
            Named(
                upper=shaped((rows, hidden_part), F32),
                lower=shaped((rows, hidden_part), F32),
                inner=shaped((3, rows, part), F32),
                outer=shaped((part, rows), F32),
            ),
            spot,
            blocks[0],
            blocks[1],
            given,
        )
        grad_upper, grad_lower, grad_outer = ready.upper, ready.lower.T, ready.outer
        grad_inner = jnp.moveaxis(ready.inner, 0, 1)
    else:
        own = pick(blocks[0], blocks[1])
        grads = jnp.concatenate([pick(own, given), pick(given, own)], axis=2).astype(F32)
        grad_upper, grad_lower = grads[0], grads[1].T
        grad_inner = grads[2, :, : 3 * part].reshape(rows, 3, part)
        grad_outer = grads[2, :, 3 * part :].T

    if near:
        mod_slots = place([member[:12] for member in got], SLOTS)
        bias_total = sum(member[12:] for member in got)
    else:
        tail = run(
            pack_kernel,
            Named(
                mods=[shaped((12, part), F32) for k in range(cuts)],
                kept=shaped((shards, 4, rows), F32),
                given=shaped((shards, 4, rows), F32),
            ),
            spot,
            mod_rows[0],
            mod_rows[1],
            bias_rows[0],
            bias_rows[1],
        )
        mod_shard = sum(exchange_list(tail.mods, TENSOR))
        mod_given, mod_kept = pick(mod_shard[6:], mod_shard[:6]), pick(mod_shard[:6], mod_shard[6:])
        mod_got, bias_got = swap(mod_given), swap(tail.given)
        mod_micro = jnp.concatenate([pick(mod_kept, mod_got), pick(mod_got, mod_kept)], axis=0)
        bias_sum = tail.kept + bias_got
        mod_slots = lax.all_gather(mod_micro, SLOTS, axis=0, tiled=True)
        bias_total = lax.psum_scatter(bias_sum, SLOTS, scatter_dimension=0, tiled=False)
    mod_slots = mod_slots.reshape(shards * micro_count, 6 * part)
    if near:
        sent = run(
            act_kernel,
            Named(sent=shaped((2 * cuts, shards * micro_count, rows), F32)),
            spot,
            got,
            jnp.moveaxis(modulate_weight[0], 1, 0),
        ).sent
        act_grad = jnp.sum(across(sent, LAYER), axis=0)
        act_all = place(gather_list(act_grad, SLOTS), SLOTS)
    else:
        act_grad = lax.dot_general(
            mod_slots, mod_weight.astype(F32), (((1,), (1,)), ((), ())), precision=HIGH
        )
        act_grad = act_grad + swap(act_grad)
        act_grad = sum(gather_list(act_grad, TENSOR))
        act_all = lax.all_gather(act_grad, SLOTS, axis=0)
    act_all = jnp.moveaxis(act_all, 0, 1).reshape(-1, width)
    cond_grad = jax.vjp(jax.nn.silu, condition)[1](act_all)[0]
    pieces = []
    rest = cond_grad
    for _ in range(3):
        pieces.append(rest.astype(BF16))
        rest = rest - pieces[-1].astype(F32)
    pieces = jnp.concatenate(pieces, axis=0)
    table_grad = dot(jnp.concatenate([class_hot.astype(BF16)] * 3, axis=0), pieces, 0, 0)
    time_grad = dot(jnp.concatenate([time_feats] * 3, axis=0), pieces, 0, 0)
    grad_mod_weight = lax.dot_general(
        act_rows.astype(F32), mod_slots, (((0,), (0,)), ((), ())), precision=HIGH
    ).reshape(rows, 6, part)
    mod_bias_sum = jnp.sum(mod_slots, axis=0).reshape(6, part)
    grad_mod_bias = lax.dynamic_slice_in_dim(mod_bias_sum, shard * bias_cols, bias_cols, 1)
    grad_in_bias = bias_total[0, : in_bias_own.shape[1]].reshape(2, -1)

    def by_micro(first, second):
        got = swap(pick(second, first))
        held = pick(first, second)
        return jnp.stack([pick(held, got), pick(got, held)])[None, :, None]

    return (
        by_micro(kept[0][4].output, kept[1][4].output),
        by_micro(input_grads[0], input_grads[1]),
        table_grad,
        time_grad,
        grad_inner[None],
        grad_in_bias[None],
        grad_outer[None],
        bias_total[2][None],
        grad_upper[None],
        bias_total[1][None],
        grad_lower[None],
        bias_total[3][None],
        grad_mod_weight[None],
        grad_mod_bias[None],
    )


def solution(mesh):
    in_specs = (
        P(None, SLOTS, TENSOR, None),
        P(None, SLOTS, TENSOR, None),
        P(None, SLOTS),
        P(None, SLOTS),
        P(None, SLOTS),
        P(),
        P(),
        P(SECTION, SLOTS, None, TENSOR),
        P(SECTION, None, (TENSOR, SLOTS)),
        P(SECTION, TENSOR, SLOTS),
        P(SECTION, SLOTS),
        P(SECTION, SLOTS, TENSOR),
        P(SECTION, (TENSOR, SLOTS)),
        P(SECTION, TENSOR, SLOTS),
        P(SECTION, SLOTS),
        P(SECTION, SLOTS, None, TENSOR),
        P(SECTION, None, (TENSOR, SLOTS)),
    )
    out_specs = (
        P(SECTION, None, SLOTS, TENSOR, None),
        P(SECTION, None, SLOTS, TENSOR, None),
        P(),
        P(),
        P(SECTION, SLOTS, None, TENSOR),
        P(SECTION, None, (TENSOR, SLOTS)),
        P(SECTION, TENSOR, SLOTS),
        P(SECTION, SLOTS),
        P(SECTION, SLOTS, TENSOR),
        P(SECTION, (TENSOR, SLOTS)),
        P(SECTION, TENSOR, SLOTS),
        P(SECTION, SLOTS),
        P(SECTION, SLOTS, None, TENSOR),
        P(SECTION, None, (TENSOR, SLOTS)),
    )
    return jax.shard_map(body, mesh=mesh, in_specs=in_specs, out_specs=out_specs, check_vma=False)
```

```python
import math
from types import SimpleNamespace as Named

import jax
import jax.numpy as jnp
from jax import lax
from jax.experimental import pallas as pl
from jax.experimental.pallas import tpu as pltpu
from jax.sharding import PartitionSpec as P

HD = 64
EPS = 1e-06
HIGH = lax.Precision.HIGHEST
F32 = jnp.float32
BF16 = jnp.bfloat16
SECTION, TENSOR, SLOTS = "section", "tensor", "dp"
LAYER = (SECTION, TENSOR)
ROWS = (SLOTS, SECTION)
SPACE = 40 * 1024 * 1024


def cyclic(axis):
    size = lax.axis_size(axis)
    return size & (size - 1) != 0


def exchange(value, axis, k):
    size = lax.axis_size(axis)
    if cyclic(axis):
        return lax.ppermute(value, axis, [(i, (i - k) % size) for i in range(size)])
    return lax.ppermute(value, axis, [(i, i ^ k) for i in range(size)])


def fetch(value, axis, k):
    size = lax.axis_size(axis)
    if cyclic(axis):
        return lax.ppermute(value, axis, [(i, (i + k) % size) for i in range(size)])
    return lax.ppermute(value, axis, [(i, i ^ k) for i in range(size)])


def partner(axis, k):
    here = lax.axis_index(axis)
    if cyclic(axis):
        return (here - k) % lax.axis_size(axis)
    return here ^ k


def swap(value):
    return lax.ppermute(value, SECTION, [(0, 1), (1, 0)])


def across(value, axis):
    return lax.all_to_all(value, axis, 0, 0)


def gather_list(value, axis):
    got = {k: fetch(value, axis, k) for k in reversed(range(1, lax.axis_size(axis)))}
    return [value] + [got[k] for k in range(1, lax.axis_size(axis))]


def exchange_list(values, axis):
    got = {k: exchange(values[k], axis, k) for k in reversed(range(1, lax.axis_size(axis)))}
    return [values[0]] + [got[k] for k in range(1, lax.axis_size(axis))]


def place(pieces, axis):
    out = jnp.zeros((len(pieces),) + pieces[0].shape, pieces[0].dtype)
    for k, piece in enumerate(pieces):
        out = lax.dynamic_update_index_in_dim(out, piece, partner(axis, k), 0)
    return out


def shaped(shape, dtype):
    return jax.ShapeDtypeStruct(shape, dtype)


class Part:
    def __init__(self, value, at=None):
        self.value, self.at = value, at
        self.shape, self.dtype = value.shape, value.dtype


def run(kernel, outs, *args, flops=0, wait=()):
    def leafy(value):
        return isinstance(value, Part)

    names = list(vars(outs))
    out_flat, out_tree = jax.tree.flatten([vars(outs)[name] for name in names])
    flat, tree = jax.tree.flatten(args, is_leaf=leafy)
    moved = sum(math.prod(leaf.shape) * leaf.dtype.itemsize for leaf in flat + out_flat)

    def inner(*refs):
        ins = list(refs[: len(flat)])
        for k, leaf in enumerate(flat):
            if leafy(leaf) and leaf.at is not None:
                ins[k] = Named(ref=ins[k], at=leaf.at)
        results = jax.tree.unflatten(out_tree, refs[len(flat) + len(wait) :])
        kernel(*jax.tree.unflatten(tree, ins), Named(**dict(zip(names, results))))

    result = pl.pallas_call(
        inner,
        out_shape=out_flat,
        in_specs=[
            pl.BlockSpec(memory_space=pltpu.SMEM if leaf.dtype == jnp.int32 else pltpu.VMEM)
            for leaf in flat
        ]
        + [pl.BlockSpec(memory_space=pl.ANY)] * len(wait),
        out_specs=[pl.BlockSpec(memory_space=pltpu.VMEM)] * len(out_flat),
        compiler_params=pltpu.CompilerParams(vmem_limit_bytes=SPACE),
        cost_estimate=pl.CostEstimate(flops=flops, bytes_accessed=moved, transcendentals=0),
    )(*[leaf.value if leafy(leaf) else leaf for leaf in flat], *wait)
    return Named(**dict(zip(names, jax.tree.unflatten(out_tree, result))))


def matrix(ref):
    if isinstance(ref, Named):
        value = ref.ref[:, ref.at]
        return value.reshape(-1, value.shape[-1])
    return ref[...]


def norm_parts(values):
    average = jnp.mean(values, axis=-1, keepdims=True)
    centred = values - average
    spread = jnp.mean(centred * centred, axis=-1, keepdims=True)
    scale = lax.rsqrt(spread + EPS)
    return centred * scale, scale


def norm_pull(grad, normed, scale):
    first = jnp.mean(grad, axis=-1, keepdims=True)
    second = jnp.mean(grad * normed, axis=-1, keepdims=True)
    return scale * (grad - first - normed * second)


def dot(left, right, left_dim, right_dim):
    return lax.dot_general(
        left, right, (((left_dim,), (right_dim,)), ((), ())), preferred_element_type=F32
    )


def joined(refs):
    return jnp.concatenate([ref[...] for ref in refs], axis=0)


def summed(refs):
    total = refs[0][...].astype(F32)
    for ref in refs[1:]:
        total = total + ref[...].astype(F32)
    return total


def spread_out(terms, refs):
    rows = refs[0].shape[0]
    for k, ref in enumerate(refs):
        ref[...] = terms[k * rows : (k + 1) * rows].astype(ref.dtype)


def column_sum(values):
    return jnp.sum(values.astype(F32), axis=0, keepdims=True)


def softmax_parts(query, key):
    scores = dot(query, key, 1, 1) * HD**-0.5
    raised = jnp.exp(scores - jnp.max(scores, axis=-1, keepdims=True))
    return raised / jnp.sum(raised, axis=-1, keepdims=True)


def assemble(spot, pieces, ref):
    own, other = pieces
    rows = own.shape[1]
    for k in range(own.shape[0]):
        for half, block in ((spot[0], own[k]), (1 - spot[0], other[k])):
            at = pl.multiple_of((2 * spot[3 + k] + half) * rows, rows)
            ref[pl.ds(at, rows), :] = block


def attend(first, mods, packed, in_bias, refs, layer):
    width = packed.shape[1] // 4
    attn_in = joined(first)
    if layer == 0:
        refs.kept[:, 2 * packed.shape[1] :] = attn_in
        normed = norm_parts(attn_in.astype(F32))[0]
        attn_in = (normed * (1.0 + mods[1:2]) + mods[0:1]).astype(BF16)
    refs.kept[:, : packed.shape[1]] = attn_in
    projected = dot(attn_in, packed[:, : 3 * width], 1, 0)
    queries = (projected[:, :width] + in_bias[0:1]).astype(BF16)
    keys = projected[:, width : 2 * width].astype(BF16)
    values = (projected[:, 2 * width :] + in_bias[1:2]).astype(BF16)
    mixed = []
    for at in range(0, width, HD):
        attention = softmax_parts(queries[:, at : at + HD], keys[:, at : at + HD])
        mixed.append(dot(attention.astype(BF16), values[:, at : at + HD], 1, 0))
    mixed = jnp.concatenate(mixed, axis=1).astype(BF16)
    refs.kept[:, packed.shape[1] : 2 * packed.shape[1]] = jnp.concatenate(
        [queries, keys, values, mixed], axis=1
    )
    spread_out(dot(mixed, packed[:, 3 * width :], 1, 1), refs.terms)


def attend_kernel(layer):
    def kernel(spot, first, mods_ref, packed_ref, bias_ref, refs):
        if isinstance(packed_ref, tuple):
            assemble(spot, packed_ref, refs.packed)
            packed_ref = refs.packed
        attend(first, mods_ref[6 * layer : 6 * layer + 6], matrix(packed_ref), bias_ref[...], refs, layer)

    return kernel


def middle_kernel(layer):
    def kernel(terms, inputs, mods_ref, bias_ref, refs):
        mods = mods_ref[6 * layer : 6 * layer + 6]
        attn_out = summed(terms) + bias_ref[2:3]
        rows = attn_out.shape[0]
        refs.kept[:rows] = attn_out
        middle = inputs[...].astype(F32) + mods[2:3] * attn_out
        refs.kept[rows:] = middle
        normed = norm_parts(middle)[0]
        refs.mlp_in[...] = (normed * (1.0 + mods[4:5]) + mods[3:4]).astype(BF16)

    return kernel


def mlp_kernel(pieces, upper, lower, bias_ref, refs):
    mlp_in = joined(pieces)
    size = upper.ref.shape[-1] if isinstance(upper, Named) else upper.shape[-1]
    wide = mlp_in.shape[1]
    refs.kept[:, :wide] = mlp_in
    values = dot(mlp_in, matrix(upper), 1, 0) + bias_ref[1:2]
    root = math.sqrt(2.0 / math.pi)
    square = values * values
    bent = jnp.tanh(root * (values + 0.044715 * values * square))
    hidden = (0.5 * values * (1.0 + bent)).astype(BF16)
    refs.kept[:, wide : wide + size] = hidden
    slope = 0.5 * (1.0 + bent) + 0.5 * values * (1.0 - bent * bent) * root * (
        1.0 + 0.134145 * square
    )
    refs.kept[:, wide + size :] = slope.astype(BF16)
    spread_out(dot(hidden, matrix(lower), 1, 1), refs.terms)


def last_kernel(layer):
    def kernel(terms, kept, mods_ref, bias_ref, refs):
        mlp_out = summed(terms) + bias_ref[3:4]
        refs.mlp_out[...] = mlp_out
        output = (kept[kept.shape[0] // 2 :] + mods_ref[6 * layer + 5 : 6 * layer + 6] * mlp_out).astype(BF16)
        refs.output[...] = output
        if layer == 0:
            normed = norm_parts(output.astype(F32))[0]
            refs.attn_in[...] = (normed * (1.0 + mods_ref[7:8]) + mods_ref[6:7]).astype(BF16)

    return kernel


def mlp_back_kernel(layer):
    def kernel(pieces, mods_ref, upper, lower, kept, refs):
        lower_grad = joined(pieces)
        if layer == 1:
            lower_grad = (lower_grad.astype(F32) * mods_ref[11:12]).astype(BF16)
        wide = lower_grad.shape[1]
        refs.grads[:, :wide] = lower_grad
        pre_grad = dot(lower_grad, matrix(lower), 1, 0)
        slope = kept[:, wide + pre_grad.shape[1] :].astype(F32)
        pre_grad = (pre_grad * slope).astype(BF16)
        refs.grads[:, wide:] = pre_grad
        spread_out(dot(pre_grad, matrix(upper), 1, 1), refs.terms)
        refs.bias[0:1] = column_sum(pre_grad)
        refs.bias[1:2] = column_sum(lower_grad)

    return kernel


def middle_back_kernel(layer):
    def kernel(terms, grad_ref, kept, mlp_out, mods_ref, refs):
        mods = mods_ref[6 * layer : 6 * layer + 6]
        grad = grad_ref[...].astype(F32)
        mid_grad = summed(terms)
        normed, scale = norm_parts(kept[kept.shape[0] // 2 :])
        middle_grad = grad + norm_pull(mid_grad * (1.0 + mods[4:5]), normed, scale)
        refs.middle_grad[...] = middle_grad
        refs.outer[...] = (middle_grad * mods[2:3]).astype(BF16)
        refs.rows[0:1] = column_sum(middle_grad * kept[: kept.shape[0] // 2])
        refs.rows[1:2] = column_sum(mid_grad)
        refs.rows[2:3] = column_sum(mid_grad * normed)
        refs.rows[3:4] = column_sum(grad * mlp_out[...])

    return kernel


def attend_back_kernel(layer):
    def kernel(pieces, packed, kept, others, refs):
        outer_grad = joined(pieces)
        wide = outer_grad.shape[1]
        refs.grads[:, :wide] = outer_grad
        packed = matrix(packed)
        width = packed.shape[1] // 4
        mixed_grad = dot(outer_grad, packed[:, 3 * width :], 1, 0).astype(BF16)
        queries, keys, values = [
            kept[:, wide + k * width : wide + (k + 1) * width] for k in range(3)
        ]
        d_queries, d_keys, d_values = [], [], []
        for at in range(0, width, HD):
            query, key = queries[:, at : at + HD], keys[:, at : at + HD]
            grad = mixed_grad[:, at : at + HD]
            attention = softmax_parts(query, key)
            weight_grad = dot(grad, values[:, at : at + HD], 1, 1)
            d_values.append(dot(attention.astype(BF16), grad, 0, 0))
            row_dot = jnp.sum(attention * weight_grad, axis=-1, keepdims=True)
            score_grad = (attention * (weight_grad - row_dot)).astype(BF16)
            d_queries.append(dot(score_grad, key, 1, 0) * HD**-0.5)
            d_keys.append(dot(score_grad, query, 0, 0) * HD**-0.5)
        stacked = jnp.concatenate(d_queries + d_keys + d_values, axis=1).astype(BF16)
        refs.grads[:, wide:] = stacked
        terms = dot(stacked, packed[:, : 3 * width], 1, 1)
        if others is None:
            spread_out(terms, refs.terms)
        else:
            refs.terms[...] = terms
        in_bias, out_bias = column_sum(stacked), column_sum(outer_grad)
        refs.out_bias[...] = out_bias
        refs.in_bias[...] = in_bias
        if layer == 0:
            normed = norm_parts(kept[:, 2 * wide :].astype(F32))[0]
            rows = jnp.concatenate([column_sum(terms), column_sum(terms * normed)], axis=0)
            if others is None:
                refs.rows[...] = rows
            else:
                middle_rows, mlp_bias, other_rows, other_bias = others
                mods = [
                    jnp.concatenate([rows, middle_rows[...]], axis=0),
                    jnp.concatenate([ref[...] for ref in other_rows], axis=0),
                ]
                send_rows(mods, [(in_bias, out_bias, mlp_bias), other_bias], refs.sent)

    return kernel


def first_back_kernel(layer):
    def kernel(terms, middle_grad, inputs, mods_ref, refs):
        in_grad = summed(terms)
        normed, scale = norm_parts(inputs[...].astype(F32))
        scale_one = mods_ref[6 * layer + 1 : 6 * layer + 2]
        input_grad = middle_grad[...] + norm_pull(in_grad * (1.0 + scale_one), normed, scale)
        refs.input_grad[...] = input_grad
        if layer == 1:
            refs.rows[0:1] = column_sum(in_grad)
            refs.rows[1:2] = column_sum(in_grad * normed)
            rounded = input_grad.astype(BF16)
            refs.grad[...] = rounded
            refs.lower[...] = (rounded.astype(F32) * mods_ref[5:6]).astype(BF16)

    return kernel


def cut(grad, ref, at):
    count, rows, half = ref.shape[0], ref.shape[2], ref.shape[3]
    for block in range(count):
        place_at = block // 2 * rows
        ref[block, at] = grad[
            place_at : place_at + rows, block % 2 * half : block % 2 * half + half
        ].astype(BF16)


def grads_kernel(mlp_kept, mlp_grads, attn_kept, attn_grads, refs):
    wide = 2 * refs.grads.shape[3]
    size, width = mlp_grads.shape[1] - wide, wide // 4
    cut(dot(mlp_kept[:, :wide], mlp_grads[:, wide:], 0, 0), refs.grads, 0)
    cut(dot(mlp_grads[:, :wide], mlp_kept[:, wide : wide + size], 0, 0), refs.grads, 1)
    inner = dot(attn_kept[:, :wide], attn_grads[:, wide:], 0, 0)
    outer = dot(attn_grads[:, :wide], attn_kept[:, wide + 3 * width : 2 * wide], 0, 0)
    cut(jnp.concatenate([inner, outer], axis=1), refs.grads, 2)


def mods_kernel(spot, got, refs):
    cuts = got.shape[0] // 2
    count = (got.shape[1] - 6) // 4
    cols = refs.inner[0].shape[1] // count
    for layer in range(2):
        refs.mods[6 * layer : 6 * layer + 6] = jnp.concatenate(
            [got[cuts * layer + t, :6] for t in range(cuts)], axis=1
        )
        rows = got[cuts * layer + spot[1], 6:]
        pieces = [rows[4 * k : 4 * k + 4] for k in range(count)]
        refs.biases[layer][...] = jnp.concatenate(pieces, axis=1)
        for k in range(2):
            refs.inner[layer][k : k + 1] = jnp.concatenate(
                [piece[0:1, k * cols : (k + 1) * cols] for piece in pieces], axis=1
            )


def bias_rows_of(part, rows, shards, in_bias, out_bias, mlp_bias):
    cols = part // shards
    pieces = []
    for z in range(shards):
        start = jnp.concatenate(
            [
                in_bias[:, z * cols : (z + 1) * cols],
                in_bias[:, 2 * part + z * cols : 2 * part + (z + 1) * cols],
                jnp.zeros((1, rows - 2 * cols), F32),
            ],
            axis=1,
        )
        at = slice(z * rows, (z + 1) * rows)
        pieces += [start, mlp_bias[0:1, at], out_bias[:, at], mlp_bias[1:2, at]]
    return jnp.concatenate(pieces, axis=0)


def send_rows(mods, biases, sent):
    cuts, part = sent.shape[0] // 2, sent.shape[2]
    shards = (sent.shape[1] - 6) // 4
    for layer in range(2):
        rows = bias_rows_of(part, part, shards, *biases[layer])
        for t in range(cuts):
            sent[cuts * layer + t, :6] = mods[layer][:, t * part : (t + 1) * part]
            sent[cuts * layer + t, 6:] = rows


def pack_kernel(spot, mod_one, mod_two, bias_one, bias_two, refs):
    core, here, cycle = spot[0], spot[1], spot[2]
    mods = jnp.concatenate([ref[...] for ref in mod_one + mod_two], axis=0)
    cuts = len(refs.mods)
    part = mods.shape[1] // cuts
    blocks = [mods[:, j * part : (j + 1) * part] for j in range(cuts)]
    for k, ref in enumerate(refs.mods):
        index = jnp.where(cycle == 1, (here - k + cuts) % cuts, here ^ k)
        chosen = blocks[0]
        for j in range(1, cuts):
            chosen = jnp.where(index == j, blocks[j], chosen)
        ref[...] = chosen
    shards, _, rows = refs.kept.shape
    first = bias_rows_of(part, rows, shards, *bias_one)
    second = bias_rows_of(part, rows, shards, *bias_two)
    for z in range(shards):
        at = slice(4 * z, 4 * z + 4)
        refs.kept[z] = jnp.where(core == 0, first[at], second[at])
        refs.given[z] = jnp.where(core == 0, second[at], first[at])


def bundle_kernel(members):
    def kernel(spot, kept, got, refs):
        for k, (weight, layer) in enumerate(members):
            refs.rows[k] = jnp.where(spot[0] == layer, kept[weight], got[weight])

    return kernel


def slots_kernel(spot, received, refs):
    cuts = received.shape[0] // 2
    shards = (received.shape[1] - 6) // 4
    mods = []
    for micro in range(2):
        total = received[cuts * micro, :6]
        for t in range(1, cuts):
            total = total + received[cuts * micro + t, :6]
        mods.append(total)
    here = spot[1]
    biases = received[here, 6:] + received[cuts + here, 6:]
    for k, ref in enumerate(refs.sent):
        ref[:6], ref[6:12] = mods
        total = biases[:4]
        for z in range(1, shards):
            total = jnp.where(spot[3 + k] == z, biases[4 * z : 4 * z + 4], total)
        ref[12:16] = total


def modulate_kernel(act, weights, mod_bias, own, refs):
    shards, _, part = refs.sent.shape
    micro = act.shape[0] // shards
    for k in range(6):
        terms = dot(act[...], weights[k], 1, 0) + mod_bias[k : k + 1]
        for z in range(shards):
            for m in range(micro):
                at = z * micro + m
                refs.sent[z, 6 * m + k : 6 * m + k + 1] = terms[at : at + 1]
    for z in range(shards):
        refs.sent[z, 6 * micro :] = own[...]


def act_kernel(spot, pieces, weights, refs):
    shards = len(pieces)
    blocks = []
    for z in range(shards):
        chosen = pieces[0][...]
        for k in range(1, shards):
            chosen = jnp.where(spot[3 + k] == z, pieces[k][...], chosen)
        blocks.append(chosen)
    total = jnp.zeros(refs.sent.shape[1:], F32)
    for k in range(6):
        rest = jnp.concatenate([b[at : at + 1] for b in blocks for at in (k, 6 + k)], axis=0)
        for _ in range(3):
            rounded = rest.astype(BF16)
            total = total + dot(rounded, weights[k], 1, 1)
            rest = rest - rounded.astype(F32)
    repeat_rows(total, refs.sent)


def condition_kernel(spot, pieces, condition, refs):
    shards = len(pieces)
    blocks = []
    for z in range(shards):
        chosen = pieces[0][...]
        for k in range(1, shards):
            chosen = jnp.where(spot[3 + k] == z, pieces[k][...], chosen)
        blocks.append(chosen)
    values = condition[...]
    gate = 1.0 / (1.0 + jnp.exp(-values))
    rest = jnp.concatenate(blocks, axis=1) * (gate * (1.0 + values * (1.0 - gate)))
    rounded = []
    for _ in range(3):
        rounded.append(rest.astype(BF16).astype(F32))
        rest = rest - rounded[-1]
    refs.pieces[...] = jnp.concatenate(rounded, axis=0).astype(BF16)


def repeat_rows(values, ref):
    for k in range(ref.shape[0]):
        ref[k] = values


def assemble_kernel(spot, first, second, given, refs):
    wide = []
    for k in range(3):
        own = jnp.where(spot[0] == 0, first[k], second[k]).astype(F32)
        other = given[k].astype(F32)
        left, right = jnp.where(spot[0] == 0, own, other), jnp.where(spot[0] == 0, other, own)
        wide.append(jnp.concatenate([left, right], axis=1))
    refs.upper[...], refs.lower[...] = wide[0], wide[1]
    width = wide[2].shape[1] // 4
    for k in range(3):
        refs.inner[k] = wide[2][:, k * width : (k + 1) * width]
    refs.outer[...] = wide[2][:, 3 * width :].T


def split_kernel(terms, refs):
    spread_out(terms[...], refs.terms)


def prepare_kernel(spot, inner, outer, upper, lower, refs):
    half = upper.shape[0] // 2
    packed = jnp.concatenate([inner[0], inner[1], inner[2], outer[...].T], axis=1)
    for k, member in enumerate((packed, upper[...], lower[...])):
        first, second = member[:half], member[half:]
        refs.kept[k] = jnp.where(spot[0] == 0, first, second)
        refs.given[k] = jnp.where(spot[0] == 0, second, first)


def sinus_features(stamps, columns):
    halfway = columns // 2
    frequency = jnp.exp(-math.log(10000.0) * jnp.arange(halfway, dtype=F32) / halfway)
    angles = stamps.astype(F32)[:, None] * frequency[None, :]
    return jnp.concatenate([jnp.cos(angles), jnp.sin(angles)], axis=-1)


def body(
    latents,
    cotangent,
    labels,
    timesteps,
    occupied,
    class_table,
    time_weight,
    project_in,
    project_in_bias,
    project_out,
    project_out_bias,
    up_weight,
    up_bias,
    down_weight,
    down_bias,
    modulate_weight,
    modulate_bias,
):
    core = lax.axis_index(SECTION)
    shard = lax.axis_index(SLOTS)
    shards = lax.axis_size(SLOTS)
    cuts = lax.axis_size(TENSOR)
    micro_count = latents.shape[0]
    width = latents.shape[3]
    own_tokens = latents.shape[2]
    tokens = own_tokens * cuts
    part = width // cuts
    rows = width // shards
    hidden_part = up_weight.shape[2]
    near = shards <= 8 and not cyclic(SLOTS) and rows == part

    def pick(first, second):
        return jnp.where(core == 0, first, second)

    spot = jnp.stack(
        [core, lax.axis_index(TENSOR), jnp.int32(1 if cyclic(TENSOR) else 0)]
        + [partner(SLOTS, k) for k in range(shards if near else 0)]
        + [partner(TENSOR, k) for k in range(cuts)]
    ).astype(jnp.int32)

    half = rows // 2
    if near:
        inner = jnp.moveaxis(project_in[0], 1, 0)
        ready = run(
            prepare_kernel,
            Named(kept=shaped((3, half, width), BF16), given=shaped((3, half, width), BF16)),
            spot,
            inner,
            project_out[0],
            up_weight[0],
            down_weight[0].T,
        )
        given = swap(ready.given)
        kept_halves, got_halves = ready.kept, given
    else:
        packed_own = jnp.concatenate(
            [project_in[0, :, 0], project_in[0, :, 1], project_in[0, :, 2], project_out[0].T], axis=1
        )
        stack = [packed_own, up_weight[0], down_weight[0].T]
        given = swap(jnp.concatenate([pick(member[half:], member[:half]) for member in stack]))
        kept_halves = [pick(member[:half], member[half:]) for member in stack]
        got_halves = [given[k * half : (k + 1) * half] for k in range(3)]

    def bundle(members, wait):
        return run(
            bundle_kernel(members),
            Named(rows=shaped((len(members), half, width), BF16)),
            spot,
            kept_halves,
            got_halves,
            wait=wait,
        ).rows

    bundles = []

    def gather_blocks(members, wait=()):
        if near:
            own = bundle(members, wait)
            bundles.append(own)
            whole = lax.all_gather(own, ROWS, axis=0)
            return [Part(whole, k) for k in range(len(members))]
        return [
            gather_rows(
                pick(kept_halves[k], got_halves[k])
                if layer == 0
                else pick(got_halves[k], kept_halves[k])
            )
            for k, layer in members
        ]

    def gather_rows(value):
        return lax.all_gather(value, ROWS, axis=0, tiled=True)

    stamps = jnp.concatenate([labels.reshape(1, -1), timesteps.reshape(1, -1)], axis=1)
    if near:
        stamps = place(gather_list(stamps, SLOTS), SLOTS).reshape(shards, -1)
    else:
        stamps = lax.all_gather(stamps, SLOTS, axis=0, tiled=True)
    flat_labels = stamps[:, :micro_count].reshape(-1)
    flat_times = stamps[:, micro_count:].reshape(-1)
    class_count = class_table.shape[0]
    class_hot = flat_labels[:, None] == jnp.arange(class_count, dtype=jnp.int32)[None, :]
    time_feats = sinus_features(flat_times, time_weight.shape[0]).astype(BF16)
    condition = dot(class_hot.astype(BF16), class_table, 1, 0) + dot(time_feats, time_weight, 1, 0)
    cond_act = jax.nn.silu(condition).astype(BF16)
    act_rows = lax.dynamic_slice_in_dim(cond_act, shard * rows, rows, 1)

    if near:
        first_pieces = gather_list(pick(kept_halves[0], got_halves[0]), SLOTS)
    else:
        (first_a,) = gather_blocks([(0, 0)])

    tokens_own = pick(latents[0, 0], latents[1, 0])
    seed_own = pick(
        cotangent[0, 0] * occupied[0, 0].astype(BF16), cotangent[1, 0] * occupied[1, 0].astype(BF16)
    )
    token_list = gather_list(tokens_own, TENSOR)

    mod_weight = modulate_weight[0].reshape(rows, -1)
    bias_cols = modulate_bias.shape[2]
    bias_full = lax.dynamic_update_slice_in_dim(
        jnp.zeros((6, part), F32), modulate_bias[0].astype(F32), shard * bias_cols, 1
    )
    mod_terms = dot(act_rows, mod_weight, 1, 0) + bias_full.reshape(1, -1)
    mod_terms = mod_terms.reshape(shards, micro_count * 6, part)
    in_bias_own = project_in_bias.astype(F32).reshape(1, -1)
    bias_own = jnp.concatenate(
        [
            jnp.pad(in_bias_own, ((0, 0), (0, rows - in_bias_own.shape[1]))),
            up_bias.astype(F32),
            project_out_bias.astype(F32),
            down_bias.astype(F32),
        ],
        axis=0,
    )
    if near:
        sent = run(
            modulate_kernel,
            Named(sent=shaped((shards, 6 * micro_count + 4, part), F32)),
            act_rows,
            jnp.moveaxis(modulate_weight[0], 1, 0),
            bias_full,
            bias_own,
        ).sent
        got = across(sent, SLOTS)
        mod_sum = jnp.sum(got[:, : micro_count * 6], axis=0).reshape(micro_count, 6, part)
        bias_all = jnp.broadcast_to(
            got[:, micro_count * 6 :].reshape(1, 4 * shards, part), (micro_count, 4 * shards, part)
        )
        sent = jnp.concatenate([mod_sum, bias_all], axis=1)
        got_all = across(jnp.repeat(sent, cuts, axis=0), LAYER)
        ready = run(
            mods_kernel,
            Named(
                mods=shaped((12, width), F32),
                biases=[shaped((4, width), F32)] * 2,
                inner=[shaped((2, part), F32)] * 2,
            ),
            spot,
            got_all,
        )
        mods, biases, in_biases = ready.mods, ready.biases, ready.inner
    else:
        mod_sum = lax.psum_scatter(mod_terms, SLOTS, scatter_dimension=0, tiled=False)
        bias_all = lax.all_gather(bias_own, SLOTS, axis=0)
        mod_got, bias_got = swap(pick(mod_sum[6:], mod_sum[:6])), swap(bias_all)
        mod_kept = pick(mod_sum[:6], mod_sum[6:])
        mod_both = jnp.concatenate([pick(mod_kept, mod_got), pick(mod_got, mod_kept)], axis=0)
        mod_list = gather_list(mod_both, TENSOR)
        mods = jnp.moveaxis(place(mod_list, TENSOR), 0, 1).reshape(12, width)
        in_biases, biases = [], []
        for member in (pick(bias_all, bias_got), pick(bias_got, bias_all)):
            cols = project_in_bias.shape[2]
            columns = member[:, 0, : 2 * cols].reshape(shards, 2, cols)
            in_biases.append(jnp.moveaxis(columns, 0, 1).reshape(2, part))
            biases.append(jnp.moveaxis(member, 0, 1).reshape(4, width))
    if near:
        first_stack = jnp.stack(first_pieces)
        first_a = (first_stack, swap(first_stack))
    first_u, first_d, second_a = gather_blocks([(1, 0), (2, 0), (0, 1)], (got, first_stack) if near else ())
    second_u, second_d = gather_blocks([(1, 1), (2, 1)], tuple(bundles))
    weights = [(first_a, first_u, first_d), (second_a, second_u, second_d)]

    def terms_out(count=1):
        return [shaped((own_tokens, width), F32)] + [
            shaped((own_tokens, width), BF16) for k in range(1, cuts)
        ]

    own_f32 = shaped((own_tokens, width), F32)
    both_f32 = shaped((2 * own_tokens, width), F32)
    own_b16 = shaped((own_tokens, width), BF16)
    attend_flops = 2 * tokens * width * width + 4 * tokens * tokens * part
    mlp_flops = 4 * tokens * width * hidden_part

    kept, packs = [], []
    inputs = tokens_own
    first = [jnp.concatenate(token_list)]
    for layer in range(2):
        packed, upper, lower = weights[layer]
        outs = Named(kept=shaped((tokens, (3 - layer) * width), BF16), terms=terms_out())
        if isinstance(packed, tuple):
            outs.packed = shaped((width, width), BF16)
        attn = run(
            attend_kernel(layer),
            outs,
            spot,
            first,
            mods,
            packed,
            in_biases[layer],
            flops=attend_flops,
        )
        packs.append(attn.packed if isinstance(packed, tuple) else packed)
        terms = exchange_list(attn.terms, TENSOR)
        middle = run(
            middle_kernel(layer),
            Named(kept=both_f32, mlp_in=own_b16),
            terms,
            inputs,
            mods,
            biases[layer],
        )
        mlp = run(
            mlp_kernel,
            Named(kept=shaped((tokens, width + 2 * hidden_part), BF16), terms=terms_out()),
            [jnp.concatenate(gather_list(middle.mlp_in, TENSOR))]
            if layer == 0
            else gather_list(middle.mlp_in, TENSOR),
            upper,
            lower,
            biases[layer],
            flops=mlp_flops,
        )
        outs = Named(mlp_out=own_f32, output=own_b16)
        if layer == 0:
            outs.attn_in = own_b16
        last = run(
            last_kernel(layer),
            outs,
            exchange_list(mlp.terms, TENSOR),
            middle.kept,
            mods,
            biases[layer],
        )
        kept.append((inputs, attn, middle, mlp, last))
        inputs = last.output
        if layer == 0:
            first = gather_list(last.attn_in, TENSOR)
            seed_list = [jnp.concatenate(gather_list(seed_own, TENSOR))]

    row = shaped((1, width), F32)
    grad_own, pieces = seed_own, seed_list
    mod_rows, bias_rows, blocks, input_grads = [None] * 2, [None] * 2, [None] * 2, [None] * 2
    for layer in (1, 0):
        packed, upper, lower = packs[layer], weights[layer][1], weights[layer][2]
        inputs, attn, middle, mlp, last = kept[layer]
        mlp_back = run(
            mlp_back_kernel(layer),
            Named(
                grads=shaped((tokens, width + hidden_part), BF16),
                terms=terms_out(),
                bias=shaped((2, hidden_part), F32),
            ),
            pieces,
            mods,
            upper,
            lower,
            mlp.kept,
            flops=mlp_flops,
        )
        middle_back = run(
            middle_back_kernel(layer),
            Named(
                middle_grad=own_f32,
                outer=own_b16,
                rows=shaped((4, width), F32),
            ),
            exchange_list(mlp_back.terms, TENSOR),
            grad_own,
            middle.kept,
            last.mlp_out,
            mods,
        )
        outs = Named(
            grads=shaped((tokens, width + 3 * part), BF16),
            terms=terms_out(),
            out_bias=row,
            in_bias=shaped((1, 3 * part), F32),
        )
        others = None
        if layer == 0 and near:
            outs.sent = shaped((2 * cuts, 6 + 4 * shards, part), F32)
            outs.terms = shaped((tokens, width), F32)
            others = (middle_back.rows, mlp_back.bias, mod_rows[1], bias_rows[1])
        elif layer == 0:
            outs.rows = shaped((2, width), F32)
        attn_back = run(
            attend_back_kernel(layer),
            outs,
            gather_list(middle_back.outer, TENSOR),
            packed,
            attn.kept,
            others,
            flops=2 * attend_flops,
        )
        grads = run(
            grads_kernel,
            Named(grads=shaped((2 * shards, 3, rows, width // 2), BF16)),
            mlp.kept,
            mlp_back.grads,
            attn.kept,
            attn_back.grads,
            flops=mlp_flops + 2 * tokens * width * width,
        ).grads
        blocks[layer] = lax.psum_scatter(grads, ROWS, scatter_dimension=0, tiled=False)
        terms = attn_back.terms
        if layer == 0 and near:
            sent = run(
                slots_kernel,
                Named(sent=[shaped((16, part), F32)] * shards),
                spot,
                across(attn_back.sent, LAYER),
            ).sent
            got = exchange_list(sent, SLOTS)
            terms = run(
                split_kernel, Named(terms=terms_out()), terms, wait=tuple(got[1:])
            ).terms
        outs = Named(input_grad=own_f32)
        if layer == 1:
            outs.rows, outs.grad, outs.lower = shaped((2, width), F32), own_b16, own_b16
        first_back = run(
            first_back_kernel(layer),
            outs,
            exchange_list(terms, TENSOR),
            middle_back.middle_grad,
            inputs,
            mods,
        )
        input_grads[layer] = first_back.input_grad
        if layer == 1 or not near:
            mod_rows[layer] = [
                attn_back.rows if layer == 0 else first_back.rows,
                middle_back.rows,
            ]
        bias_rows[layer] = (attn_back.in_bias, attn_back.out_bias, mlp_back.bias)

        if layer == 1:
            grad_own = first_back.grad
            pieces = gather_list(first_back.lower, TENSOR)

    given = swap(pick(blocks[1], blocks[0]))
    if near:
        ready = run(
            assemble_kernel,
            Named(
                upper=shaped((rows, hidden_part), F32),
                lower=shaped((rows, hidden_part), F32),
                inner=shaped((3, rows, part), F32),
                outer=shaped((part, rows), F32),
            ),
            spot,
            blocks[0],
            blocks[1],
            given,
        )
        grad_upper, grad_lower, grad_outer = ready.upper, ready.lower.T, ready.outer
        grad_inner = jnp.moveaxis(ready.inner, 0, 1)
    else:
        own = pick(blocks[0], blocks[1])
        grads = jnp.concatenate([pick(own, given), pick(given, own)], axis=2).astype(F32)
        grad_upper, grad_lower = grads[0], grads[1].T
        grad_inner = grads[2, :, : 3 * part].reshape(rows, 3, part)
        grad_outer = grads[2, :, 3 * part :].T

    if near:
        mod_slots = place([member[:12] for member in got], SLOTS)
        bias_total = sum(member[12:] for member in got)
    else:
        tail = run(
            pack_kernel,
            Named(
                mods=[shaped((12, part), F32) for k in range(cuts)],
                kept=shaped((shards, 4, rows), F32),
                given=shaped((shards, 4, rows), F32),
            ),
            spot,
            mod_rows[0],
            mod_rows[1],
            bias_rows[0],
            bias_rows[1],
        )
        mod_shard = sum(exchange_list(tail.mods, TENSOR))
        mod_given, mod_kept = pick(mod_shard[6:], mod_shard[:6]), pick(mod_shard[:6], mod_shard[6:])
        mod_got, bias_got = swap(mod_given), swap(tail.given)
        mod_micro = jnp.concatenate([pick(mod_kept, mod_got), pick(mod_got, mod_kept)], axis=0)
        bias_sum = tail.kept + bias_got
        mod_slots = lax.all_gather(mod_micro, SLOTS, axis=0, tiled=True)
        bias_total = lax.psum_scatter(bias_sum, SLOTS, scatter_dimension=0, tiled=False)
    mod_slots = mod_slots.reshape(shards * micro_count, 6 * part)
    if near:
        sent = run(
            act_kernel,
            Named(sent=shaped((2 * cuts, shards * micro_count, rows), F32)),
            spot,
            got,
            jnp.moveaxis(modulate_weight[0], 1, 0),
        ).sent
        act_grad = jnp.sum(across(sent, LAYER), axis=0)
        pieces = run(
            condition_kernel,
            Named(pieces=shaped((3 * shards * micro_count, width), BF16)),
            spot,
            gather_list(act_grad, SLOTS),
            condition,
        ).pieces
    else:
        act_grad = lax.dot_general(
            mod_slots, mod_weight.astype(F32), (((1,), (1,)), ((), ())), precision=HIGH
        )
        act_grad = act_grad + swap(act_grad)
        act_grad = sum(gather_list(act_grad, TENSOR))
        act_all = lax.all_gather(act_grad, SLOTS, axis=0)
        act_all = jnp.moveaxis(act_all, 0, 1).reshape(-1, width)
        rest = jax.vjp(jax.nn.silu, condition)[1](act_all)[0]
        pieces = []
        for _ in range(3):
            pieces.append(rest.astype(BF16))
            rest = rest - pieces[-1].astype(F32)
        pieces = jnp.concatenate(pieces, axis=0)
    table_grad = dot(jnp.concatenate([class_hot.astype(BF16)] * 3, axis=0), pieces, 0, 0)
    time_grad = dot(jnp.concatenate([time_feats] * 3, axis=0), pieces, 0, 0)
    grad_mod_weight = lax.dot_general(
        act_rows.astype(F32), mod_slots, (((0,), (0,)), ((), ())), precision=HIGH
    ).reshape(rows, 6, part)
    mod_bias_sum = jnp.sum(mod_slots, axis=0).reshape(6, part)
    grad_mod_bias = lax.dynamic_slice_in_dim(mod_bias_sum, shard * bias_cols, bias_cols, 1)
    grad_in_bias = bias_total[0, : in_bias_own.shape[1]].reshape(2, -1)

    def by_micro(first, second):
        got = swap(pick(second, first))
        held = pick(first, second)
        return jnp.stack([pick(held, got), pick(got, held)])[None, :, None]

    return (
        by_micro(kept[0][4].output, kept[1][4].output),
        by_micro(input_grads[0], input_grads[1]),
        table_grad,
        time_grad,
        grad_inner[None],
        grad_in_bias[None],
        grad_outer[None],
        bias_total[2][None],
        grad_upper[None],
        bias_total[1][None],
        grad_lower[None],
        bias_total[3][None],
        grad_mod_weight[None],
        grad_mod_bias[None],
    )


def solution(mesh):
    in_specs = (
        P(None, SLOTS, TENSOR, None),
        P(None, SLOTS, TENSOR, None),
        P(None, SLOTS),
        P(None, SLOTS),
        P(None, SLOTS),
        P(),
        P(),
        P(SECTION, SLOTS, None, TENSOR),
        P(SECTION, None, (TENSOR, SLOTS)),
        P(SECTION, TENSOR, SLOTS),
        P(SECTION, SLOTS),
        P(SECTION, SLOTS, TENSOR),
        P(SECTION, (TENSOR, SLOTS)),
        P(SECTION, TENSOR, SLOTS),
        P(SECTION, SLOTS),
        P(SECTION, SLOTS, None, TENSOR),
        P(SECTION, None, (TENSOR, SLOTS)),
    )
    out_specs = (
        P(SECTION, None, SLOTS, TENSOR, None),
        P(SECTION, None, SLOTS, TENSOR, None),
        P(),
        P(),
        P(SECTION, SLOTS, None, TENSOR),
        P(SECTION, None, (TENSOR, SLOTS)),
        P(SECTION, TENSOR, SLOTS),
        P(SECTION, SLOTS),
        P(SECTION, SLOTS, TENSOR),
        P(SECTION, (TENSOR, SLOTS)),
        P(SECTION, TENSOR, SLOTS),
        P(SECTION, SLOTS),
        P(SECTION, SLOTS, None, TENSOR),
        P(SECTION, None, (TENSOR, SLOTS)),
    )
    return jax.shard_map(body, mesh=mesh, in_specs=in_specs, out_specs=out_specs, check_vma=False)
```
